128 devices in a mesh: img: 64 (over z, y, x), head: 2 (over core).
Axes of the slice: x: 4, y: 4, z: 4, core: 2. Of those that a mesh axis runs over, the one named last changes fastest.
Arguments:
- tokens: bfloat16 [128, 256, 3200], P('img', 'head'), may hold values from -180 to 180
- tap_early: bfloat16 [128, 256, 3200], P('img', 'head'), may hold values from -6 to 6
- tap_mid: bfloat16 [128, 256, 3200], P('img', 'head'), may hold values from -6 to 6
- tile_counts: int32 [51], replicated, may hold values from 1 to 5, 128 in all
- qkv_weight: bfloat16 [3200, 6144], P('img', 'head'), may hold values from -1 to 1
- out_weight: bfloat16 [2048, 3200], P('head'), may hold values from -0.125 to 0.125
- layer_scale: float32 [3200], replicated, may hold values from 0.5 to 4
- layer_logits: float32 [4], replicated, may hold values from -1 to 1
- proj_weight: bfloat16 [3200, 4096], P(None, 'head'), may hold values from -0.109375 to 0.109375
- proj_bias: float32 [4096], P('head'), may hold values from -5 to 5
- grad_out: bfloat16 [384, 256, 4096], P('img', None, 'head'), may hold values from -6 to 6
Outputs:
- owner_rows: bfloat16 [384, 256, 4096], P('img', None, 'head')
- grad_joined: bfloat16 [128, 256, 3200], P('img', 'head')
The draws below stay inside these ranges and needn't reach their ends.
Inputs may be any that keep to these rules, and one draw needn't show every extreme that they name: `tile_counts`: tiles of the samples in order make up the 128 tiles, 2 to each index of img.
All inputs are finite; a program needn't handle non-finite values.
Results may differ from the reference program's by a relative error of at most 0.017.
Values may be sent and summed in bfloat16 or wider, within the bound.
No kernel may reach another device: no remote copies, remote signals or barrier semaphores. Data moves between devices by JAX's collectives and lax.ppermute only.
A program may use at most 192 MiB of HBM per device.

```python
import math
import jax
import jax.numpy as jnp
import numpy as np
from jax import lax

D = 3200
HEADS = 16
HEAD_DIM = 128
PF = 4096
TILE_TOK = 256
TG = 2
MAXT = 5
OWN_TILES = 6
TILES = 128
SAMPLES = 51
N_IMG = 64
N_HEAD = 2


def draw_tokens(key, part):
    key = jax.random.fold_in(key, 11)
    shape_all = (TILES, TILE_TOK, D)
    values = jax.random.truncated_normal(key, -6.0, 6.0, shape_all, jnp.float32)
    return values.astype(jnp.bfloat16)


def draw_qkv_weight(key, part):
    key = jax.random.fold_in(key, 23)
    keys_list = jax.random.split(key, 1)
    base_values = jax.random.truncated_normal(keys_list[0], -4.0, 4.0, (D, HEADS, 3, HEAD_DIM), jnp.float32) / math.sqrt(D)
    part_scale = jnp.array([1.6, 1.6, 1.0], jnp.float32)
    weights = base_values * part_scale[None, None, :, None]
    return weights.reshape(D, HEADS * 3 * HEAD_DIM).astype(jnp.bfloat16)


def block_levels(stream_key, extent, cuts, smallest, largest):
    def one(dim, blocks):
        draws = jax.random.uniform(jax.random.fold_in(jax.random.fold_in(stream_key, 6), dim), (blocks,), jnp.float32, smallest / len(cuts), largest / len(cuts))
        return jnp.repeat(jnp.exp(draws), extent[dim] // blocks).reshape((-1,) + (1,) * (len(extent) - dim - 1))

    level = one(*cuts[0])
    for cut in cuts[1:]:
        level = level * one(*cut)
    return level


def split_up(number_of, total, reach, lean):
    weights = [(1 << 20) // math.isqrt(grade ** lean) + 1 for grade in range(2, number_of + 1)]
    rest, given = total - reach - (number_of - 1), [1] * (number_of - 1)
    while rest > 0:
        free = [i for i in range(number_of - 1) if given[i] < reach]
        pool, remaining = sum([weights[i] for i in free]), rest
        for i in free:
            extra = min(reach - given[i], max(1, remaining * weights[i] // pool), rest)
            given[i] = given[i] + extra
            rest = rest - extra
    return np.array([reach] + given)


def uneven_parts(stream_key, amount, total, most, skew):
    if amount == 2:
        one = jax.random.randint(stream_key, (), max(1, total - most), min(most, total - 1) + 1)
        return jnp.stack([one, total - one])
    lengths = jnp.asarray(split_up(amount, total, most, skew), jnp.int32)
    twos = (amount - 1) // 2
    giver, receiver = lengths[1:1 + 2 * twos:2], lengths[2:2 + 2 * twos:2]
    margin = jnp.minimum(giver - 1, most - receiver)
    passed = jax.random.randint(jax.random.fold_in(stream_key, 1), (twos,), 0, 1 << 20) % (margin + 1)
    lengths = lengths.at[1:1 + 2 * twos:2].set(giver - passed).at[2:2 + 2 * twos:2].set(receiver + passed)
    return lengths[jax.random.permutation(jax.random.fold_in(stream_key, 2), amount)]


def noise(own_key, extent, width, bound, pieces=(), held_as=jnp.bfloat16):
    values = width * jax.random.normal(own_key, extent, jnp.float32)
    if pieces:
        values = values * block_levels(own_key, extent, pieces, -0.22, 0.18)
    return jnp.clip(values, -bound, bound).astype(held_as)


def setup_inputs(seed: int = 0) -> dict:
    splits = jax.random.split(jax.random.key(seed), 12)
    tokens = draw_tokens(jax.random.fold_in(splits[11], 71), 0)
    tap_early = noise(splits[1], (TILES, TILE_TOK, D), 1.0, 6.0, ((0, 64), (1, 2)))
    tap_mid = noise(splits[2], (TILES, TILE_TOK, D), 1.0, 6.0, ((0, 64), (1, 2)))
    tile_counts = uneven_parts(splits[3], SAMPLES, TILES, MAXT, 2).astype(jnp.int32)
    qkv_weight = draw_qkv_weight(jax.random.fold_in(splits[11], 71), 0)
    out_weight = noise(splits[5], (HEADS * HEAD_DIM, D), (HEADS * HEAD_DIM) ** -0.5, 0.125, ((0, 2),))
    layer_scale = jnp.clip(jnp.exp(jax.random.uniform(splits[6], (D,), jnp.float32, math.log(0.5), math.log(4.0))), 0.5, 4.0)
    layer_logits = jnp.clip(jax.random.uniform(splits[7], (4,), jnp.float32, -1.0, 1.0), -1.0, 1.0)
    proj_weight = noise(splits[8], (D, PF), D ** -0.5, 0.109375, ((1, 2),))
    proj_bias = noise(splits[9], (PF,), 1.0, 5.0, ((0, 2),), jnp.float32)
    grad_out = noise(splits[10], (N_IMG * OWN_TILES, TILE_TOK, PF), 1.0, 6.0, ((0, 64), (2, 2)))
    return {"tokens": tokens, "tap_early": tap_early, "tap_mid": tap_mid, "tile_counts": tile_counts, "qkv_weight": qkv_weight, "out_weight": out_weight, "layer_scale": layer_scale, "layer_logits": layer_logits, "proj_weight": proj_weight, "proj_bias": proj_bias, "grad_out": grad_out}


inv_root_two = 0.7071067811865476
inv_root_tau = 0.3989422804014327

def tile_owners(tile_counts, tile_total, tile_group):
    counts_int = tile_counts.astype(jnp.int32)
    starts = jnp.cumsum(counts_int) - counts_int
    tile_index = jnp.arange(tile_total, dtype=jnp.int32)
    start_of = lax.optimization_barrier(jnp.max(jnp.where(starts[None, :] <= tile_index[:, None], starts[None, :], -1), axis=1))
    owner_of = (start_of // tile_group).astype(jnp.int32)
    owners_total = tile_total // tile_group
    edge_tiles = jnp.arange(owners_total + 1, dtype=jnp.int32) * tile_group
    first_tile = lax.optimization_barrier(jnp.min(jnp.where(starts[None, :] >= edge_tiles[:, None], starts[None, :], tile_total), axis=1))
    return (owner_of, first_tile.astype(jnp.int32))

def gelu_slope(values):
    cumulative = 0.5 * (1.0 + jax.scipy.special.erf(values * inv_root_two))
    return cumulative + values * jnp.exp(-0.5 * values * values) * inv_root_tau

def rms_rows(values):
    return values * lax.rsqrt(lax.optimization_barrier(jnp.mean(values * values, axis=-1, keepdims=True)) + 1e-06)

def round_trip(values):
    return lax.optimization_barrier(values.astype(jnp.bfloat16)).astype(jnp.float32)

def attend(qkv_tile):
    queries = qkv_tile[:, :, 0].astype(jnp.float32)
    keys_tile = qkv_tile[:, :, 1].astype(jnp.float32)
    values_tile = qkv_tile[:, :, 2].astype(jnp.float32)
    scores = jnp.einsum('pnd,qnd->npq', queries, keys_tile) / math.sqrt(HEAD_DIM)
    scores = scores - lax.optimization_barrier(jnp.max(scores, axis=-1, keepdims=True))
    raised = jnp.exp(scores)
    soft_weights = (raised / lax.optimization_barrier(jnp.sum(raised, axis=-1, keepdims=True))).astype(jnp.bfloat16)
    mixed = jnp.einsum('npq,qnd->pnd', soft_weights.astype(jnp.float32), values_tile)
    return mixed.astype(jnp.bfloat16).reshape(TILE_TOK, HEADS * HEAD_DIM)

def reference(tokens, tap_early, tap_mid, tile_counts, qkv_weight, out_weight, layer_scale, layer_logits, proj_weight, proj_bias, grad_out):
    flat_rows = TILES * TILE_TOK
    inputs = tokens.astype(jnp.float32).reshape(flat_rows, D)
    normed = rms_rows(inputs).astype(jnp.bfloat16)
    qkv_all = jnp.dot(normed, qkv_weight, preferred_element_type=jnp.float32).astype(jnp.bfloat16)
    qkv_all = qkv_all.reshape(TILES, TILE_TOK, HEADS, 3, HEAD_DIM)
    attended = lax.map(attend, qkv_all).reshape(flat_rows, HEADS * HEAD_DIM)
    heads_width = HEADS // N_HEAD * HEAD_DIM
    mixed_sum = jnp.zeros((flat_rows, D), jnp.float32)
    for member in range(N_HEAD):
        partial_sum = jnp.dot(attended[:, member * heads_width:(member + 1) * heads_width], out_weight[member * heads_width:(member + 1) * heads_width], preferred_element_type=jnp.float32)
        mixed_sum = mixed_sum + round_trip(partial_sum)
    layer_out = inputs + layer_scale * mixed_sum
    raised_logits = jnp.exp(layer_logits)
    mixing = raised_logits / jnp.sum(raised_logits)
    joined_rows = mixing[0] * tap_early.astype(jnp.float32).reshape(flat_rows, D) + mixing[1] * tap_mid.astype(jnp.float32).reshape(flat_rows, D) + mixing[2] * inputs + mixing[3] * layer_out
    centre = lax.optimization_barrier(jnp.mean(joined_rows, axis=-1, keepdims=True))
    shifted = joined_rows - centre
    inverse_std = lax.rsqrt(lax.optimization_barrier(jnp.mean(shifted * shifted, axis=-1, keepdims=True)) + 1e-05)
    normal_rows = shifted * inverse_std
    z_rows = normal_rows.astype(jnp.bfloat16)
    preact = jnp.dot(z_rows, proj_weight, preferred_element_type=jnp.float32) + proj_bias
    projected = jax.nn.gelu(preact, approximate=False).astype(jnp.bfloat16).reshape(TILES, TILE_TOK, PF)
    owner_of, first_tile = tile_owners(tile_counts, TILES, TG)
    slot_tiles = first_tile[:N_IMG, None] + jnp.arange(OWN_TILES, dtype=jnp.int32)[None, :]
    live_slots = slot_tiles < first_tile[1:, None]
    picked = jnp.take(projected, jnp.clip(slot_tiles, 0, TILES - 1).reshape(-1), axis=0).reshape(N_IMG, OWN_TILES, TILE_TOK, PF)
    owner_rows = jnp.where(live_slots[:, :, None, None], picked, jnp.zeros((), jnp.bfloat16)).reshape(N_IMG * OWN_TILES, TILE_TOK, PF)
    slot_of = jnp.arange(TILES, dtype=jnp.int32) - first_tile[owner_of]
    back_rows = jnp.take(grad_out, (owner_of * OWN_TILES + slot_of).astype(jnp.int32), axis=0).reshape(flat_rows, PF)
    slope_rows = (back_rows.astype(jnp.float32) * gelu_slope(preact)).astype(jnp.bfloat16)
    cols_width = PF // N_HEAD
    grad_norm = jnp.zeros((flat_rows, D), jnp.float32)
    for member in range(N_HEAD):
        partial_sum = jnp.dot(slope_rows[:, member * cols_width:(member + 1) * cols_width], proj_weight[:, member * cols_width:(member + 1) * cols_width].T, preferred_element_type=jnp.float32)
        grad_norm = grad_norm + round_trip(partial_sum)
    grad_joined = (grad_norm - lax.optimization_barrier(jnp.mean(grad_norm, axis=-1, keepdims=True)) - normal_rows * lax.optimization_barrier(jnp.mean(grad_norm * normal_rows, axis=-1, keepdims=True))) * inverse_std
    return (owner_rows, grad_joined.astype(jnp.bfloat16).reshape(TILES, TILE_TOK, D))
```

```python
import functools
import math

import jax
import jax.numpy as jnp
from jax import lax
from jax.experimental import pallas as pl
from jax.experimental.pallas import tpu as pltpu
from jax.sharding import Mesh, PartitionSpec as P

HEAD_DIM = 128
LINE = 4
IMG = ("z", "y", "x")
VMEM_BYTES = 56 * 1024 * 1024

inv_root_two = 0.7071067811865476
inv_root_tau = 0.3989422804014327


def swap(array):
    return lax.ppermute(array, "head", [(0, 1), (1, 0)])


def along_z(array, by):
    return lax.ppermute(array, "z", [(i, (i + by) % LINE) for i in range(LINE)])


def along_img(array, by):
    peers = lax.axis_size(IMG)
    pairs = [(i, i + by) for i in range(peers) if 0 <= i + by < peers]
    return lax.ppermute(array, IMG, pairs)


def tile_owners(tile_counts, tile_total, tile_group):
    starts = jnp.cumsum(tile_counts) - tile_counts
    tile_index = jnp.arange(tile_total, dtype=jnp.int32)
    start_of = jnp.max(
        jnp.where(starts[None, :] <= tile_index[:, None], starts[None, :], -1), axis=1
    )
    owner_of = start_of // tile_group
    owners_total = tile_total // tile_group
    edge_tiles = jnp.arange(owners_total + 1, dtype=jnp.int32) * tile_group
    first_tile = jnp.min(
        jnp.where(starts[None, :] >= edge_tiles[:, None], starts[None, :], tile_total), axis=1
    )
    return (owner_of, first_tile)


def norm_kernel(tokens_ref, out_ref, ordered):
    rows = tokens_ref[0].astype(jnp.float32)
    normed = rows * lax.rsqrt(jnp.mean(rows * rows, axis=-1, keepdims=True) + 1e-06)
    groups = LINE * LINE
    share = rows.shape[1] // (LINE * groups)
    for line in range(LINE):
        for group in range(groups):
            source = (line * groups + group) * share
            target = (group * LINE + line) * share
            ordered[:, target : target + share] = normed[:, source : source + share]
    out_ref[0] = ordered[...].astype(jnp.bfloat16)


def norm_rows(tokens):
    tiles, half, depth = tokens.shape
    block = 64
    spec = pl.BlockSpec((1, block, depth), lambda t, r: (t, r, 0))
    return pl.pallas_call(
        norm_kernel,
        grid=(tiles, half // block),
        out_shape=jax.ShapeDtypeStruct(tokens.shape, jnp.bfloat16),
        in_specs=[spec],
        out_specs=spec,
        scratch_shapes=[pltpu.VMEM((block, depth), jnp.float32)],
        compiler_params=pltpu.CompilerParams(vmem_limit_bytes=VMEM_BYTES),
        name="norm",
    )(tokens)


def attend_kernel(own_ref, other_ref, weight_ref, out_ref, total):
    step = pl.program_id(0)
    tiles, half, depth = own_ref.shape
    rows = jnp.concatenate(
        [own_ref[...].reshape(tiles * half, depth), other_ref[...].reshape(tiles * half, depth)], axis=0
    )
    part = jnp.dot(rows, weight_ref[...], preferred_element_type=jnp.float32)

    @pl.when(step == 0)
    def _():
        total[...] = part

    @pl.when(step > 0)
    def _():
        total[...] += part

    @pl.when(step == pl.num_programs(0) - 1)
    def _():
        heads = out_ref.shape[2] // HEAD_DIM
        for tile in range(tiles):
            for head in range(heads):

                def piece(kind):
                    start = (head * 3 + kind) * HEAD_DIM
                    columns = slice(start, start + HEAD_DIM)
                    low = total[tile * half : (tile + 1) * half, columns]
                    high = total[(tiles + tile) * half : (tiles + tile + 1) * half, columns]
                    return jnp.concatenate([low, high], axis=0).astype(jnp.bfloat16)

                scores = lax.dot_general(
                    piece(0), piece(1), (((1,), (1,)), ((), ())), preferred_element_type=jnp.float32
                ) * (1.0 / math.sqrt(HEAD_DIM))
                scores = scores - jnp.max(scores, axis=-1, keepdims=True)
                raised = jnp.exp(scores)
                soft = (raised / jnp.sum(raised, axis=-1, keepdims=True)).astype(jnp.bfloat16)
                mixed = jnp.dot(soft, piece(2), preferred_element_type=jnp.float32)
                out_ref[tile, :, head * HEAD_DIM : (head + 1) * HEAD_DIM] = mixed.astype(jnp.bfloat16)


def attend(own, other, weight):
    tiles, half, depth = own.shape
    width = weight.shape[1]
    out_width = width // 3
    block = 640
    return pl.pallas_call(
        attend_kernel,
        grid=(depth // block,),
        out_shape=jax.ShapeDtypeStruct((tiles, 2 * half, out_width), jnp.bfloat16),
        in_specs=[
            pl.BlockSpec((tiles, half, block), lambda k: (0, 0, k)),
            pl.BlockSpec((tiles, half, block), lambda k: (0, 0, k)),
            pl.BlockSpec((block, width), lambda k: (k, 0)),
        ],
        out_specs=pl.BlockSpec((tiles, 2 * half, out_width), lambda k: (0, 0, 0)),
        scratch_shapes=[pltpu.VMEM((2 * tiles * half, width), jnp.float32)],
        compiler_params=pltpu.CompilerParams(vmem_limit_bytes=VMEM_BYTES),
        cost_estimate=pl.CostEstimate(
            flops=2 * tiles * 2 * half * depth * width,
            bytes_accessed=2 * depth * width + 4 * tiles * half * depth,
            transcendentals=0,
        ),
        name="attend",
    )(own, other, weight)


def out_kernel(line_ref, *refs):
    attended = refs[:LINE]
    weights = refs[LINE : 2 * LINE]
    own_ref, other_ref = refs[2 * LINE :]
    tiles, half, block = own_ref.shape
    for part_ref, start in ((other_ref, half), (own_ref, 0)):
        total = None
        for rows_ref, weight_ref in zip(attended, weights):
            rows = rows_ref[:, start : start + half].reshape(tiles * half, rows_ref.shape[2])
            term = jnp.dot(rows, weight_ref[...], preferred_element_type=jnp.float32)
            total = term if total is None else total + term
        part_ref[...] = total.astype(jnp.bfloat16).reshape(tiles, half, block)


def out_project(line_arg, attended, out_weight):
    tiles, full, share = attended[0].shape
    half = full // 2
    depth = out_weight.shape[1]
    block = 640

    def weight_spec(k):
        return pl.BlockSpec((share, block), lambda n, line: ((line[0] + k) % LINE, n))

    part = pl.BlockSpec((tiles, half, block), lambda n, line: (0, 0, n))
    shape = jax.ShapeDtypeStruct((tiles, half, depth), jnp.bfloat16)
    return pl.pallas_call(
        out_kernel,
        grid_spec=pltpu.PrefetchScalarGridSpec(
            num_scalar_prefetch=1,
            grid=(depth // block,),
            in_specs=[pl.BlockSpec((tiles, full, share), lambda n, line: (0, 0, 0))] * LINE
            + [weight_spec(k) for k in range(LINE)],
            out_specs=[part, part],
        ),
        out_shape=[shape, shape],
        compiler_params=pltpu.CompilerParams(vmem_limit_bytes=VMEM_BYTES),
        cost_estimate=pl.CostEstimate(
            flops=2 * tiles * full * share * LINE * depth,
            bytes_accessed=2 * LINE * share * depth,
            transcendentals=0,
        ),
        name="out",
    )(line_arg, *attended, *([out_weight] * LINE))


def join_kernel(
    mixing_ref, tokens_ref, early_ref, mid_ref, own_ref, other_ref, scale_ref, z_ref, inverse_ref
):
    inputs = tokens_ref[0].astype(jnp.float32)
    attended_out = own_ref[0].astype(jnp.float32) + other_ref[0].astype(jnp.float32)
    layer_out = inputs + scale_ref[...] * attended_out
    joined = (
        mixing_ref[0] * early_ref[0].astype(jnp.float32)
        + mixing_ref[1] * mid_ref[0].astype(jnp.float32)
        + mixing_ref[2] * inputs
        + mixing_ref[3] * layer_out
    )
    centre = jnp.mean(joined, axis=-1, keepdims=True)
    shifted = joined - centre
    inverse = lax.rsqrt(jnp.mean(shifted * shifted, axis=-1, keepdims=True) + 1e-05)
    z_ref[0] = (shifted * inverse).astype(jnp.bfloat16)
    inverse_ref[0] = jnp.broadcast_to(inverse, inverse_ref.shape[1:])


def join_rows(mixing, tokens, early, mid, own, other, scale):
    tiles, half, depth = tokens.shape
    block = 32
    spec = pl.BlockSpec((1, block, depth), lambda t, r: (t, r, 0))
    return pl.pallas_call(
        join_kernel,
        grid=(tiles, half // block),
        out_shape=[
            jax.ShapeDtypeStruct(tokens.shape, jnp.bfloat16),
            jax.ShapeDtypeStruct((tiles, half, 128), jnp.float32),
        ],
        in_specs=[pl.BlockSpec(memory_space=pltpu.SMEM)]
        + [spec] * 5
        + [pl.BlockSpec((1, depth), lambda t, r: (0, 0))],
        out_specs=[spec, pl.BlockSpec((1, block, 128), lambda t, r: (t, r, 0))],
        compiler_params=pltpu.CompilerParams(vmem_limit_bytes=VMEM_BYTES),
        name="join",
    )(mixing, tokens, early, mid, own, other, scale)


def final_kernel(own_ref, other_ref, z_ref, inverse_ref, out_ref):
    grad = own_ref[0].astype(jnp.float32) + other_ref[0].astype(jnp.float32)
    normal = z_ref[0].astype(jnp.float32)
    mean = jnp.mean(grad, axis=-1, keepdims=True)
    along = jnp.mean(grad * normal, axis=-1, keepdims=True)
    out_ref[0] = ((grad - mean - normal * along) * inverse_ref[0, :, :1]).astype(jnp.bfloat16)


def final_rows(own, other, z_rows, inverse):
    tiles, half, depth = own.shape
    block = 32
    spec = pl.BlockSpec((1, block, depth), lambda t, r: (t, r, 0))
    return pl.pallas_call(
        final_kernel,
        grid=(tiles, half // block),
        out_shape=jax.ShapeDtypeStruct(own.shape, jnp.bfloat16),
        in_specs=[spec, spec, spec, pl.BlockSpec((1, block, 128), lambda t, r: (t, r, 0))],
        out_specs=spec,
        compiler_params=pltpu.CompilerParams(vmem_limit_bytes=VMEM_BYTES),
        name="final",
    )(own, other, z_rows, inverse)


def activate(preact):
    raised = jnp.exp(-0.5 * preact * preact)
    step = 1.0 / (1.0 + 0.3275911 * inv_root_two * jnp.abs(preact))
    series = 1.061405429 * step - 1.453152027
    series = series * step + 1.421413741
    series = series * step - 0.284496736
    series = series * step + 0.254829592
    tail = 0.5 * series * step * raised
    return jnp.where(preact >= 0.0, 1.0 - tail, tail), raised * inv_root_tau


def home_kernel(
    core_ref, own_ref, other_ref, weight_ref, bias_ref, back_own_ref, back_other_ref,
    projected_ref, grad_own_ref, grad_other_ref, own_total, other_total,
):
    step = pl.program_id(0)
    core = core_ref[0]
    tiles, half, depth = own_ref.shape
    block = weight_ref.shape[1]

    @pl.when(step == 0)
    def _():
        own_total[...] = jnp.zeros_like(own_total)
        other_total[...] = jnp.zeros_like(other_total)

    parts = (
        (own_ref, back_own_ref, own_total, core),
        (other_ref, back_other_ref, other_total, 1 - core),
    )
    for rows_ref, back_ref, total, place in parts:
        rows = rows_ref[...].reshape(tiles * half, depth)
        preact = jnp.dot(rows, weight_ref[...], preferred_element_type=jnp.float32) + bias_ref[...]
        cumulative, density = activate(preact)
        projected = (preact * cumulative).astype(jnp.bfloat16)
        projected_ref[:, pl.ds(place, 1)] = projected.reshape(tiles, 1, half, block)
        slope = cumulative + preact * density
        back = back_ref[...].reshape(tiles * half, block).astype(jnp.float32)
        slope_rows = (back * slope).astype(jnp.bfloat16)
        total[...] += lax.dot_general(
            slope_rows, weight_ref[...], (((1,), (1,)), ((), ())), preferred_element_type=jnp.float32
        )

    @pl.when(step == pl.num_programs(0) - 1)
    def _():
        grad_own_ref[...] = own_total[...].astype(jnp.bfloat16).reshape(tiles, half, depth)
        grad_other_ref[...] = other_total[...].astype(jnp.bfloat16).reshape(tiles, half, depth)


def home_rows(core, own, other, weight, bias, back):
    tiles, half, depth = own.shape
    width = weight.shape[1]
    block = 512
    back = back.reshape(tiles, 2, half, width)
    whole = pl.BlockSpec((tiles, half, depth), lambda n, c: (0, 0, 0))
    projected, grad_own, grad_other = pl.pallas_call(
        home_kernel,
        grid_spec=pltpu.PrefetchScalarGridSpec(
            num_scalar_prefetch=1,
            grid=(width // block,),
            in_specs=[
                whole,
                whole,
                pl.BlockSpec((depth, block), lambda n, c: (0, n)),
                pl.BlockSpec((1, block), lambda n, c: (0, n)),
                pl.BlockSpec((tiles, 1, half, block), lambda n, c: (0, c[0], 0, n)),
                pl.BlockSpec((tiles, 1, half, block), lambda n, c: (0, 1 - c[0], 0, n)),
            ],
            out_specs=[
                pl.BlockSpec((tiles, 2, half, block), lambda n, c: (0, 0, 0, n)),
                whole,
                whole,
            ],
            scratch_shapes=[
                pltpu.VMEM((tiles * half, depth), jnp.float32),
                pltpu.VMEM((tiles * half, depth), jnp.float32),
            ],
        ),
        out_shape=[
            jax.ShapeDtypeStruct((tiles, 2, half, width), jnp.bfloat16),
            jax.ShapeDtypeStruct((tiles, half, depth), jnp.bfloat16),
            jax.ShapeDtypeStruct((tiles, half, depth), jnp.bfloat16),
        ],
        compiler_params=pltpu.CompilerParams(vmem_limit_bytes=VMEM_BYTES),
        cost_estimate=pl.CostEstimate(
            flops=8 * tiles * half * depth * width,
            bytes_accessed=2 * depth * width,
            transcendentals=0,
        ),
        name="home",
    )(core, own, other, weight, bias, back, back)
    return projected.reshape(tiles, 2 * half, width), grad_own, grad_other


def owner_kernel(core_ref, own_ref, other_ref, weight_ref, bias_ref, projected_ref):
    core = core_ref[0]
    tiles, half, depth = own_ref.shape
    block = weight_ref.shape[1]
    for rows_ref, place in ((own_ref, core), (other_ref, 1 - core)):
        rows = rows_ref[...].reshape(tiles * half, depth)
        preact = jnp.dot(rows, weight_ref[...], preferred_element_type=jnp.float32) + bias_ref[...]
        projected = (preact * activate(preact)[0]).astype(jnp.bfloat16)
        projected_ref[:, pl.ds(place, 1)] = projected.reshape(tiles, 1, half, block)


def owner_project(core, own, other, weight, bias):
    tiles, half, depth = own.shape
    width = weight.shape[1]
    block = 512
    whole = pl.BlockSpec((tiles, half, depth), lambda n, c: (0, 0, 0))
    projected = pl.pallas_call(
        owner_kernel,
        grid_spec=pltpu.PrefetchScalarGridSpec(
            num_scalar_prefetch=1,
            grid=(width // block,),
            in_specs=[
                whole,
                whole,
                pl.BlockSpec((depth, block), lambda n, c: (0, n)),
                pl.BlockSpec((1, block), lambda n, c: (0, n)),
            ],
            out_specs=pl.BlockSpec((tiles, 2, half, block), lambda n, c: (0, 0, 0, n)),
        ),
        out_shape=jax.ShapeDtypeStruct((tiles, 2, half, width), jnp.bfloat16),
        compiler_params=pltpu.CompilerParams(vmem_limit_bytes=VMEM_BYTES),
        cost_estimate=pl.CostEstimate(
            flops=4 * tiles * half * depth * width,
            bytes_accessed=2 * depth * width,
            transcendentals=0,
        ),
        name="owner",
    )(core, own, other, weight, bias)
    return projected.reshape(tiles, 2 * half, width)


def on_device(
    tokens, tap_early, tap_mid, tile_counts, qkv_weight, out_weight, layer_scale, layer_logits,
    proj_weight, proj_bias, grad_out,
):
    tile_group, token_share, depth = tokens.shape
    img_count = lax.axis_size(IMG)
    place = lax.axis_index(IMG)
    line_place = lax.axis_index("z")
    core = lax.axis_index("head")
    core_arg = core.astype(jnp.int32).reshape(1)
    tile_total = tile_group * img_count
    own_tiles = grad_out.shape[0]
    owner_of, first_tile = tile_owners(tile_counts, tile_total, tile_group)
    my_first = first_tile[place]

    far_back = []
    for within in range(tile_group):
        tile = (place + 2) * tile_group + within
        slot = jnp.clip(tile - my_first, 0, own_tiles - 1)
        far_back.append(along_img(lax.dynamic_slice_in_dim(grad_out, slot, 1, axis=0), 2))
    slot = jnp.clip((place + 1) * tile_group - my_first, 0, own_tiles - tile_group)
    near_back = along_img(lax.dynamic_slice_in_dim(grad_out, slot, tile_group, axis=0), 1)

    depth_share, width = qkv_weight.shape
    share = width // LINE
    received = []
    for distance in range(LINE):
        target = (line_place + distance) % LINE
        columns = lax.dynamic_slice_in_dim(qkv_weight, target * share, share, axis=1)
        received.append(along_z(columns, distance) if distance else columns)
    ladder = jnp.stack([received[(LINE - 1 - j) % LINE] for j in range(2 * LINE - 1)], axis=0)
    sent = lax.dynamic_slice_in_dim(ladder, LINE - 1 - line_place, LINE, axis=0)
    gathered = lax.all_gather(sent.reshape(LINE * depth_share, share), ("y", "x"), axis=0, tiled=True)
    weight = gathered

    normed = norm_rows(tokens)
    from_low = along_z(normed, 1)
    from_high = along_z(normed, -1)
    from_low, from_high, far_back[0] = lax.optimization_barrier((from_low, from_high, far_back[0]))
    far_first = along_z(from_low[:1], 1)
    far_second = along_z(from_high[1:], -1)
    far_first, far_second, far_back[1] = lax.optimization_barrier((far_first, far_second, far_back[1]))
    from_far = jnp.concatenate([far_first, far_second], axis=0)
    att_far = along_z(attend(from_far, swap(from_far), weight), 2)
    att_low = along_z(attend(from_low, swap(from_low), weight), -1)
    att_high = along_z(attend(from_high, swap(from_high), weight), 1)
    att_own = attend(normed, swap(normed), weight)
    part_own, part_other = out_project(
        line_place.astype(jnp.int32).reshape(1), [att_own, att_low, att_far, att_high], out_weight
    )
    raised_logits = jnp.exp(layer_logits)
    mixing = raised_logits / jnp.sum(raised_logits)
    z_rows, inverse_std = join_rows(
        mixing, tokens, tap_early, tap_mid, part_own, swap(part_other), layer_scale.reshape(1, -1)
    )

    near = along_img(z_rows, -1)
    far = along_img(z_rows, -2)

    back = []
    for within in range(tile_group):
        tile = place * tile_group + within
        owner = owner_of[tile]
        slot = jnp.clip(tile - my_first, 0, own_tiles - 1)
        here = lax.dynamic_index_in_dim(grad_out, slot, axis=0, keepdims=False)
        back.append(
            jnp.where(
                owner == place,
                here,
                jnp.where(owner == place - 1, near_back[within], far_back[within][0]),
            )
        )
    back_rows = jnp.stack(back, axis=0)

    bias = proj_bias.reshape(1, -1)
    projected, grad_own, grad_other = home_rows(
        core_arg, z_rows, swap(z_rows), proj_weight, bias, back_rows
    )
    grad_joined = final_rows(grad_own, swap(grad_other), z_rows, inverse_std)

    near_projected = owner_project(core_arg, near, swap(near), proj_weight, bias)
    far_projected = owner_project(core_arg, far, swap(far), proj_weight, bias)

    offset = my_first - place * tile_group
    held = first_tile[place + 1] - my_first
    at_hand = [
        source[within]
        for source in (projected, near_projected, far_projected)
        for within in range(tile_group)
    ]
    slots = []
    for slot in range(own_tiles):
        later = at_hand[min(slot + 1, len(at_hand) - 1)]
        picked = jnp.where(offset == 0, at_hand[slot], later)
        slots.append(jnp.where(slot < held, picked, jnp.zeros((), jnp.bfloat16)))
    owner_rows = jnp.stack(slots, axis=0)
    return (owner_rows, grad_joined)


def solution(mesh):
    cores = mesh.devices.shape[-1]
    inner = Mesh(mesh.devices.reshape(LINE, LINE, LINE, cores), IMG + ("head",))
    return jax.shard_map(
        on_device,
        mesh=inner,
        in_specs=(
            P(IMG, "head", None),
            P(IMG, "head", None),
            P(IMG, "head", None),
            P(),
            P(IMG, "head"),
            P("head", None),
            P(),
            P(),
            P(None, "head"),
            P("head"),
            P(IMG, None, "head"),
        ),
        out_specs=(P(IMG, None, "head"), P(IMG, "head", None)),
        check_vma=False,
    )
```

```python
import functools
import math

import jax
import jax.numpy as jnp
from jax import lax
from jax.experimental import pallas as pl
from jax.experimental.pallas import tpu as pltpu
from jax.sharding import Mesh, PartitionSpec as P

HEAD_DIM = 128
LINE = 4
IMG = ("z", "y", "x")
VMEM_BYTES = 56 * 1024 * 1024

inv_root_two = 0.7071067811865476
inv_root_tau = 0.3989422804014327


def swap(array):
    return lax.ppermute(array, "head", [(0, 1), (1, 0)])


def along_z(array, by):
    return lax.ppermute(array, "z", [(i, (i + by) % LINE) for i in range(LINE)])


def along_img(array, by):
    peers = lax.axis_size(IMG)
    pairs = [(i, i + by) for i in range(peers) if 0 <= i + by < peers]
    return lax.ppermute(array, IMG, pairs)


def around(place, side):
    return place - place % LINE + (place % LINE + side) % LINE


def two_on(array, by):
    peers = lax.axis_size(IMG)
    side = -by // 2
    ends = [(i, i + by) for i in range(peers) if 0 <= i + by < peers]
    halfway = lax.ppermute(array, IMG, [(i, around(i, side)) for i, _ in ends])
    return halfway, lambda held: lax.ppermute(held, IMG, [(around(i, side), j) for i, j in ends])


def tile_owners(tile_counts, tile_total, tile_group):
    starts = jnp.cumsum(tile_counts) - tile_counts
    tile_index = jnp.arange(tile_total, dtype=jnp.int32)
    start_of = jnp.max(
        jnp.where(starts[None, :] <= tile_index[:, None], starts[None, :], -1), axis=1
    )
    owner_of = start_of // tile_group
    owners_total = tile_total // tile_group
    edge_tiles = jnp.arange(owners_total + 1, dtype=jnp.int32) * tile_group
    first_tile = jnp.min(
        jnp.where(starts[None, :] >= edge_tiles[:, None], starts[None, :], tile_total), axis=1
    )
    return (owner_of, first_tile)


def norm_kernel(tokens_ref, out_ref, ordered):
    rows = tokens_ref[0].astype(jnp.float32)
    normed = rows * lax.rsqrt(jnp.mean(rows * rows, axis=-1, keepdims=True) + 1e-06)
    groups = LINE * LINE
    share = rows.shape[1] // (LINE * groups)
    for line in range(LINE):
        for group in range(groups):
            source = (line * groups + group) * share
            target = (group * LINE + line) * share
            ordered[:, target : target + share] = normed[:, source : source + share]
    out_ref[0] = ordered[...].astype(jnp.bfloat16)


def norm_rows(tokens):
    tiles, half, depth = tokens.shape
    block = 64
    spec = pl.BlockSpec((1, block, depth), lambda t, r: (t, r, 0))
    return pl.pallas_call(
        norm_kernel,
        grid=(tiles, half // block),
        out_shape=jax.ShapeDtypeStruct(tokens.shape, jnp.bfloat16),
        in_specs=[spec],
        out_specs=spec,
        scratch_shapes=[pltpu.VMEM((block, depth), jnp.float32)],
        compiler_params=pltpu.CompilerParams(vmem_limit_bytes=VMEM_BYTES),
        name="norm",
    )(tokens)


def attend_kernel(own_ref, other_ref, weight_ref, out_ref, total):
    step = pl.program_id(0)
    tiles, half, depth = own_ref.shape
    rows = jnp.concatenate(
        [own_ref[...].reshape(tiles * half, depth), other_ref[...].reshape(tiles * half, depth)], axis=0
    )
    part = jnp.dot(rows, weight_ref[...], preferred_element_type=jnp.float32)

    @pl.when(step == 0)
    def _():
        total[...] = part

    @pl.when(step > 0)
    def _():
        total[...] += part

    @pl.when(step == pl.num_programs(0) - 1)
    def _():
        heads = out_ref.shape[2] // HEAD_DIM
        for tile in range(tiles):
            for head in range(heads):

                def piece(kind):
                    start = (head * 3 + kind) * HEAD_DIM
                    columns = slice(start, start + HEAD_DIM)
                    low = total[tile * half : (tile + 1) * half, columns]
                    high = total[(tiles + tile) * half : (tiles + tile + 1) * half, columns]
                    return jnp.concatenate([low, high], axis=0).astype(jnp.bfloat16)

                scores = lax.dot_general(
                    piece(0), piece(1), (((1,), (1,)), ((), ())), preferred_element_type=jnp.float32
                ) * (1.0 / math.sqrt(HEAD_DIM))
                scores = scores - jnp.max(scores, axis=-1, keepdims=True)
                raised = jnp.exp(scores)
                soft = (raised / jnp.sum(raised, axis=-1, keepdims=True)).astype(jnp.bfloat16)
                mixed = jnp.dot(soft, piece(2), preferred_element_type=jnp.float32)
                out_ref[tile, :, head * HEAD_DIM : (head + 1) * HEAD_DIM] = mixed.astype(jnp.bfloat16)


def attend(own, other, weight):
    tiles, half, depth = own.shape
    width = weight.shape[1]
    out_width = width // 3
    block = 640
    return pl.pallas_call(
        attend_kernel,
        grid=(depth // block,),
        out_shape=jax.ShapeDtypeStruct((tiles, 2 * half, out_width), jnp.bfloat16),
        in_specs=[
            pl.BlockSpec((tiles, half, block), lambda k: (0, 0, k)),
            pl.BlockSpec((tiles, half, block), lambda k: (0, 0, k)),
            pl.BlockSpec((block, width), lambda k: (k, 0)),
        ],
        out_specs=pl.BlockSpec((tiles, 2 * half, out_width), lambda k: (0, 0, 0)),
        scratch_shapes=[pltpu.VMEM((2 * tiles * half, width), jnp.float32)],
        compiler_params=pltpu.CompilerParams(vmem_limit_bytes=VMEM_BYTES),
        cost_estimate=pl.CostEstimate(
            flops=2 * tiles * 2 * half * depth * width,
            bytes_accessed=2 * depth * width + 4 * tiles * half * depth,
            transcendentals=0,
        ),
        name="attend",
    )(own, other, weight)


def out_kernel(start, line_ref, *refs):
    attended = refs[:LINE]
    weights = refs[LINE : 2 * LINE]
    part_ref = refs[2 * LINE]
    tiles, half, block = part_ref.shape
    total = None
    for rows_ref, weight_ref in zip(attended, weights):
        rows = rows_ref[...].reshape(tiles * half, rows_ref.shape[2])
        term = jnp.dot(rows, weight_ref[...], preferred_element_type=jnp.float32)
        total = term if total is None else total + term
    part_ref[...] = total.astype(jnp.bfloat16).reshape(tiles, half, block)


def out_project(line_arg, attended, out_weight, part):
    tiles, full, share = attended[0].shape
    half = full // 2
    depth = out_weight.shape[1]
    block = 640

    def weight_spec(k):
        return pl.BlockSpec((share, block), lambda n, line: ((line[0] + k) % LINE, n))

    return pl.pallas_call(
        functools.partial(out_kernel, part),
        grid_spec=pltpu.PrefetchScalarGridSpec(
            num_scalar_prefetch=1,
            grid=(depth // block,),
            in_specs=[pl.BlockSpec((tiles, half, share), lambda n, line: (0, part, 0))] * LINE
            + [weight_spec(k) for k in range(LINE)],
            out_specs=pl.BlockSpec((tiles, half, block), lambda n, line: (0, 0, n)),
        ),
        out_shape=jax.ShapeDtypeStruct((tiles, half, depth), jnp.bfloat16),
        compiler_params=pltpu.CompilerParams(vmem_limit_bytes=VMEM_BYTES),
        cost_estimate=pl.CostEstimate(
            flops=2 * tiles * full * share * LINE * depth,
            bytes_accessed=2 * LINE * share * depth,
            transcendentals=0,
        ),
        name="out",
    )(line_arg, *attended, *([out_weight] * LINE))


def join_kernel(
    mixing_ref, tokens_ref, early_ref, mid_ref, own_ref, other_ref, scale_ref, z_ref, inverse_ref
):
    inputs = tokens_ref[0].astype(jnp.float32)
    attended_out = own_ref[0].astype(jnp.float32) + other_ref[0].astype(jnp.float32)
    joined = (
        mixing_ref[0] * early_ref[0].astype(jnp.float32)
        + mixing_ref[1] * mid_ref[0].astype(jnp.float32)
        + (mixing_ref[2] + mixing_ref[3]) * inputs
        + (mixing_ref[3] * scale_ref[...]) * attended_out
    )
    centre = jnp.mean(joined, axis=-1, keepdims=True)
    shifted = joined - centre
    inverse = lax.rsqrt(jnp.mean(shifted * shifted, axis=-1, keepdims=True) + 1e-05)
    z_ref[0] = (shifted * inverse).astype(jnp.bfloat16)
    inverse_ref[0] = jnp.broadcast_to(inverse, inverse_ref.shape[1:])


def join_rows(mixing, tokens, early, mid, own, other, scale):
    tiles, half, depth = tokens.shape
    block = 64
    spec = pl.BlockSpec((1, block, depth), lambda t, r: (t, r, 0))
    return pl.pallas_call(
        join_kernel,
        grid=(tiles, half // block),
        out_shape=[
            jax.ShapeDtypeStruct(tokens.shape, jnp.bfloat16),
            jax.ShapeDtypeStruct((tiles, half, 128), jnp.float32),
        ],
        in_specs=[pl.BlockSpec(memory_space=pltpu.SMEM)]
        + [spec] * 5
        + [pl.BlockSpec((1, depth), lambda t, r: (0, 0))],
        out_specs=[spec, pl.BlockSpec((1, block, 128), lambda t, r: (t, r, 0))],
        compiler_params=pltpu.CompilerParams(vmem_limit_bytes=VMEM_BYTES),
        name="join",
    )(mixing, tokens, early, mid, own, other, scale)


def final_kernel(own_ref, other_ref, z_ref, inverse_ref, out_ref):
    grad = own_ref[0].astype(jnp.float32) + other_ref[0].astype(jnp.float32)
    normal = z_ref[0].astype(jnp.float32)
    mean = jnp.mean(grad, axis=-1, keepdims=True)
    along = jnp.mean(grad * normal, axis=-1, keepdims=True)
    out_ref[0] = ((grad - mean - normal * along) * inverse_ref[0, :, :1]).astype(jnp.bfloat16)


def final_rows(own, other, z_rows, inverse):
    tiles, half, depth = own.shape
    block = 64
    spec = pl.BlockSpec((1, block, depth), lambda t, r: (t, r, 0))
    return pl.pallas_call(
        final_kernel,
        grid=(tiles, half // block),
        out_shape=jax.ShapeDtypeStruct(own.shape, jnp.bfloat16),
        in_specs=[spec, spec, spec, pl.BlockSpec((1, block, 128), lambda t, r: (t, r, 0))],
        out_specs=spec,
        compiler_params=pltpu.CompilerParams(vmem_limit_bytes=VMEM_BYTES),
        name="final",
    )(own, other, z_rows, inverse)


def activate(preact):
    raised = jnp.exp(-0.5 * preact * preact)
    step = 1.0 / (1.0 + 0.3275911 * inv_root_two * jnp.abs(preact))
    series = 1.061405429 * step - 1.453152027
    series = series * step + 1.421413741
    series = series * step - 0.284496736
    series = series * step + 0.254829592
    tail = 0.5 * series * step * raised
    return jnp.where(preact >= 0.0, 1.0 - tail, tail), raised * inv_root_tau


def home_kernel(
    core_ref, own_ref, other_ref, weight_ref, bias_ref, back_own_ref, back_other_ref,
    projected_ref, grad_own_ref, grad_other_ref, own_total, other_total,
):
    step = pl.program_id(0)
    core = core_ref[0]
    tiles, half, depth = own_ref.shape
    block = weight_ref.shape[1]

    @pl.when(step == 0)
    def _():
        own_total[...] = jnp.zeros_like(own_total)
        other_total[...] = jnp.zeros_like(other_total)

    parts = (
        (own_ref, back_own_ref, own_total, core),
        (other_ref, back_other_ref, other_total, 1 - core),
    )
    for rows_ref, back_ref, total, place in parts:
        rows = rows_ref[...].reshape(tiles * half, depth)
        preact = jnp.dot(rows, weight_ref[...], preferred_element_type=jnp.float32) + bias_ref[...]
        cumulative, density = activate(preact)
        projected = (preact * cumulative).astype(jnp.bfloat16)
        projected_ref[:, pl.ds(place, 1)] = projected.reshape(tiles, 1, half, block)
        slope = cumulative + preact * density
        back = back_ref[...].reshape(tiles * half, block).astype(jnp.float32)
        slope_rows = (back * slope).astype(jnp.bfloat16)
        total[...] += lax.dot_general(
            slope_rows, weight_ref[...], (((1,), (1,)), ((), ())), preferred_element_type=jnp.float32
        )

    @pl.when(step == pl.num_programs(0) - 1)
    def _():
        grad_own_ref[...] = own_total[...].astype(jnp.bfloat16).reshape(tiles, half, depth)
        grad_other_ref[...] = other_total[...].astype(jnp.bfloat16).reshape(tiles, half, depth)


def home_rows(core, own, other, weight, bias, back):
    tiles, half, depth = own.shape
    width = weight.shape[1]
    block = 512
    back = back.reshape(tiles, 2, half, width)
    whole = pl.BlockSpec((tiles, half, depth), lambda n, c: (0, 0, 0))
    projected, grad_own, grad_other = pl.pallas_call(
        home_kernel,
        grid_spec=pltpu.PrefetchScalarGridSpec(
            num_scalar_prefetch=1,
            grid=(width // block,),
            in_specs=[
                whole,
                whole,
                pl.BlockSpec((depth, block), lambda n, c: (0, n)),
                pl.BlockSpec((1, block), lambda n, c: (0, n)),
                pl.BlockSpec((tiles, 1, half, block), lambda n, c: (0, c[0], 0, n)),
                pl.BlockSpec((tiles, 1, half, block), lambda n, c: (0, 1 - c[0], 0, n)),
            ],
            out_specs=[
                pl.BlockSpec((tiles, 2, half, block), lambda n, c: (0, 0, 0, n)),
                whole,
                whole,
            ],
            scratch_shapes=[
                pltpu.VMEM((tiles * half, depth), jnp.float32),
                pltpu.VMEM((tiles * half, depth), jnp.float32),
            ],
        ),
        out_shape=[
            jax.ShapeDtypeStruct((tiles, 2, half, width), jnp.bfloat16),
            jax.ShapeDtypeStruct((tiles, half, depth), jnp.bfloat16),
            jax.ShapeDtypeStruct((tiles, half, depth), jnp.bfloat16),
        ],
        compiler_params=pltpu.CompilerParams(vmem_limit_bytes=VMEM_BYTES),
        cost_estimate=pl.CostEstimate(
            flops=8 * tiles * half * depth * width,
            bytes_accessed=2 * depth * width,
            transcendentals=0,
        ),
        name="home",
    )(core, own, other, weight, bias, back, back)
    return projected.reshape(tiles, 2 * half, width), grad_own, grad_other


def owner_kernel(core_ref, own_ref, other_ref, weight_ref, bias_ref, projected_ref):
    core = core_ref[0]
    tiles, half, depth = own_ref.shape
    block = weight_ref.shape[1]
    rows = jnp.concatenate(
        [own_ref[...].reshape(tiles * half, depth), other_ref[...].reshape(tiles * half, depth)], axis=0
    )
    preact = jnp.dot(rows, weight_ref[...], preferred_element_type=jnp.float32) + bias_ref[...]
    projected = (preact * activate(preact)[0]).astype(jnp.bfloat16)
    projected = projected.reshape(2, tiles, 1, half, block)
    projected_ref[:, pl.ds(core, 1)] = projected[0]
    projected_ref[:, pl.ds(1 - core, 1)] = projected[1]


def owner_project(core, own, other, weight, bias):
    tiles, half, depth = own.shape
    width = weight.shape[1]
    block = 512
    whole = pl.BlockSpec((tiles, half, depth), lambda n, c: (0, 0, 0))
    projected = pl.pallas_call(
        owner_kernel,
        grid_spec=pltpu.PrefetchScalarGridSpec(
            num_scalar_prefetch=1,
            grid=(width // block,),
            in_specs=[
                whole,
                whole,
                pl.BlockSpec((depth, block), lambda n, c: (0, n)),
                pl.BlockSpec((1, block), lambda n, c: (0, n)),
            ],
            out_specs=pl.BlockSpec((tiles, 2, half, block), lambda n, c: (0, 0, 0, n)),
        ),
        out_shape=jax.ShapeDtypeStruct((tiles, 2, half, width), jnp.bfloat16),
        compiler_params=pltpu.CompilerParams(vmem_limit_bytes=VMEM_BYTES),
        cost_estimate=pl.CostEstimate(
            flops=4 * tiles * half * depth * width,
            bytes_accessed=2 * depth * width,
            transcendentals=0,
        ),
        name="owner",
    )(core, own, other, weight, bias)
    return projected.reshape(tiles, 2 * half, width)


def on_device(
    tokens, tap_early, tap_mid, tile_counts, qkv_weight, out_weight, layer_scale, layer_logits,
    proj_weight, proj_bias, grad_out,
):
    tile_group, token_share, depth = tokens.shape
    img_count = lax.axis_size(IMG)
    place = lax.axis_index(IMG)
    line_place = lax.axis_index("z")
    core = lax.axis_index("head")
    core_arg = core.astype(jnp.int32).reshape(1)
    tile_total = tile_group * img_count
    own_tiles = grad_out.shape[0]
    owner_of, first_tile = tile_owners(tile_counts, tile_total, tile_group)
    my_first = first_tile[place]

    depth_share, width = qkv_weight.shape
    share = width // LINE
    received = []
    for distance in range(LINE):
        target = (line_place + distance) % LINE
        columns = lax.dynamic_slice_in_dim(qkv_weight, target * share, share, axis=1)
        received.append(along_z(columns, distance) if distance else columns)
    normed = norm_rows(tokens)
    normed, received = lax.optimization_barrier((normed, received))
    ladder = jnp.stack([received[(LINE - 1 - j) % LINE] for j in range(2 * LINE - 1)], axis=0)
    sent = lax.dynamic_slice_in_dim(ladder, LINE - 1 - line_place, LINE, axis=0)
    weight = lax.all_gather(sent.reshape(LINE * depth_share, share), ("y", "x"), axis=0, tiled=True)

    from_low = along_z(normed, 1)
    from_high = along_z(normed, -1)
    far_first = along_z(from_low[:1], 1)
    far_second = along_z(from_high[1:], -1)
    far_first, far_second, weight, first_slot = lax.optimization_barrier(
        (far_first, far_second, weight, my_first)
    )
    packets = []
    for distance in (1, 2):
        for within in range(tile_group):
            tile = (place + distance) * tile_group + within
            slot = jnp.clip(tile - first_slot, 0, own_tiles - 1)
            packets.append(lax.dynamic_slice_in_dim(grad_out, slot, 1, axis=0))
    halfway, far_on = two_on(packets[3], 2)
    near_back = [along_img(packets[0], 1)]

    from_far = jnp.concatenate([far_first, far_second], axis=0)
    att_far = along_z(attend(from_far, swap(from_far), weight), 2)
    att_low = along_z(attend(from_low, swap(from_low), weight), -1)
    att_high = along_z(attend(from_high, swap(from_high), weight), 1)
    att_own = attend(normed, swap(normed), weight)
    att_own, halfway, near_back[0], packets[1] = lax.optimization_barrier(
        (att_own, halfway, near_back[0], packets[1])
    )
    near_back.append(along_img(packets[1], 1))
    far_back = [None, far_on(halfway)]
    attended = [att_own, att_low, att_far, att_high]
    line_arg = line_place.astype(jnp.int32).reshape(1)
    part_other = swap(out_project(line_arg, attended, out_weight, 1))
    part_own = out_project(line_arg, attended, out_weight, 0)
    part_own, part_other, far_back[1], near_back[1], packets[2] = lax.optimization_barrier(
        (part_own, part_other, far_back[1], near_back[1], packets[2])
    )
    far_back[0] = along_img(packets[2], 2)
    raised_logits = jnp.exp(layer_logits)
    mixing = raised_logits / jnp.sum(raised_logits)
    z_rows, inverse_std = join_rows(
        mixing, tokens, tap_early, tap_mid, part_own, part_other, layer_scale.reshape(1, -1)
    )

    halfway, far_on = two_on(z_rows[1:], -2)
    far_first = along_img(z_rows[:1], -2)
    near_first = along_img(z_rows[:1], -1)
    near_first, halfway, second = lax.optimization_barrier((near_first, halfway, z_rows[1:]))
    near_second = along_img(second, -1)
    far_second = far_on(halfway)

    back = []
    for within in range(tile_group):
        tile = place * tile_group + within
        owner = owner_of[tile]
        slot = jnp.clip(tile - my_first, 0, own_tiles - 1)
        here = lax.dynamic_index_in_dim(grad_out, slot, axis=0, keepdims=False)
        back.append(
            jnp.where(
                owner == place,
                here,
                jnp.where(owner == place - 1, near_back[within][0], far_back[within][0]),
            )
        )
    back_rows = jnp.stack(back, axis=0)

    bias = proj_bias.reshape(1, -1)
    projected, grad_own, grad_other = home_rows(
        core_arg, z_rows, swap(z_rows), proj_weight, bias, back_rows
    )
    far_first, _ = lax.optimization_barrier((far_first, grad_other))
    grad_joined = final_rows(grad_own, swap(grad_other), z_rows, inverse_std)
    far_second, _ = lax.optimization_barrier((far_second, grad_joined))
    near_second, _ = lax.optimization_barrier((near_second, grad_joined))
    guests = [
        owner_project(core_arg, rows, swap(rows), proj_weight, bias)
        for rows in (near_first, near_second, far_first, far_second)
    ]

    offset = my_first - place * tile_group
    held = first_tile[place + 1] - my_first
    at_hand = [tile for source in (projected, *guests) for tile in source]
    slots = []
    for slot in range(own_tiles):
        later = at_hand[min(slot + 1, len(at_hand) - 1)]
        picked = jnp.where(offset == 0, at_hand[slot], later)
        slots.append(jnp.where(slot < held, picked, jnp.zeros((), jnp.bfloat16)))
    owner_rows = jnp.stack(slots, axis=0)
    return (owner_rows, grad_joined)


def solution(mesh):
    cores = mesh.devices.shape[-1]
    inner = Mesh(mesh.devices.reshape(LINE, LINE, LINE, cores), IMG + ("head",))
    return jax.shard_map(
        on_device,
        mesh=inner,
        in_specs=(
            P(IMG, "head", None),
            P(IMG, "head", None),
            P(IMG, "head", None),
            P(),
            P(IMG, "head"),
            P("head", None),
            P(),
            P(),
            P(None, "head"),
            P("head"),
            P(IMG, None, "head"),
        ),
        out_specs=(P(IMG, None, "head"), P(IMG, "head", None)),
        check_vma=False,
    )
```

```python
import functools
import math

import jax
import jax.numpy as jnp
from jax import lax
from jax.experimental import pallas as pl
from jax.experimental.pallas import tpu as pltpu
from jax.sharding import Mesh, PartitionSpec as P

HEAD_DIM = 128
LINE = 4
IMG = ("z", "y", "x")
VMEM_BYTES = 56 * 1024 * 1024
SMALL_COST = pl.CostEstimate(flops=1, bytes_accessed=1, transcendentals=0)

inv_root_two = 0.7071067811865476
inv_root_tau = 0.3989422804014327


def swap(array):
    return lax.ppermute(array, "head", [(0, 1), (1, 0)])


def along_z(array, by):
    return lax.ppermute(array, "z", [(i, (i + by) % LINE) for i in range(LINE)])


def along_img(array, by):
    peers = lax.axis_size(IMG)
    pairs = [(i, i + by) for i in range(peers) if 0 <= i + by < peers]
    return lax.ppermute(array, IMG, pairs)


def around(place, side):
    return place - place % LINE + (place % LINE + side) % LINE


def ring_x(array, by):
    peers = lax.axis_size(IMG)
    return lax.ppermute(array, IMG, [(i, around(i, by)) for i in range(peers)])


def next_line(array, columns):
    peers = lax.axis_size(IMG)
    pairs = [(i, i + LINE) for i in range(peers - LINE) if i % LINE < columns]
    return lax.ppermute(array, IMG, pairs)


def two_back(array):
    peers = lax.axis_size(IMG)

    def middle(i):
        return i - LINE + 1 if i % LINE == 1 else around(i, 1)

    ends = [(i, i - 2) for i in range(2, peers)]
    halfway = lax.ppermute(array, IMG, [(i, middle(i)) for i, _ in ends])
    return halfway, lambda held: lax.ppermute(held, IMG, [(middle(i), j) for i, j in ends])


def tile_owners(tile_counts, tile_total, tile_group):
    starts = jnp.cumsum(tile_counts) - tile_counts
    tile_index = jnp.arange(tile_total, dtype=jnp.int32)
    start_of = jnp.max(
        jnp.where(starts[None, :] <= tile_index[:, None], starts[None, :], -1), axis=1
    )
    owner_of = start_of // tile_group
    owners_total = tile_total // tile_group
    edge_tiles = jnp.arange(owners_total + 1, dtype=jnp.int32) * tile_group
    first_tile = jnp.min(
        jnp.where(starts[None, :] >= edge_tiles[:, None], starts[None, :], tile_total), axis=1
    )
    return (owner_of, first_tile)


def norm_kernel(tokens_ref, out_ref, ordered):
    rows = tokens_ref[0].astype(jnp.float32)
    normed = rows * lax.rsqrt(jnp.mean(rows * rows, axis=-1, keepdims=True) + 1e-06)
    groups = LINE * LINE
    share = rows.shape[1] // (LINE * groups)
    for line in range(LINE):
        for group in range(groups):
            source = (line * groups + group) * share
            target = (group * LINE + line) * share
            ordered[:, target : target + share] = normed[:, source : source + share]
    out_ref[0] = ordered[...].astype(jnp.bfloat16)


def norm_rows(tokens):
    tiles, half, depth = tokens.shape
    block = 64
    spec = pl.BlockSpec((1, block, depth), lambda t, r: (t, r, 0))
    return pl.pallas_call(
        norm_kernel,
        grid=(tiles, half // block),
        out_shape=jax.ShapeDtypeStruct(tokens.shape, jnp.bfloat16),
        in_specs=[spec],
        out_specs=spec,
        scratch_shapes=[pltpu.VMEM((block, depth), jnp.float32)],
        compiler_params=pltpu.CompilerParams(vmem_limit_bytes=VMEM_BYTES),
        cost_estimate=SMALL_COST,
        name="norm",
    )(tokens)


def attend_kernel(count, *refs):
    sources, weight_hbm = refs[: 2 * count], refs[2 * count]
    outs = refs[2 * count + 1 : 3 * count + 1]
    rows, weight, qkv, row_sems, weight_sem = refs[3 * count + 1 :]
    _, _, tiles, half, depth = rows.shape
    heads = weight.shape[1] // (3 * HEAD_DIM)

    def fetch(index):
        slot = index % 2
        return [
            pltpu.make_async_copy(sources[2 * index + part], rows.at[slot, part], row_sems.at[slot, part])
            for part in range(2)
        ]

    weight_copy = pltpu.make_async_copy(weight_hbm, weight, weight_sem)
    pending = fetch(0)
    for copy in pending:
        copy.start()
    weight_copy.start()
    for index in range(count):
        current = pending
        if index + 1 < count:
            pending = fetch(index + 1)
            for copy in pending:
                copy.start()
        for copy in current:
            copy.wait()
        if index == 0:
            weight_copy.wait()
        block = rows[index % 2].reshape(2 * tiles * half, depth)
        qkv[...] = jnp.dot(block, weight[...], preferred_element_type=jnp.float32).astype(jnp.bfloat16)
        for tile in range(tiles):
            for head in range(heads):

                def piece(kind):
                    start = (head * 3 + kind) * HEAD_DIM
                    columns = slice(start, start + HEAD_DIM)
                    low = qkv[tile * half : (tile + 1) * half, columns]
                    high = qkv[(tiles + tile) * half : (tiles + tile + 1) * half, columns]
                    return jnp.concatenate([low, high], axis=0)

                scores = lax.dot_general(
                    piece(0), piece(1), (((1,), (1,)), ((), ())), preferred_element_type=jnp.float32
                ) * (1.0 / math.sqrt(HEAD_DIM))
                scores = scores - jnp.max(scores, axis=-1, keepdims=True)
                raised = jnp.exp(scores)
                inverse = 1.0 / jnp.sum(raised, axis=-1, keepdims=True)
                soft = (raised * inverse).astype(jnp.bfloat16)
                mixed = jnp.dot(soft, piece(2), preferred_element_type=jnp.float32)
                outs[index][tile, :, head * HEAD_DIM : (head + 1) * HEAD_DIM] = mixed.astype(jnp.bfloat16)


def attend(pairs, weight):
    count = len(pairs)
    tiles, half, depth = pairs[0][0].shape
    width = weight.shape[1]
    shape = (tiles, 2 * half, width // 3)
    return pl.pallas_call(
        functools.partial(attend_kernel, count),
        out_shape=[jax.ShapeDtypeStruct(shape, jnp.bfloat16)] * count,
        in_specs=[pl.BlockSpec(memory_space=pl.ANY)] * (2 * count + 1),
        out_specs=[pl.BlockSpec(memory_space=pltpu.VMEM)] * count,
        scratch_shapes=[
            pltpu.VMEM((2, 2, tiles, half, depth), jnp.bfloat16),
            pltpu.VMEM((depth, width), jnp.bfloat16),
            pltpu.VMEM((2 * tiles * half, width), jnp.bfloat16),
            pltpu.SemaphoreType.DMA((2, 2)),
            pltpu.SemaphoreType.DMA,
        ],
        compiler_params=pltpu.CompilerParams(vmem_limit_bytes=VMEM_BYTES),
        cost_estimate=SMALL_COST,
        name="attend",
    )(*[rows for pair in pairs for rows in pair], weight)


def out_kernel(start, line_ref, *refs):
    attended = refs[:LINE]
    weights = refs[LINE : 2 * LINE]
    part_ref = refs[2 * LINE]
    tiles, half, block = part_ref.shape
    total = None
    for rows_ref, weight_ref in zip(attended, weights):
        rows = rows_ref[...].reshape(tiles * half, rows_ref.shape[2])
        term = jnp.dot(rows, weight_ref[...], preferred_element_type=jnp.float32)
        total = term if total is None else total + term
    part_ref[...] = total.astype(jnp.bfloat16).reshape(tiles, half, block)


def out_project(line_arg, attended, out_weight, part):
    tiles, full, share = attended[0].shape
    half = full // 2
    depth = out_weight.shape[1]
    block = 640

    def weight_spec(k):
        return pl.BlockSpec((share, block), lambda n, line: ((line[0] + k) % LINE, n))

    return pl.pallas_call(
        functools.partial(out_kernel, part),
        grid_spec=pltpu.PrefetchScalarGridSpec(
            num_scalar_prefetch=1,
            grid=(depth // block,),
            in_specs=[pl.BlockSpec((tiles, half, share), lambda n, line: (0, part, 0))] * LINE
            + [weight_spec(k) for k in range(LINE)],
            out_specs=pl.BlockSpec((tiles, half, block), lambda n, line: (0, 0, n)),
        ),
        out_shape=jax.ShapeDtypeStruct((tiles, half, depth), jnp.bfloat16),
        compiler_params=pltpu.CompilerParams(vmem_limit_bytes=VMEM_BYTES),
        cost_estimate=SMALL_COST,
        name="out",
    )(line_arg, *attended, *([out_weight] * LINE))


def join_kernel(
    mixing_ref, tokens_ref, early_ref, mid_ref, own_ref, other_ref, scale_ref, z_ref, inverse_ref
):
    inputs = tokens_ref[0].astype(jnp.float32)
    attended_out = own_ref[0].astype(jnp.float32) + other_ref[0].astype(jnp.float32)
    joined = (
        mixing_ref[0] * early_ref[0].astype(jnp.float32)
        + mixing_ref[1] * mid_ref[0].astype(jnp.float32)
        + (mixing_ref[2] + mixing_ref[3]) * inputs
        + (mixing_ref[3] * scale_ref[...]) * attended_out
    )
    centre = jnp.mean(joined, axis=-1, keepdims=True)
    shifted = joined - centre
    inverse = lax.rsqrt(jnp.mean(shifted * shifted, axis=-1, keepdims=True) + 1e-05)
    z_ref[0] = (shifted * inverse).astype(jnp.bfloat16)
    inverse_ref[0] = jnp.broadcast_to(inverse, inverse_ref.shape[1:])


def join_rows(mixing, tokens, early, mid, own, other, scale):
    tiles, half, depth = tokens.shape
    block = 64
    spec = pl.BlockSpec((1, block, depth), lambda t, r: (t, r, 0))
    return pl.pallas_call(
        join_kernel,
        grid=(tiles, half // block),
        out_shape=[
            jax.ShapeDtypeStruct(tokens.shape, jnp.bfloat16),
            jax.ShapeDtypeStruct((tiles, half, 128), jnp.float32),
        ],
        in_specs=[pl.BlockSpec(memory_space=pltpu.SMEM)]
        + [spec] * 5
        + [pl.BlockSpec((1, depth), lambda t, r: (0, 0))],
        out_specs=[spec, pl.BlockSpec((1, block, 128), lambda t, r: (t, r, 0))],
        compiler_params=pltpu.CompilerParams(vmem_limit_bytes=VMEM_BYTES),
        cost_estimate=SMALL_COST,
        name="join",
    )(mixing, tokens, early, mid, own, other, scale)


def final_kernel(own_ref, other_ref, z_ref, inverse_ref, out_ref):
    grad = own_ref[0].astype(jnp.float32) + other_ref[0].astype(jnp.float32)
    normal = z_ref[0].astype(jnp.float32)
    mean = jnp.mean(grad, axis=-1, keepdims=True)
    along = jnp.mean(grad * normal, axis=-1, keepdims=True)
    out_ref[0] = ((grad - mean - normal * along) * inverse_ref[0, :, :1]).astype(jnp.bfloat16)


def final_rows(own, other, z_rows, inverse):
    tiles, half, depth = own.shape
    block = 64
    spec = pl.BlockSpec((1, block, depth), lambda t, r: (t, r, 0))
    return pl.pallas_call(
        final_kernel,
        grid=(tiles, half // block),
        out_shape=jax.ShapeDtypeStruct(own.shape, jnp.bfloat16),
        in_specs=[spec, spec, spec, pl.BlockSpec((1, block, 128), lambda t, r: (t, r, 0))],
        out_specs=spec,
        compiler_params=pltpu.CompilerParams(vmem_limit_bytes=VMEM_BYTES),
        cost_estimate=SMALL_COST,
        name="final",
    )(own, other, z_rows, inverse)


def activate(preact):
    raised = jnp.exp(-0.5 * preact * preact)
    step = 1.0 / (1.0 + 0.3275911 * inv_root_two * jnp.abs(preact))
    series = 1.061405429 * step - 1.453152027
    series = series * step + 1.421413741
    series = series * step - 0.284496736
    series = series * step + 0.254829592
    tail = 0.5 * series * step * raised
    return jnp.where(preact >= 0.0, 1.0 - tail, tail), raised * inv_root_tau


def project_kernel(core_ref, own_ref, other_ref, weight_ref, bias_ref, projected_ref, slope_ref):
    core = core_ref[0]
    tiles, half, depth = own_ref.shape
    block = weight_ref.shape[1]
    rows = jnp.concatenate(
        [own_ref[...].reshape(tiles * half, depth), other_ref[...].reshape(tiles * half, depth)], axis=0
    )
    preact = jnp.dot(rows, weight_ref[...], preferred_element_type=jnp.float32) + bias_ref[...]
    cumulative, density = activate(preact)
    projected = (preact * cumulative).astype(jnp.bfloat16).reshape(2, tiles, 1, half, block)
    projected_ref[:, pl.ds(core, 1)] = projected[0]
    projected_ref[:, pl.ds(1 - core, 1)] = projected[1]
    slope_ref[...] = cumulative + preact * density


def home_project(core, own, other, weight, bias):
    tiles, half, depth = own.shape
    width = weight.shape[1]
    block = 512
    whole = pl.BlockSpec((tiles, half, depth), lambda n, c: (0, 0, 0))
    projected, slope = pl.pallas_call(
        project_kernel,
        grid_spec=pltpu.PrefetchScalarGridSpec(
            num_scalar_prefetch=1,
            grid=(width // block,),
            in_specs=[
                whole,
                whole,
                pl.BlockSpec((depth, block), lambda n, c: (0, n)),
                pl.BlockSpec((1, block), lambda n, c: (0, n)),
            ],
            out_specs=[
                pl.BlockSpec((tiles, 2, half, block), lambda n, c: (0, 0, 0, n)),
                pl.BlockSpec((2 * tiles * half, block), lambda n, c: (0, n)),
            ],
        ),
        out_shape=[
            jax.ShapeDtypeStruct((tiles, 2, half, width), jnp.bfloat16),
            jax.ShapeDtypeStruct((2 * tiles * half, width), jnp.float32),
        ],
        compiler_params=pltpu.CompilerParams(vmem_limit_bytes=VMEM_BYTES),
        cost_estimate=SMALL_COST,
        name="project",
    )(core, own, other, weight, bias)
    return projected.reshape(tiles, 2 * half, width), slope


def grad_kernel(core_ref, slope_ref, back_own_ref, back_other_ref, weight_ref, own_ref, other_ref, total):
    step = pl.program_id(0)
    tiles, half, depth = own_ref.shape
    rows, block = slope_ref.shape
    back = jnp.concatenate(
        [ref[...].reshape(tiles * half, block) for ref in (back_own_ref, back_other_ref)], axis=0
    )
    slope_rows = (back.astype(jnp.float32) * slope_ref[...]).astype(jnp.bfloat16)
    term = lax.dot_general(
        slope_rows, weight_ref[...], (((1,), (1,)), ((), ())), preferred_element_type=jnp.float32
    )

    @pl.when(step == 0)
    def _():
        total[...] = term

    @pl.when(step > 0)
    def _():
        total[...] += term

    @pl.when(step == pl.num_programs(0) - 1)
    def _():
        own_ref[...] = total[: tiles * half].astype(jnp.bfloat16).reshape(tiles, half, depth)
        other_ref[...] = total[tiles * half :].astype(jnp.bfloat16).reshape(tiles, half, depth)


def home_grad(core, slope, back, weight):
    tiles, full, width = back.shape
    half = full // 2
    depth = weight.shape[0]
    block = 512
    back = back.reshape(tiles, 2, half, width)
    whole = pl.BlockSpec((tiles, half, depth), lambda n, c: (0, 0, 0))
    shape = jax.ShapeDtypeStruct((tiles, half, depth), jnp.bfloat16)
    return pl.pallas_call(
        grad_kernel,
        grid_spec=pltpu.PrefetchScalarGridSpec(
            num_scalar_prefetch=1,
            grid=(width // block,),
            in_specs=[
                pl.BlockSpec((tiles * full, block), lambda n, c: (0, n)),
                pl.BlockSpec((tiles, 1, half, block), lambda n, c: (0, c[0], 0, n)),
                pl.BlockSpec((tiles, 1, half, block), lambda n, c: (0, 1 - c[0], 0, n)),
                pl.BlockSpec((depth, block), lambda n, c: (0, n)),
            ],
            out_specs=[whole, whole],
            scratch_shapes=[pltpu.VMEM((tiles * full, depth), jnp.float32)],
        ),
        out_shape=[shape, shape],
        compiler_params=pltpu.CompilerParams(vmem_limit_bytes=VMEM_BYTES),
        cost_estimate=SMALL_COST,
        name="grad",
    )(core, slope, back, back, weight)


def owner_kernel(count, core_ref, *refs):
    sources = refs[: 2 * count]
    weight_ref, bias_ref, projected_ref = refs[2 * count :]
    core = core_ref[0]
    _, half, depth = sources[0].shape
    block = weight_ref.shape[1]
    rows = jnp.concatenate([source[0] for source in sources], axis=0)
    preact = jnp.dot(rows, weight_ref[...], preferred_element_type=jnp.float32) + bias_ref[...]
    projected = (preact * activate(preact)[0]).astype(jnp.bfloat16)
    projected = projected.reshape(count, 2, half, block)
    for index in range(count):
        projected_ref[index, pl.ds(core, 1)] = projected[index, :1]
        projected_ref[index, pl.ds(1 - core, 1)] = projected[index, 1:]


def owner_project(core, pairs, weight, bias):
    count = len(pairs)
    _, half, depth = pairs[0][0].shape
    width = weight.shape[1]
    block = 512
    projected = pl.pallas_call(
        functools.partial(owner_kernel, count),
        grid_spec=pltpu.PrefetchScalarGridSpec(
            num_scalar_prefetch=1,
            grid=(width // block,),
            in_specs=[pl.BlockSpec((1, half, depth), lambda n, c: (0, 0, 0))] * (2 * count)
            + [
                pl.BlockSpec((depth, block), lambda n, c: (0, n)),
                pl.BlockSpec((1, block), lambda n, c: (0, n)),
            ],
            out_specs=pl.BlockSpec((count, 2, half, block), lambda n, c: (0, 0, 0, n)),
        ),
        out_shape=jax.ShapeDtypeStruct((count, 2, half, width), jnp.bfloat16),
        compiler_params=pltpu.CompilerParams(vmem_limit_bytes=VMEM_BYTES),
        cost_estimate=SMALL_COST,
        name="owner",
    )(core, *[rows for pair in pairs for rows in pair], weight, bias)
    return projected.reshape(count, 2 * half, width)


def on_device(
    tokens, tap_early, tap_mid, tile_counts, qkv_weight, out_weight, layer_scale, layer_logits,
    proj_weight, proj_bias, grad_out,
):
    tile_group, token_share, depth = tokens.shape
    img_count = lax.axis_size(IMG)
    place = lax.axis_index(IMG)
    line_place = lax.axis_index("z")
    core = lax.axis_index("head")
    core_arg = core.astype(jnp.int32).reshape(1)
    tile_total = tile_group * img_count
    own_tiles = grad_out.shape[0]
    owner_of, first_tile = tile_owners(tile_counts, tile_total, tile_group)
    my_first = first_tile[place]

    depth_share, width = qkv_weight.shape
    share = width // LINE
    received = []
    for distance in range(LINE):
        target = (line_place + distance) % LINE
        columns = lax.dynamic_slice_in_dim(qkv_weight, target * share, share, axis=1)
        received.append(along_z(columns, distance) if distance else columns)
    normed = norm_rows(tokens)
    normed, received = lax.optimization_barrier((normed, received))
    ladder = jnp.stack([received[(LINE - 1 - j) % LINE] for j in range(2 * LINE - 1)], axis=0)
    sent = lax.dynamic_slice_in_dim(ladder, LINE - 1 - line_place, LINE, axis=0)
    weight = lax.all_gather(sent.reshape(LINE * depth_share, share), ("y", "x"), axis=0, tiled=True)

    def packet(distance, within, count, first):
        tile = (place + distance) * tile_group + within
        slot = jnp.clip(tile - first, 0, own_tiles - count)
        return lax.dynamic_slice_in_dim(grad_out, slot, count, axis=0)

    near_line = [ring_x(packet(1, 0, 1, my_first), 1)]
    from_low = along_z(normed, 1)
    from_high = along_z(normed, -1)
    from_low, from_high, near_line[0], second_first = lax.optimization_barrier(
        (from_low, from_high, near_line[0], my_first)
    )
    near_line.append(ring_x(packet(1, 1, 1, second_first), 1))
    far_first = along_z(from_low[:1], 1)
    far_second = along_z(from_high[1:], -1)
    near_next = [next_line(near_line[0], 1)]
    far_first, far_second, weight, near_line[1], near_next[0], far_slot = lax.optimization_barrier(
        (far_first, far_second, weight, near_line[1], near_next[0], my_first)
    )
    far_line = ring_x(packet(2, 0, tile_group, far_slot), 2)
    near_next.append(next_line(near_line[1], 1))

    from_far = jnp.concatenate([far_first, far_second], axis=0)
    att_far, att_low, att_high = attend(
        [(rows, swap(rows)) for rows in (from_far, from_low, from_high)], weight
    )
    (att_own,) = attend([(normed, swap(normed))], weight)
    att_far, att_low, att_high = along_z(att_far, 2), along_z(att_low, -1), along_z(att_high, 1)
    att_own, near_next[1] = lax.optimization_barrier((att_own, near_next[1]))
    attended = [att_own, att_low, att_far, att_high]
    line_arg = line_place.astype(jnp.int32).reshape(1)
    part_other = swap(out_project(line_arg, attended, out_weight, 1))
    part_own = out_project(line_arg, attended, out_weight, 0)
    part_own, part_other, far_line = lax.optimization_barrier((part_own, part_other, far_line))
    far_next = next_line(far_line, 2)
    raised_logits = jnp.exp(layer_logits)
    mixing = raised_logits / jnp.sum(raised_logits)
    z_rows, inverse_std = join_rows(
        mixing, tokens, tap_early, tap_mid, part_own, part_other, layer_scale.reshape(1, -1)
    )

    halfway, far_on = two_back(z_rows[1:])
    far_first = along_img(z_rows[:1], -2)
    near_first = along_img(z_rows[:1], -1)
    bias = proj_bias.reshape(1, -1)
    projected, slope = home_project(core_arg, z_rows, swap(z_rows), proj_weight, bias)
    near_first, far_first, halfway, second, slope = lax.optimization_barrier(
        (near_first, far_first, halfway, z_rows[1:], slope)
    )
    near_second = along_img(second, -1)
    far_second = far_on(halfway)

    def guests(first, second):
        return owner_project(
            core_arg, [(first, swap(first)), (second, swap(second))], proj_weight, bias
        )

    early = guests(near_first, far_first)
    far_next, slope, _ = lax.optimization_barrier((far_next, slope, early))

    column = place % LINE
    back = []
    for within in range(tile_group):
        tile = place * tile_group + within
        owner = owner_of[tile]
        slot = jnp.clip(tile - my_first, 0, own_tiles - 1)
        here = lax.dynamic_index_in_dim(grad_out, slot, axis=0, keepdims=False)
        near = jnp.where(column < 1, near_next[within][0], near_line[within][0])
        far = jnp.where(column < 2, far_next[within], far_line[within])
        back.append(jnp.where(owner == place, here, jnp.where(owner == place - 1, near, far)))
    back_rows = jnp.stack(back, axis=0)
    grad_own, grad_other = home_grad(core_arg, slope, back_rows, proj_weight)
    near_second, far_second, _ = lax.optimization_barrier((near_second, far_second, grad_other))
    late = guests(near_second, far_second)
    grad_joined = final_rows(grad_own, swap(grad_other), z_rows, inverse_std)

    offset = my_first - place * tile_group
    held = first_tile[place + 1] - my_first
    at_hand = [projected[0], projected[1], early[0], late[0], early[1], late[1]]
    slots = []
    for slot in range(own_tiles):
        later = at_hand[min(slot + 1, len(at_hand) - 1)]
        picked = jnp.where(offset == 0, at_hand[slot], later)
        slots.append(jnp.where(slot < held, picked, jnp.zeros((), jnp.bfloat16)))
    owner_rows = jnp.stack(slots, axis=0)
    return (owner_rows, grad_joined)


def solution(mesh):
    cores = mesh.devices.shape[-1]
    inner = Mesh(mesh.devices.reshape(LINE, LINE, LINE, cores), IMG + ("head",))
    return jax.shard_map(
        on_device,
        mesh=inner,
        in_specs=(
            P(IMG, "head", None),
            P(IMG, "head", None),
            P(IMG, "head", None),
            P(),
            P(IMG, "head"),
            P("head", None),
            P(),
            P(),
            P(None, "head"),
            P("head"),
            P(IMG, None, "head"),
        ),
        out_specs=(P(IMG, None, "head"), P(IMG, "head", None)),
        check_vma=False,
    )
```

```python
import functools
import math

import jax
import jax.numpy as jnp
from jax import lax
from jax.experimental import pallas as pl
from jax.experimental.pallas import tpu as pltpu
from jax.sharding import Mesh, PartitionSpec as P

HEAD_DIM = 128
LINE = 4
IMG = ("z", "y", "x")
VMEM_BYTES = 56 * 1024 * 1024
SMALL_COST = pl.CostEstimate(flops=1, bytes_accessed=1, transcendentals=0)

inv_root_two = 0.7071067811865476
inv_root_tau = 0.3989422804014327


def swap(array):
    return lax.ppermute(array, "head", [(0, 1), (1, 0)])


def along_z(array, by):
    return lax.ppermute(array, "z", [(i, (i + by) % LINE) for i in range(LINE)])


def along_img(array, by):
    peers = lax.axis_size(IMG)
    pairs = [(i, i + by) for i in range(peers) if 0 <= i + by < peers]
    return lax.ppermute(array, IMG, pairs)


def around(place, side):
    return place - place % LINE + (place % LINE + side) % LINE


def two_on(array, by):
    peers = lax.axis_size(IMG)
    side = -by // 2
    turning = 2 if by > 0 else 1

    def middle(i):
        return i + side + LINE * (by // 2) if i % LINE == turning else around(i, side)

    ends = [(i, i + by) for i in range(peers) if 0 <= i + by < peers]
    halfway = lax.ppermute(array, IMG, [(i, middle(i)) for i, _ in ends])
    return halfway, lambda held: lax.ppermute(held, IMG, [(middle(i), j) for i, j in ends])


def tile_owners(tile_counts, tile_total, tile_group):
    starts = jnp.cumsum(tile_counts) - tile_counts
    tile_index = jnp.arange(tile_total, dtype=jnp.int32)
    start_of = jnp.max(
        jnp.where(starts[None, :] <= tile_index[:, None], starts[None, :], -1), axis=1
    )
    owner_of = start_of // tile_group
    owners_total = tile_total // tile_group
    edge_tiles = jnp.arange(owners_total + 1, dtype=jnp.int32) * tile_group
    first_tile = jnp.min(
        jnp.where(starts[None, :] >= edge_tiles[:, None], starts[None, :], tile_total), axis=1
    )
    return (owner_of, first_tile)


def norm_kernel(tokens_ref, out_ref, ordered):
    rows = tokens_ref[0].astype(jnp.float32)
    normed = rows * lax.rsqrt(jnp.mean(rows * rows, axis=-1, keepdims=True) + 1e-06)
    groups = LINE * LINE
    share = rows.shape[1] // (LINE * groups)
    for line in range(LINE):
        for group in range(groups):
            source = (line * groups + group) * share
            target = (group * LINE + line) * share
            ordered[:, target : target + share] = normed[:, source : source + share]
    out_ref[0] = ordered[...].astype(jnp.bfloat16)


def norm_rows(tokens):
    tiles, half, depth = tokens.shape
    block = 64
    spec = pl.BlockSpec((1, block, depth), lambda t, r: (t, r, 0))
    return pl.pallas_call(
        norm_kernel,
        grid=(tiles, half // block),
        out_shape=jax.ShapeDtypeStruct(tokens.shape, jnp.bfloat16),
        in_specs=[spec],
        out_specs=spec,
        scratch_shapes=[pltpu.VMEM((block, depth), jnp.float32)],
        compiler_params=pltpu.CompilerParams(vmem_limit_bytes=VMEM_BYTES),
        cost_estimate=SMALL_COST,
        name="norm",
    )(tokens)


def attend_kernel(layout, *refs):
    count = len(layout)
    pieces = sum(2 * len(tiles) for tiles in layout)
    sources, weight_hbm = list(refs[:pieces]), refs[pieces]
    outs = refs[pieces + 1 : pieces + 1 + count]
    rows, weight, qkv, row_sems, weight_sem = refs[pieces + 1 + count :]
    _, _, tiles, half, depth = rows.shape
    heads = weight.shape[1] // (3 * HEAD_DIM)

    def fetch(index):
        slot = index % 2
        copies = []
        for part in range(2):
            start = 0
            for place, length in enumerate(layout[index]):
                target = rows.at[slot, part, pl.ds(start, length)]
                copies.append(
                    pltpu.make_async_copy(sources.pop(0), target, row_sems.at[slot, part, place])
                )
                start += length
        return copies

    weight_copy = pltpu.make_async_copy(weight_hbm, weight, weight_sem)
    pending = fetch(0)
    for copy in pending:
        copy.start()
    weight_copy.start()
    for index in range(count):
        current = pending
        if index + 1 < count:
            pending = fetch(index + 1)
            for copy in pending:
                copy.start()
        for copy in current:
            copy.wait()
        if index == 0:
            weight_copy.wait()
        block = rows[index % 2].reshape(2 * tiles * half, depth)
        qkv[...] = jnp.dot(block, weight[...], preferred_element_type=jnp.float32).astype(jnp.bfloat16)
        for tile in range(tiles):
            for head in range(heads):

                def piece(kind):
                    start = (head * 3 + kind) * HEAD_DIM
                    columns = slice(start, start + HEAD_DIM)
                    low = qkv[tile * half : (tile + 1) * half, columns]
                    high = qkv[(tiles + tile) * half : (tiles + tile + 1) * half, columns]
                    return jnp.concatenate([low, high], axis=0)

                scores = lax.dot_general(
                    piece(0), piece(1), (((1,), (1,)), ((), ())), preferred_element_type=jnp.float32
                ) * (1.0 / math.sqrt(HEAD_DIM))
                scores = scores - jnp.max(scores, axis=-1, keepdims=True)
                raised = jnp.exp(scores)
                inverse = 1.0 / jnp.sum(raised, axis=-1, keepdims=True)
                soft = (raised * inverse).astype(jnp.bfloat16)
                mixed = jnp.dot(soft, piece(2), preferred_element_type=jnp.float32)
                outs[index][tile, :, head * HEAD_DIM : (head + 1) * HEAD_DIM] = mixed.astype(jnp.bfloat16)


def attend(sources, weight):
    layout = tuple(tuple(array.shape[0] for array in own) for own, _ in sources)
    tiles = sum(layout[0])
    _, half, depth = sources[0][0][0].shape
    width = weight.shape[1]
    shape = (tiles, 2 * half, width // 3)
    arrays = [array for own, other in sources for array in (*own, *other)]
    return pl.pallas_call(
        functools.partial(attend_kernel, layout),
        out_shape=[jax.ShapeDtypeStruct(shape, jnp.bfloat16)] * len(layout),
        in_specs=[pl.BlockSpec(memory_space=pl.ANY)] * (len(arrays) + 1),
        out_specs=[pl.BlockSpec(memory_space=pltpu.VMEM)] * len(layout),
        scratch_shapes=[
            pltpu.VMEM((2, 2, tiles, half, depth), jnp.bfloat16),
            pltpu.VMEM((depth, width), jnp.bfloat16),
            pltpu.VMEM((2 * tiles * half, width), jnp.bfloat16),
            pltpu.SemaphoreType.DMA((2, 2, tiles)),
            pltpu.SemaphoreType.DMA,
        ],
        compiler_params=pltpu.CompilerParams(vmem_limit_bytes=VMEM_BYTES),
        cost_estimate=SMALL_COST,
        name="attend",
    )(*arrays, weight)


def out_kernel(line_ref, *refs):
    attended, weight_ref, part_ref, rows = refs[:LINE], refs[LINE], refs[LINE + 1], refs[LINE + 2]
    tiles, half, block = part_ref.shape
    share = attended[0].shape[2]

    @pl.when(pl.program_id(0) == 0)
    def _():
        for distance, source in enumerate(attended):
            start = pl.multiple_of(lax.rem(line_ref[0] + distance, LINE) * share, share)
            rows[:, pl.ds(start, share)] = source[...].reshape(tiles * half, share)

    total = jnp.dot(rows[...], weight_ref[...], preferred_element_type=jnp.float32)
    part_ref[...] = total.astype(jnp.bfloat16).reshape(tiles, half, block)


def out_project(line_arg, attended, out_weight, part):
    tiles, full, share = attended[0].shape
    half = full // 2
    depth = out_weight.shape[1]
    block = 640
    return pl.pallas_call(
        out_kernel,
        grid_spec=pltpu.PrefetchScalarGridSpec(
            num_scalar_prefetch=1,
            grid=(depth // block,),
            in_specs=[pl.BlockSpec((tiles, half, share), lambda n, line: (0, part, 0))] * LINE
            + [pl.BlockSpec((LINE * share, block), lambda n, line: (0, n))],
            out_specs=pl.BlockSpec((tiles, half, block), lambda n, line: (0, 0, n)),
            scratch_shapes=[pltpu.VMEM((tiles * half, LINE * share), jnp.bfloat16)],
        ),
        out_shape=jax.ShapeDtypeStruct((tiles, half, depth), jnp.bfloat16),
        compiler_params=pltpu.CompilerParams(vmem_limit_bytes=VMEM_BYTES),
        cost_estimate=SMALL_COST,
        name="out",
    )(line_arg, *attended, out_weight)


def join_kernel(
    mixing_ref, tokens_ref, early_ref, mid_ref, own_ref, other_ref, scale_ref, z_ref, inverse_ref
):
    inputs = tokens_ref[0].astype(jnp.float32)
    attended_out = own_ref[0].astype(jnp.float32) + other_ref[0].astype(jnp.float32)
    joined = (
        mixing_ref[0] * early_ref[0].astype(jnp.float32)
        + mixing_ref[1] * mid_ref[0].astype(jnp.float32)
        + (mixing_ref[2] + mixing_ref[3]) * inputs
        + (mixing_ref[3] * scale_ref[...]) * attended_out
    )
    centre = jnp.mean(joined, axis=-1, keepdims=True)
    shifted = joined - centre
    inverse = lax.rsqrt(jnp.mean(shifted * shifted, axis=-1, keepdims=True) + 1e-05)
    z_ref[0] = (shifted * inverse).astype(jnp.bfloat16)
    inverse_ref[0] = jnp.broadcast_to(inverse, inverse_ref.shape[1:])


def join_rows(tile, mixing, tokens, early, mid, own, other, scale):
    _, half, depth = tokens.shape
    block = 64
    spec = pl.BlockSpec((1, block, depth), lambda r: (tile, r, 0))
    return pl.pallas_call(
        join_kernel,
        grid=(half // block,),
        out_shape=[
            jax.ShapeDtypeStruct((1, half, depth), jnp.bfloat16),
            jax.ShapeDtypeStruct((1, half, 128), jnp.float32),
        ],
        in_specs=[pl.BlockSpec(memory_space=pltpu.SMEM)]
        + [spec] * 5
        + [pl.BlockSpec((1, depth), lambda r: (0, 0))],
        out_specs=[
            pl.BlockSpec((1, block, depth), lambda r: (0, r, 0)),
            pl.BlockSpec((1, block, 128), lambda r: (0, r, 0)),
        ],
        compiler_params=pltpu.CompilerParams(vmem_limit_bytes=VMEM_BYTES),
        cost_estimate=SMALL_COST,
        name="join",
    )(mixing, tokens, early, mid, own, other, scale)


def final_kernel(own_ref, other_ref, z_ref, later_z_ref, inverse_ref, later_inverse_ref, out_ref):
    first = pl.program_id(0) == 0
    grad = own_ref[0].astype(jnp.float32) + other_ref[0].astype(jnp.float32)
    normal = jnp.where(first, z_ref[0], later_z_ref[0]).astype(jnp.float32)
    inverse = jnp.where(first, inverse_ref[0, :, :1], later_inverse_ref[0, :, :1])
    mean = jnp.mean(grad, axis=-1, keepdims=True)
    along = jnp.mean(grad * normal, axis=-1, keepdims=True)
    out_ref[0] = ((grad - mean - normal * along) * inverse).astype(jnp.bfloat16)


def final_rows(own, other, z_tiles, inverse_tiles):
    tiles, half, depth = own.shape
    block = 64
    spec = pl.BlockSpec((1, block, depth), lambda t, r: (t, r, 0))
    z_spec = pl.BlockSpec((1, block, depth), lambda t, r: (0, r, 0))
    inverse_spec = pl.BlockSpec((1, block, 128), lambda t, r: (0, r, 0))
    return pl.pallas_call(
        final_kernel,
        grid=(tiles, half // block),
        out_shape=jax.ShapeDtypeStruct(own.shape, jnp.bfloat16),
        in_specs=[spec, spec, z_spec, z_spec, inverse_spec, inverse_spec],
        out_specs=spec,
        compiler_params=pltpu.CompilerParams(vmem_limit_bytes=VMEM_BYTES),
        cost_estimate=SMALL_COST,
        name="final",
    )(own, other, *z_tiles, *inverse_tiles)


def activate(preact):
    raised = jnp.exp(-0.5 * preact * preact)
    step = 1.0 / (1.0 + 0.3275911 * inv_root_two * jnp.abs(preact))
    series = 1.061405429 * step - 1.453152027
    series = series * step + 1.421413741
    series = series * step - 0.284496736
    series = series * step + 0.254829592
    tail = 0.5 * series * step * raised
    return jnp.where(preact >= 0.0, 1.0 - tail, tail), raised * inv_root_tau


def project_kernel(core_ref, *refs):
    sources = refs[:-4]
    weight_ref, bias_ref, projected_ref, slope_ref = refs[-4:]
    core = core_ref[0]
    tiles, _, half, block = projected_ref.shape
    rows = jnp.concatenate([source[0] for source in sources], axis=0)
    preact = jnp.dot(rows, weight_ref[...], preferred_element_type=jnp.float32) + bias_ref[...]
    cumulative, density = activate(preact)
    projected = (preact * cumulative).astype(jnp.bfloat16).reshape(2, tiles, 1, half, block)
    projected_ref[:, pl.ds(core, 1)] = projected[0]
    projected_ref[:, pl.ds(1 - core, 1)] = projected[1]
    slope_ref[...] = cumulative + preact * density


def home_project(core, own, other, weight, bias):
    tiles = len(own)
    _, half, depth = own[0].shape
    width = weight.shape[1]
    block = 512
    projected, slope = pl.pallas_call(
        project_kernel,
        grid_spec=pltpu.PrefetchScalarGridSpec(
            num_scalar_prefetch=1,
            grid=(width // block,),
            in_specs=[pl.BlockSpec((1, half, depth), lambda n, c: (0, 0, 0))] * (2 * tiles)
            + [
                pl.BlockSpec((depth, block), lambda n, c: (0, n)),
                pl.BlockSpec((1, block), lambda n, c: (0, n)),
            ],
            out_specs=[
                pl.BlockSpec((tiles, 2, half, block), lambda n, c: (0, 0, 0, n)),
                pl.BlockSpec((2 * tiles * half, block), lambda n, c: (0, n)),
            ],
        ),
        out_shape=[
            jax.ShapeDtypeStruct((tiles, 2, half, width), jnp.bfloat16),
            jax.ShapeDtypeStruct((2 * tiles * half, width), jnp.float32),
        ],
        compiler_params=pltpu.CompilerParams(vmem_limit_bytes=VMEM_BYTES),
        cost_estimate=SMALL_COST,
        name="project",
    )(core, *own, *other, weight, bias)
    return projected.reshape(tiles, 2 * half, width), slope


def grad_kernel(core_ref, slope_ref, back_own_ref, back_other_ref, weight_ref, own_ref, other_ref, total):
    step = pl.program_id(0)
    tiles, half, depth = own_ref.shape
    rows, block = slope_ref.shape
    back = jnp.concatenate(
        [ref[...].reshape(tiles * half, block) for ref in (back_own_ref, back_other_ref)], axis=0
    )
    slope_rows = (back.astype(jnp.float32) * slope_ref[...]).astype(jnp.bfloat16)
    term = lax.dot_general(
        slope_rows, weight_ref[...], (((1,), (1,)), ((), ())), preferred_element_type=jnp.float32
    )

    @pl.when(step == 0)
    def _():
        total[...] = term

    @pl.when(step > 0)
    def _():
        total[...] += term

    @pl.when(step == pl.num_programs(0) - 1)
    def _():
        own_ref[...] = total[: tiles * half].astype(jnp.bfloat16).reshape(tiles, half, depth)
        other_ref[...] = total[tiles * half :].astype(jnp.bfloat16).reshape(tiles, half, depth)


def home_grad(core, slope, back, weight):
    tiles, full, width = back.shape
    half = full // 2
    depth = weight.shape[0]
    block = 512
    back = back.reshape(tiles, 2, half, width)
    whole = pl.BlockSpec((tiles, half, depth), lambda n, c: (0, 0, 0))
    shape = jax.ShapeDtypeStruct((tiles, half, depth), jnp.bfloat16)
    return pl.pallas_call(
        grad_kernel,
        grid_spec=pltpu.PrefetchScalarGridSpec(
            num_scalar_prefetch=1,
            grid=(width // block,),
            in_specs=[
                pl.BlockSpec((tiles * full, block), lambda n, c: (0, n)),
                pl.BlockSpec((tiles, 1, half, block), lambda n, c: (0, c[0], 0, n)),
                pl.BlockSpec((tiles, 1, half, block), lambda n, c: (0, 1 - c[0], 0, n)),
                pl.BlockSpec((depth, block), lambda n, c: (0, n)),
            ],
            out_specs=[whole, whole],
            scratch_shapes=[pltpu.VMEM((tiles * full, depth), jnp.float32)],
        ),
        out_shape=[shape, shape],
        compiler_params=pltpu.CompilerParams(vmem_limit_bytes=VMEM_BYTES),
        cost_estimate=SMALL_COST,
        name="grad",
    )(core, slope, back, back, weight)


def owner_kernel(count, core_ref, *refs):
    sources = refs[: 2 * count]
    weight_ref, bias_ref, projected_ref = refs[2 * count :]
    core = core_ref[0]
    _, half, depth = sources[0].shape
    block = weight_ref.shape[1]
    rows = jnp.concatenate([source[0] for source in sources], axis=0)
    preact = jnp.dot(rows, weight_ref[...], preferred_element_type=jnp.float32) + bias_ref[...]
    projected = (preact * activate(preact)[0]).astype(jnp.bfloat16)
    projected = projected.reshape(count, 2, half, block)
    for index in range(count):
        projected_ref[index, pl.ds(core, 1)] = projected[index, :1]
        projected_ref[index, pl.ds(1 - core, 1)] = projected[index, 1:]


def owner_project(core, pairs, weight, bias):
    count = len(pairs)
    _, half, depth = pairs[0][0].shape
    width = weight.shape[1]
    block = 512
    projected = pl.pallas_call(
        functools.partial(owner_kernel, count),
        grid_spec=pltpu.PrefetchScalarGridSpec(
            num_scalar_prefetch=1,
            grid=(width // block,),
            in_specs=[pl.BlockSpec((1, half, depth), lambda n, c: (0, 0, 0))] * (2 * count)
            + [
                pl.BlockSpec((depth, block), lambda n, c: (0, n)),
                pl.BlockSpec((1, block), lambda n, c: (0, n)),
            ],
            out_specs=pl.BlockSpec((count, 2, half, block), lambda n, c: (0, 0, 0, n)),
        ),
        out_shape=jax.ShapeDtypeStruct((count, 2, half, width), jnp.bfloat16),
        compiler_params=pltpu.CompilerParams(vmem_limit_bytes=VMEM_BYTES),
        cost_estimate=SMALL_COST,
        name="owner",
    )(core, *[rows for pair in pairs for rows in pair], weight, bias)
    return projected.reshape(count, 2 * half, width)


def on_device(
    tokens, tap_early, tap_mid, tile_counts, qkv_weight, out_weight, layer_scale, layer_logits,
    proj_weight, proj_bias, grad_out,
):
    tile_group, token_share, depth = tokens.shape
    img_count = lax.axis_size(IMG)
    place = lax.axis_index(IMG)
    line_place = lax.axis_index("z")
    core = lax.axis_index("head")
    core_arg = core.astype(jnp.int32).reshape(1)
    tile_total = tile_group * img_count
    own_tiles = grad_out.shape[0]
    owner_of, first_tile = tile_owners(tile_counts, tile_total, tile_group)
    my_first = first_tile[place]

    depth_share, width = qkv_weight.shape
    share = width // LINE
    received = []
    for distance in range(LINE):
        target = (line_place + distance) % LINE
        columns = lax.dynamic_slice_in_dim(qkv_weight, target * share, share, axis=1)
        received.append(along_z(columns, distance) if distance else columns)
    normed = norm_rows(tokens)
    normed, received = lax.optimization_barrier((normed, received))
    ladder = jnp.stack([received[(LINE - 1 - j) % LINE] for j in range(2 * LINE - 1)], axis=0)
    sent = lax.dynamic_slice_in_dim(ladder, LINE - 1 - line_place, LINE, axis=0)
    weight = lax.all_gather(sent.reshape(LINE * depth_share, share), ("y", "x"), axis=0, tiled=True)

    def packet(distance, within, count, first):
        tile = (place + distance) * tile_group + within
        slot = jnp.clip(tile - first, 0, own_tiles - count)
        return lax.dynamic_slice_in_dim(grad_out, slot, count, axis=0)

    from_low = along_z(normed, 1)
    from_high = along_z(normed, -1)

    def packet(distance, within, count):
        tile = (place + distance) * tile_group + within
        slot = jnp.clip(tile - my_first, 0, own_tiles - count)
        return lax.dynamic_slice_in_dim(grad_out, slot, count, axis=0)

    packets = [packet(distance, within, 1) for distance in (1, 2) for within in range(tile_group)]
    from_low, from_high, packets = lax.optimization_barrier((from_low, from_high, packets))
    far_first = along_z(from_low[:1], 1)
    far_second = along_z(from_high[1:], -1)
    weight, packets = lax.optimization_barrier((weight, packets))
    halfway, far_on = two_on(packets[3], 2)
    far_back = [along_img(packets[2], 2), None]
    near_back = [along_img(packets[0], 1), along_img(packets[1], 1)]

    far_others = [swap(far_first), swap(far_second)]
    att_low, att_high = attend(
        [([rows], [swap(rows)]) for rows in (from_low, from_high)], weight
    )
    far_first, far_second, att_low = lax.optimization_barrier((far_first, far_second, att_low))
    (att_far,) = attend([([far_first, far_second], far_others)], weight)
    (att_own,) = attend([([normed], [swap(normed)])], weight)
    att_far, att_low, att_high = along_z(att_far, 2), along_z(att_low, -1), along_z(att_high, 1)
    att_own, halfway, near_back[0] = lax.optimization_barrier((att_own, halfway, near_back[0]))
    far_back[1] = far_on(halfway)
    attended = [att_own, att_low, att_far, att_high]
    line_arg = line_place.astype(jnp.int32).reshape(1)
    part_other = swap(out_project(line_arg, attended, out_weight, 1))
    part_own = out_project(line_arg, attended, out_weight, 0)
    raised_logits = jnp.exp(layer_logits)
    mixing = raised_logits / jnp.sum(raised_logits)
    scale = layer_scale.reshape(1, -1)
    joined = [
        join_rows(tile, mixing, tokens, tap_early, tap_mid, part_own, part_other, scale)
        for tile in range(tile_group)
    ]
    z_tiles = [z_rows for z_rows, _ in joined]
    inverse_tiles = [inverse for _, inverse in joined]

    near_first = along_img(z_tiles[0], -1)
    far_first = along_img(z_tiles[0], -2)
    halfway, far_on = two_on(z_tiles[1], -2)
    bias = proj_bias.reshape(1, -1)
    projected, slope = home_project(
        core_arg, z_tiles, [swap(z_rows) for z_rows in z_tiles], proj_weight, bias
    )
    slope, near_back[1], far_back[1] = lax.optimization_barrier((slope, near_back[1], far_back[1]))

    back = []
    for within in range(tile_group):
        tile = place * tile_group + within
        owner = owner_of[tile]
        slot = jnp.clip(tile - my_first, 0, own_tiles - 1)
        here = lax.dynamic_index_in_dim(grad_out, slot, axis=0, keepdims=False)
        near, far = near_back[within][0], far_back[within][0]
        back.append(jnp.where(owner == place, here, jnp.where(owner == place - 1, near, far)))
    back_rows = jnp.stack(back, axis=0)
    grad_own, grad_other = home_grad(core_arg, slope, back_rows, proj_weight)

    near_first, far_first, halfway, second, grad_other = lax.optimization_barrier(
        (near_first, far_first, halfway, z_tiles[1], grad_other)
    )
    near_second = along_img(second, -1)
    far_second = far_on(halfway)

    def guests(first, second):
        return owner_project(
            core_arg, [(first, swap(first)), (second, swap(second))], proj_weight, bias
        )

    early = guests(near_first, far_first)
    grad_joined = final_rows(grad_own, swap(grad_other), z_tiles, inverse_tiles)
    near_second, far_second, early, grad_joined = lax.optimization_barrier(
        (near_second, far_second, early, grad_joined)
    )
    late = guests(near_second, far_second)

    offset = my_first - place * tile_group
    held = first_tile[place + 1] - my_first
    at_hand = [projected[0], projected[1], early[0], late[0], early[1], late[1]]
    slots = []
    for slot in range(own_tiles):
        later = at_hand[min(slot + 1, len(at_hand) - 1)]
        picked = jnp.where(offset == 0, at_hand[slot], later)
        slots.append(jnp.where(slot < held, picked, jnp.zeros((), jnp.bfloat16)))
    owner_rows = jnp.stack(slots, axis=0)
    return (owner_rows, grad_joined)


def solution(mesh):
    cores = mesh.devices.shape[-1]
    inner = Mesh(mesh.devices.reshape(LINE, LINE, LINE, cores), IMG + ("head",))
    return jax.shard_map(
        on_device,
        mesh=inner,
        in_specs=(
            P(IMG, "head", None),
            P(IMG, "head", None),
            P(IMG, "head", None),
            P(),
            P(IMG, "head"),
            P("head", None),
            P(),
            P(),
            P(None, "head"),
            P("head"),
            P(IMG, None, "head"),
        ),
        out_specs=(P(IMG, None, "head"), P(IMG, "head", None)),
        check_vma=False,
    )
```

```python
import functools
import math

import jax
import jax.numpy as jnp
from jax import lax
from jax.experimental import pallas as pl
from jax.experimental.pallas import tpu as pltpu
from jax.sharding import Mesh, PartitionSpec as P

HEAD_DIM = 128
LINE = 4
IMG = ("z", "y", "x")
VMEM_BYTES = 56 * 1024 * 1024
SMALL_COST = pl.CostEstimate(flops=1, bytes_accessed=1, transcendentals=0)

inv_root_two = 0.7071067811865476
inv_root_tau = 0.3989422804014327


def swap(array):
    return lax.ppermute(array, "head", [(0, 1), (1, 0)])


def along_z(array, by):
    return lax.ppermute(array, "z", [(i, (i + by) % LINE) for i in range(LINE)])


def along_img(array, by):
    peers = lax.axis_size(IMG)
    pairs = [(i, i + by) for i in range(peers) if 0 <= i + by < peers]
    return lax.ppermute(array, IMG, pairs)


def tile_owners(tile_counts, tile_total, tile_group):
    starts = jnp.cumsum(tile_counts) - tile_counts
    tile_index = jnp.arange(tile_total, dtype=jnp.int32)
    start_of = jnp.max(
        jnp.where(starts[None, :] <= tile_index[:, None], starts[None, :], -1), axis=1
    )
    owner_of = start_of // tile_group
    owners_total = tile_total // tile_group
    edge_tiles = jnp.arange(owners_total + 1, dtype=jnp.int32) * tile_group
    first_tile = jnp.min(
        jnp.where(starts[None, :] >= edge_tiles[:, None], starts[None, :], tile_total), axis=1
    )
    return (owner_of, first_tile)


def norm_kernel(tokens_ref, out_ref, ordered):
    rows = tokens_ref[0].astype(jnp.float32)
    normed = rows * lax.rsqrt(jnp.mean(rows * rows, axis=-1, keepdims=True) + 1e-06)
    groups = LINE * LINE
    share = rows.shape[1] // (LINE * groups)
    for line in range(LINE):
        for group in range(groups):
            source = (line * groups + group) * share
            target = (group * LINE + line) * share
            ordered[:, target : target + share] = normed[:, source : source + share]
    out_ref[0] = ordered[...].astype(jnp.bfloat16)


def norm_rows(tokens):
    tiles, half, depth = tokens.shape
    block = 64
    spec = pl.BlockSpec((1, block, depth), lambda t, r: (t, r, 0))
    return pl.pallas_call(
        norm_kernel,
        grid=(tiles, half // block),
        out_shape=jax.ShapeDtypeStruct(tokens.shape, jnp.bfloat16),
        in_specs=[spec],
        out_specs=spec,
        scratch_shapes=[pltpu.VMEM((block, depth), jnp.float32)],
        compiler_params=pltpu.CompilerParams(vmem_limit_bytes=VMEM_BYTES),
        cost_estimate=SMALL_COST,
        name="norm",
    )(tokens)


def attend_kernel(layout, *refs):
    count = len(layout)
    pieces = sum(2 * len(tiles) for tiles in layout)
    sources, weight_hbm = list(refs[:pieces]), refs[pieces]
    outs = refs[pieces + 1 : pieces + 1 + count]
    rows, weight, qkv, row_sems, weight_sem = refs[pieces + 1 + count :]
    _, _, tiles, half, depth = rows.shape
    heads = weight.shape[1] // (3 * HEAD_DIM)

    def fetch(index):
        slot = index % 2
        copies = []
        for part in range(2):
            start = 0
            for place, length in enumerate(layout[index]):
                target = rows.at[slot, part, pl.ds(start, length)]
                copies.append(
                    pltpu.make_async_copy(sources.pop(0), target, row_sems.at[slot, part, place])
                )
                start += length
        return copies

    weight_copy = pltpu.make_async_copy(weight_hbm, weight, weight_sem)
    pending = fetch(0)
    for copy in pending:
        copy.start()
    weight_copy.start()
    for index in range(count):
        current = pending
        if index + 1 < count:
            pending = fetch(index + 1)
            for copy in pending:
                copy.start()
        for copy in current:
            copy.wait()
        if index == 0:
            weight_copy.wait()
        block = rows[index % 2].reshape(2 * tiles * half, depth)
        qkv[...] = jnp.dot(block, weight[...], preferred_element_type=jnp.float32).astype(jnp.bfloat16)
        for tile in range(tiles):
            for head in range(heads):

                def piece(kind):
                    start = (head * 3 + kind) * HEAD_DIM
                    columns = slice(start, start + HEAD_DIM)
                    low = qkv[tile * half : (tile + 1) * half, columns]
                    high = qkv[(tiles + tile) * half : (tiles + tile + 1) * half, columns]
                    return jnp.concatenate([low, high], axis=0)

                scores = lax.dot_general(
                    piece(0), piece(1), (((1,), (1,)), ((), ())), preferred_element_type=jnp.float32
                ) * (1.0 / math.sqrt(HEAD_DIM))
                scores = scores - jnp.max(scores, axis=-1, keepdims=True)
                raised = jnp.exp(scores)
                inverse = 1.0 / jnp.sum(raised, axis=-1, keepdims=True)
                soft = (raised * inverse).astype(jnp.bfloat16)
                mixed = jnp.dot(soft, piece(2), preferred_element_type=jnp.float32)
                columns = slice(head * HEAD_DIM, (head + 1) * HEAD_DIM)
                outs[index][:, tile, :, columns] = mixed.astype(jnp.bfloat16).reshape(2, half, HEAD_DIM)


def attend(sources, weight):
    layout = tuple(tuple(array.shape[0] for array in own) for own, _ in sources)
    tiles = sum(layout[0])
    _, half, depth = sources[0][0][0].shape
    width = weight.shape[1]
    shape = (2, tiles, half, width // 3)
    arrays = [array for own, other in sources for array in (*own, *other)]
    return pl.pallas_call(
        functools.partial(attend_kernel, layout),
        out_shape=[jax.ShapeDtypeStruct(shape, jnp.bfloat16)] * len(layout),
        in_specs=[pl.BlockSpec(memory_space=pl.ANY)] * (len(arrays) + 1),
        out_specs=[pl.BlockSpec(memory_space=pltpu.VMEM)] * len(layout),
        scratch_shapes=[
            pltpu.VMEM((2, 2, tiles, half, depth), jnp.bfloat16),
            pltpu.VMEM((depth, width), jnp.bfloat16),
            pltpu.VMEM((2 * tiles * half, width), jnp.bfloat16),
            pltpu.SemaphoreType.DMA((2, 2, tiles)),
            pltpu.SemaphoreType.DMA,
        ],
        compiler_params=pltpu.CompilerParams(vmem_limit_bytes=VMEM_BYTES),
        cost_estimate=SMALL_COST,
        name="attend",
    )(*arrays, weight)


def join_kernel(line_ref, mixing_ref, *refs):
    own, other = refs[:LINE], refs[LINE : 2 * LINE]
    own_weight_ref, other_weight_ref, scale_ref = refs[2 * LINE : 2 * LINE + 3]
    inputs_hbm = refs[2 * LINE + 3 : 2 * LINE + 6]
    z_ref, first_ref, second_ref, inverse_ref, rows, total, inputs, sems = refs[2 * LINE + 6 :]
    step = pl.program_id(0)
    _, tiles, half, share = own[0].shape
    block = own_weight_ref.shape[1]
    copies = [
        pltpu.make_async_copy(source, inputs.at[i], sems.at[i]) for i, source in enumerate(inputs_hbm)
    ]

    @pl.when(step == 0)
    def _():
        for copy in copies:
            copy.start()
        for distance in range(LINE):
            start = pl.multiple_of(lax.rem(line_ref[0] + distance, LINE) * share, share)
            rows[0, :, pl.ds(start, share)] = own[distance][0].reshape(tiles * half, share)
            rows[1, :, pl.ds(start, share)] = other[distance][...].reshape(tiles * half, share)

    part = jnp.dot(rows[0], own_weight_ref[...], preferred_element_type=jnp.float32)
    part += jnp.dot(rows[1], other_weight_ref[...], preferred_element_type=jnp.float32)
    total[:, pl.ds(pl.multiple_of(step * block, block), block)] = part

    @pl.when(step == pl.num_programs(0) - 1)
    def _():
        for copy in copies:
            copy.wait()
        chunk = 64
        scale = mixing_ref[3] * scale_ref[...]
        for tile in range(tiles):
            for start in range(0, half, chunk):
                span = slice(start, start + chunk)
                joined = (
                    (mixing_ref[2] + mixing_ref[3]) * inputs[0, tile, span].astype(jnp.float32)
                    + mixing_ref[0] * inputs[1, tile, span].astype(jnp.float32)
                    + mixing_ref[1] * inputs[2, tile, span].astype(jnp.float32)
                    + scale * total[tile * half + start : tile * half + start + chunk]
                )
                centre = jnp.mean(joined, axis=-1, keepdims=True)
                shifted = joined - centre
                inverse = lax.rsqrt(jnp.mean(shifted * shifted, axis=-1, keepdims=True) + 1e-05)
                z_rows = (shifted * inverse).astype(jnp.bfloat16)
                z_ref[tile, span] = z_rows
                (first_ref, second_ref)[tile][0, span] = z_rows
                inverse_ref[tile, span] = jnp.broadcast_to(inverse, (chunk, 128))


def join_rows(line_arg, mixing, attended, swapped, weights, scale, inputs):
    _, tiles, half, share = attended[0].shape
    depth = weights[0].shape[1]
    block = 640
    weight_spec = pl.BlockSpec((LINE * share, block), lambda n, line: (0, n))
    return pl.pallas_call(
        join_kernel,
        grid_spec=pltpu.PrefetchScalarGridSpec(
            num_scalar_prefetch=1,
            grid=(depth // block,),
            in_specs=[pl.BlockSpec(memory_space=pltpu.SMEM)]
            + [pl.BlockSpec((1, tiles, half, share), lambda n, line: (0, 0, 0, 0))] * LINE
            + [pl.BlockSpec((tiles, half, share), lambda n, line: (0, 0, 0))] * LINE
            + [weight_spec, weight_spec, pl.BlockSpec((1, depth), lambda n, line: (0, 0))]
            + [pl.BlockSpec(memory_space=pl.ANY)] * 3,
            out_specs=[
                pl.BlockSpec((tiles, half, depth), lambda n, line: (0, 0, 0)),
                pl.BlockSpec((1, half, depth), lambda n, line: (0, 0, 0)),
                pl.BlockSpec((1, half, depth), lambda n, line: (0, 0, 0)),
                pl.BlockSpec((tiles, half, 128), lambda n, line: (0, 0, 0)),
            ],
            scratch_shapes=[
                pltpu.VMEM((2, tiles * half, LINE * share), jnp.bfloat16),
                pltpu.VMEM((tiles * half, depth), jnp.float32),
                pltpu.VMEM((3, tiles, half, depth), jnp.bfloat16),
                pltpu.SemaphoreType.DMA((3,)),
            ],
        ),
        out_shape=[
            jax.ShapeDtypeStruct((tiles, half, depth), jnp.bfloat16),
            jax.ShapeDtypeStruct((1, half, depth), jnp.bfloat16),
            jax.ShapeDtypeStruct((1, half, depth), jnp.bfloat16),
            jax.ShapeDtypeStruct((tiles, half, 128), jnp.float32),
        ],
        compiler_params=pltpu.CompilerParams(vmem_limit_bytes=VMEM_BYTES),
        cost_estimate=SMALL_COST,
        name="join",
    )(line_arg, mixing, *attended, *swapped, *weights, scale, *inputs)


def final_kernel(own_ref, other_ref, z_ref, inverse_ref, out_ref):
    grad = own_ref[0].astype(jnp.float32) + other_ref[0].astype(jnp.float32)
    normal = z_ref[0].astype(jnp.float32)
    mean = jnp.mean(grad, axis=-1, keepdims=True)
    along = jnp.mean(grad * normal, axis=-1, keepdims=True)
    out_ref[0] = ((grad - mean - normal * along) * inverse_ref[0, :, :1]).astype(jnp.bfloat16)


def final_rows(own, other, z_rows, inverse):
    tiles, half, depth = own.shape
    block = 64
    spec = pl.BlockSpec((1, block, depth), lambda t, r: (t, r, 0))
    return pl.pallas_call(
        final_kernel,
        grid=(tiles, half // block),
        out_shape=jax.ShapeDtypeStruct(own.shape, jnp.bfloat16),
        in_specs=[spec, spec, spec, pl.BlockSpec((1, block, 128), lambda t, r: (t, r, 0))],
        out_specs=spec,
        compiler_params=pltpu.CompilerParams(vmem_limit_bytes=VMEM_BYTES),
        cost_estimate=SMALL_COST,
        name="final",
    )(own, other, z_rows, inverse)


def activate(preact):
    raised = jnp.exp(-0.5 * preact * preact)
    step = 1.0 / (1.0 + 0.3275911 * inv_root_two * jnp.abs(preact))
    series = 1.061405429 * step - 1.453152027
    series = series * step + 1.421413741
    series = series * step - 0.284496736
    series = series * step + 0.254829592
    tail = 0.5 * series * step * raised
    return jnp.where(preact >= 0.0, 1.0 - tail, tail), raised * inv_root_tau


def project_kernel(core_ref, own_ref, other_ref, weight_ref, bias_ref, projected_ref, slope_ref):
    core = core_ref[0]
    tiles, half, depth = own_ref.shape
    block = weight_ref.shape[1]
    rows = jnp.concatenate(
        [own_ref[...].reshape(tiles * half, depth), other_ref[...].reshape(tiles * half, depth)], axis=0
    )
    preact = jnp.dot(rows, weight_ref[...], preferred_element_type=jnp.float32) + bias_ref[...]
    cumulative, density = activate(preact)
    projected = (preact * cumulative).astype(jnp.bfloat16).reshape(2, tiles, 1, half, block)
    projected_ref[:, pl.ds(core, 1)] = projected[0]
    projected_ref[:, pl.ds(1 - core, 1)] = projected[1]
    slope_ref[...] = cumulative + preact * density


def home_project(core, own, other, weight, bias):
    tiles, half, depth = own.shape
    width = weight.shape[1]
    block = 512
    whole = pl.BlockSpec((tiles, half, depth), lambda n, c: (0, 0, 0))
    projected, slope = pl.pallas_call(
        project_kernel,
        grid_spec=pltpu.PrefetchScalarGridSpec(
            num_scalar_prefetch=1,
            grid=(width // block,),
            in_specs=[
                whole,
                whole,
                pl.BlockSpec((depth, block), lambda n, c: (0, n)),
                pl.BlockSpec((1, block), lambda n, c: (0, n)),
            ],
            out_specs=[
                pl.BlockSpec((tiles, 2, half, block), lambda n, c: (0, 0, 0, n)),
                pl.BlockSpec((2 * tiles * half, block), lambda n, c: (0, n)),
            ],
        ),
        out_shape=[
            jax.ShapeDtypeStruct((tiles, 2, half, width), jnp.bfloat16),
            jax.ShapeDtypeStruct((2 * tiles * half, width), jnp.float32),
        ],
        compiler_params=pltpu.CompilerParams(vmem_limit_bytes=VMEM_BYTES),
        cost_estimate=SMALL_COST,
        name="project",
    )(core, own, other, weight, bias)
    return projected.reshape(tiles, 2 * half, width), slope


def grad_kernel(core_ref, slope_ref, back_own_ref, back_other_ref, weight_ref, own_ref, other_ref, total):
    step = pl.program_id(0)
    tiles, half, depth = own_ref.shape
    rows, block = slope_ref.shape
    back = jnp.concatenate(
        [ref[...].reshape(tiles * half, block) for ref in (back_own_ref, back_other_ref)], axis=0
    )
    slope_rows = (back.astype(jnp.float32) * slope_ref[...]).astype(jnp.bfloat16)
    term = lax.dot_general(
        slope_rows, weight_ref[...], (((1,), (1,)), ((), ())), preferred_element_type=jnp.float32
    )

    @pl.when(step == 0)
    def _():
        total[...] = term

    @pl.when(step > 0)
    def _():
        total[...] += term

    @pl.when(step == pl.num_programs(0) - 1)
    def _():
        own_ref[...] = total[: tiles * half].astype(jnp.bfloat16).reshape(tiles, half, depth)
        other_ref[...] = total[tiles * half :].astype(jnp.bfloat16).reshape(tiles, half, depth)


def home_grad(core, slope, back, weight):
    tiles, full, width = back.shape
    half = full // 2
    depth = weight.shape[0]
    block = 512
    back = back.reshape(tiles, 2, half, width)
    whole = pl.BlockSpec((tiles, half, depth), lambda n, c: (0, 0, 0))
    shape = jax.ShapeDtypeStruct((tiles, half, depth), jnp.bfloat16)
    return pl.pallas_call(
        grad_kernel,
        grid_spec=pltpu.PrefetchScalarGridSpec(
            num_scalar_prefetch=1,
            grid=(width // block,),
            in_specs=[
                pl.BlockSpec((tiles * full, block), lambda n, c: (0, n)),
                pl.BlockSpec((tiles, 1, half, block), lambda n, c: (0, c[0], 0, n)),
                pl.BlockSpec((tiles, 1, half, block), lambda n, c: (0, 1 - c[0], 0, n)),
                pl.BlockSpec((depth, block), lambda n, c: (0, n)),
            ],
            out_specs=[whole, whole],
            scratch_shapes=[pltpu.VMEM((tiles * full, depth), jnp.float32)],
        ),
        out_shape=[shape, shape],
        compiler_params=pltpu.CompilerParams(vmem_limit_bytes=VMEM_BYTES),
        cost_estimate=SMALL_COST,
        name="grad",
    )(core, slope, back, back, weight)


def owner_kernel(count, core_ref, *refs):
    sources = refs[: 2 * count]
    weight_ref, bias_ref, projected_ref = refs[2 * count :]
    core = core_ref[0]
    _, half, _ = sources[0].shape
    block = weight_ref.shape[1]
    rows = jnp.concatenate([source[0] for source in sources], axis=0)
    preact = jnp.dot(rows, weight_ref[...], preferred_element_type=jnp.float32) + bias_ref[...]
    projected = (preact * activate(preact)[0]).astype(jnp.bfloat16).reshape(2, count, 1, half, block)
    projected_ref[:, pl.ds(core, 1)] = projected[0]
    projected_ref[:, pl.ds(1 - core, 1)] = projected[1]


def owner_project(core, own, weight, bias):
    count = len(own)
    _, half, depth = own[0].shape
    width = weight.shape[1]
    block = 512
    projected = pl.pallas_call(
        functools.partial(owner_kernel, count),
        grid_spec=pltpu.PrefetchScalarGridSpec(
            num_scalar_prefetch=1,
            grid=(width // block,),
            in_specs=[pl.BlockSpec((1, half, depth), lambda n, c: (0, 0, 0))] * (2 * count)
            + [
                pl.BlockSpec((depth, block), lambda n, c: (0, n)),
                pl.BlockSpec((1, block), lambda n, c: (0, n)),
            ],
            out_specs=pl.BlockSpec((count, 2, half, block), lambda n, c: (0, 0, 0, n)),
        ),
        out_shape=jax.ShapeDtypeStruct((count, 2, half, width), jnp.bfloat16),
        compiler_params=pltpu.CompilerParams(vmem_limit_bytes=VMEM_BYTES),
        cost_estimate=SMALL_COST,
        name="owner",
    )(core, *own, *[swap(rows) for rows in own], weight, bias)
    return projected.reshape(count, 2 * half, width)


def on_device(
    tokens, tap_early, tap_mid, tile_counts, qkv_weight, out_weight, layer_scale, layer_logits,
    proj_weight, proj_bias, grad_out,
):
    tile_group, token_share, depth = tokens.shape
    img_count = lax.axis_size(IMG)
    place = lax.axis_index(IMG)
    line_place = lax.axis_index("z")
    core = lax.axis_index("head")
    core_arg = core.astype(jnp.int32).reshape(1)
    tile_total = tile_group * img_count
    own_tiles = grad_out.shape[0]
    owner_of, first_tile = tile_owners(tile_counts, tile_total, tile_group)
    my_first = first_tile[place]

    depth_share, width = qkv_weight.shape
    share = width // LINE
    received = []
    for distance in range(LINE):
        target = (line_place + distance) % LINE
        columns = lax.dynamic_slice_in_dim(qkv_weight, target * share, share, axis=1)
        received.append(along_z(columns, distance) if distance else columns)
    normed = norm_rows(tokens)
    normed, received = lax.optimization_barrier((normed, received))
    ladder = jnp.stack([received[(LINE - 1 - j) % LINE] for j in range(2 * LINE - 1)], axis=0)
    sent = lax.dynamic_slice_in_dim(ladder, LINE - 1 - line_place, LINE, axis=0)
    weight = lax.all_gather(sent.reshape(LINE * depth_share, share), ("y", "x"), axis=0, tiled=True)

    def packet(distance, within, count, first):
        tile = (place + distance) * tile_group + within
        slot = jnp.clip(tile - first, 0, own_tiles - count)
        return lax.dynamic_slice_in_dim(grad_out, slot, count, axis=0)

    from_low = along_z(normed, 1)
    from_high = along_z(normed, -1)

    def packet(distance, within, count):
        tile = (place + distance) * tile_group + within
        slot = jnp.clip(tile - my_first, 0, own_tiles - count)
        return lax.dynamic_slice_in_dim(grad_out, slot, count, axis=0)

    packets = [packet(2, 0, 1), packet(2, 1, 1), packet(1, 0, tile_group)]
    other_weight = swap(out_weight)
    from_low, from_high, packets, other_weight = lax.optimization_barrier(
        (from_low, from_high, packets, other_weight)
    )
    far_first = along_z(from_low[:1], 1)
    far_second = along_z(from_high[1:], -1)
    far_first, far_second, weight, packets = lax.optimization_barrier(
        (far_first, far_second, weight, packets)
    )
    far_back = [along_img(packets[0], 2), along_img(packets[1], 2)]
    near_back = along_img(packets[2], 1)

    att_low, att_high, att_own = attend(
        [([rows], [swap(rows)]) for rows in (from_low, from_high, normed)], weight
    )
    far_first, far_second, att_own, far_back[0] = lax.optimization_barrier(
        (far_first, far_second, att_own, far_back[0])
    )
    (att_far,) = attend(
        [([far_first, far_second], [swap(far_first), swap(far_second)])], weight
    )
    attended = [att_own, along_z(att_low, -1), along_z(att_far, 2), along_z(att_high, 1)]
    raised_logits = jnp.exp(layer_logits)
    mixing = raised_logits / jnp.sum(raised_logits)
    z_rows, z_first, z_second, inverse_std = join_rows(
        line_place.astype(jnp.int32).reshape(1),
        mixing,
        attended,
        [swap(rows[1]) for rows in attended],
        [out_weight, other_weight],
        layer_scale.reshape(1, -1),
        [tokens, tap_early, tap_mid],
    )

    near = [along_img(z_first, -1)]
    far = [along_img(z_first, -2)]
    bias = proj_bias.reshape(1, -1)
    projected, slope = home_project(core_arg, z_rows, swap(z_rows), proj_weight, bias)
    near[0], far[0], second, slope = lax.optimization_barrier((near[0], far[0], z_second, slope))
    near.append(along_img(second, -1))
    far.append(along_img(second, -2))
    early = owner_project(core_arg, [near[0], far[0]], proj_weight, bias)
    slope, early, near_back, far_back[1] = lax.optimization_barrier(
        (slope, early, near_back, far_back[1])
    )

    back = []
    for within in range(tile_group):
        tile = place * tile_group + within
        owner = owner_of[tile]
        slot = jnp.clip(tile - my_first, 0, own_tiles - 1)
        here = lax.dynamic_index_in_dim(grad_out, slot, axis=0, keepdims=False)
        other = jnp.where(owner == place - 1, near_back[within], far_back[within][0])
        back.append(jnp.where(owner == place, here, other))
    back_rows = jnp.stack(back, axis=0)
    grad_own, grad_other = home_grad(core_arg, slope, back_rows, proj_weight)

    grad_joined = final_rows(grad_own, swap(grad_other), z_rows, inverse_std)
    near[1], far[1], grad_joined = lax.optimization_barrier((near[1], far[1], grad_joined))
    late = owner_project(core_arg, [near[1], far[1]], proj_weight, bias)

    offset = my_first - place * tile_group
    held = first_tile[place + 1] - my_first
    at_hand = [projected[0], projected[1], early[0], late[0], early[1], late[1]]
    slots = []
    for slot in range(own_tiles):
        later = at_hand[min(slot + 1, len(at_hand) - 1)]
        picked = jnp.where(offset == 0, at_hand[slot], later)
        slots.append(jnp.where(slot < held, picked, jnp.zeros((), jnp.bfloat16)))
    owner_rows = jnp.stack(slots, axis=0)
    return (owner_rows, grad_joined)


def solution(mesh):
    cores = mesh.devices.shape[-1]
    inner = Mesh(mesh.devices.reshape(LINE, LINE, LINE, cores), IMG + ("head",))
    return jax.shard_map(
        on_device,
        mesh=inner,
        in_specs=(
            P(IMG, "head", None),
            P(IMG, "head", None),
            P(IMG, "head", None),
            P(),
            P(IMG, "head"),
            P("head", None),
            P(),
            P(),
            P(None, "head"),
            P("head"),
            P(IMG, None, "head"),
        ),
        out_specs=(P(IMG, None, "head"), P(IMG, "head", None)),
        check_vma=False,
    )
```

```python
import functools
import math

import jax
import jax.numpy as jnp
from jax import lax
from jax.experimental import pallas as pl
from jax.experimental.pallas import tpu as pltpu
from jax.sharding import Mesh, PartitionSpec as P

HEAD_DIM = 128
LINE = 4
IMG = ("z", "y", "x")
VMEM_BYTES = 56 * 1024 * 1024
SMALL_COST = pl.CostEstimate(flops=1, bytes_accessed=1, transcendentals=0)

inv_root_two = 0.7071067811865476
inv_root_tau = 0.3989422804014327


def swap(array):
    return lax.ppermute(array, "head", [(0, 1), (1, 0)])


def along_z(array, by):
    return lax.ppermute(array, "z", [(i, (i + by) % LINE) for i in range(LINE)])


def along_img(array, by):
    peers = lax.axis_size(IMG)
    pairs = [(i, i + by) for i in range(peers) if 0 <= i + by < peers]
    return lax.ppermute(array, IMG, pairs)


def tile_owners(tile_counts, tile_total, tile_group):
    starts = jnp.cumsum(tile_counts) - tile_counts
    tile_index = jnp.arange(tile_total, dtype=jnp.int32)
    start_of = jnp.max(
        jnp.where(starts[None, :] <= tile_index[:, None], starts[None, :], -1), axis=1
    )
    owner_of = start_of // tile_group
    owners_total = tile_total // tile_group
    edge_tiles = jnp.arange(owners_total + 1, dtype=jnp.int32) * tile_group
    first_tile = jnp.min(
        jnp.where(starts[None, :] >= edge_tiles[:, None], starts[None, :], tile_total), axis=1
    )
    return (owner_of, first_tile)


def norm_kernel(tokens_ref, out_ref, ordered):
    rows = tokens_ref[0].astype(jnp.float32)
    normed = rows * lax.rsqrt(jnp.mean(rows * rows, axis=-1, keepdims=True) + 1e-06)
    groups = LINE * LINE
    share = rows.shape[1] // (LINE * groups)
    for line in range(LINE):
        for group in range(groups):
            source = (line * groups + group) * share
            target = (group * LINE + line) * share
            ordered[:, target : target + share] = normed[:, source : source + share]
    out_ref[0] = ordered[...].astype(jnp.bfloat16)


def norm_rows(tokens):
    tiles, half, depth = tokens.shape
    block = 64
    spec = pl.BlockSpec((1, block, depth), lambda t, r: (t, r, 0))
    return pl.pallas_call(
        norm_kernel,
        grid=(tiles, half // block),
        out_shape=jax.ShapeDtypeStruct(tokens.shape, jnp.bfloat16),
        in_specs=[spec],
        out_specs=spec,
        scratch_shapes=[pltpu.VMEM((block, depth), jnp.float32)],
        compiler_params=pltpu.CompilerParams(vmem_limit_bytes=VMEM_BYTES),
        cost_estimate=SMALL_COST,
        name="norm",
    )(tokens)


def attend_kernel(layout, *refs):
    count = len(layout)
    pieces = sum(2 * len(tiles) for tiles in layout)
    sources, weight_hbm = list(refs[:pieces]), refs[pieces]
    outs = refs[pieces + 1 : pieces + 1 + count]
    rows, weight, qkv, row_sems, weight_sem = refs[pieces + 1 + count :]
    _, _, tiles, half, depth = rows.shape
    heads = weight.shape[1] // (3 * HEAD_DIM)

    def fetch(index):
        slot = index % 2
        copies = []
        for part in range(2):
            start = 0
            for place, length in enumerate(layout[index]):
                target = rows.at[slot, part, pl.ds(start, length)]
                copies.append(
                    pltpu.make_async_copy(sources.pop(0), target, row_sems.at[slot, part, place])
                )
                start += length
        return copies

    weight_copy = pltpu.make_async_copy(weight_hbm, weight, weight_sem)
    pending = fetch(0)
    for copy in pending:
        copy.start()
    weight_copy.start()
    for index in range(count):
        current = pending
        if index + 1 < count:
            pending = fetch(index + 1)
            for copy in pending:
                copy.start()
        for copy in current:
            copy.wait()
        if index == 0:
            weight_copy.wait()
        block = rows[index % 2].reshape(2 * tiles * half, depth)
        qkv[...] = jnp.dot(block, weight[...], preferred_element_type=jnp.float32).astype(jnp.bfloat16)
        for tile in range(tiles):
            for head in range(heads):

                def piece(kind):
                    start = (head * 3 + kind) * HEAD_DIM
                    columns = slice(start, start + HEAD_DIM)
                    low = qkv[tile * half : (tile + 1) * half, columns]
                    high = qkv[(tiles + tile) * half : (tiles + tile + 1) * half, columns]
                    return jnp.concatenate([low, high], axis=0)

                scores = lax.dot_general(
                    piece(0), piece(1), (((1,), (1,)), ((), ())), preferred_element_type=jnp.float32
                ) * (1.0 / math.sqrt(HEAD_DIM))
                scores = scores - jnp.max(scores, axis=-1, keepdims=True)
                raised = jnp.exp(scores)
                inverse = 1.0 / jnp.sum(raised, axis=-1, keepdims=True)
                soft = (raised * inverse).astype(jnp.bfloat16)
                mixed = jnp.dot(soft, piece(2), preferred_element_type=jnp.float32)
                columns = slice(head * HEAD_DIM, (head + 1) * HEAD_DIM)
                outs[index][:, tile, :, columns] = mixed.astype(jnp.bfloat16).reshape(2, half, HEAD_DIM)


def attend(sources, weight):
    layout = tuple(tuple(array.shape[0] for array in own) for own, _ in sources)
    tiles = sum(layout[0])
    _, half, depth = sources[0][0][0].shape
    width = weight.shape[1]
    shape = (2, tiles, half, width // 3)
    arrays = [array for own, other in sources for array in (*own, *other)]
    return pl.pallas_call(
        functools.partial(attend_kernel, layout),
        out_shape=[jax.ShapeDtypeStruct(shape, jnp.bfloat16)] * len(layout),
        in_specs=[pl.BlockSpec(memory_space=pl.ANY)] * (len(arrays) + 1),
        out_specs=[pl.BlockSpec(memory_space=pltpu.VMEM)] * len(layout),
        scratch_shapes=[
            pltpu.VMEM((2, 2, tiles, half, depth), jnp.bfloat16),
            pltpu.VMEM((depth, width), jnp.bfloat16),
            pltpu.VMEM((2 * tiles * half, width), jnp.bfloat16),
            pltpu.SemaphoreType.DMA((2, 2, tiles)),
            pltpu.SemaphoreType.DMA,
        ],
        compiler_params=pltpu.CompilerParams(vmem_limit_bytes=VMEM_BYTES),
        cost_estimate=SMALL_COST,
        name="attend",
    )(*arrays, weight)


def join_kernel(line_ref, mixing_ref, *refs):
    own, other = refs[:LINE], refs[LINE : 2 * LINE]
    own_weight_ref, other_weight_ref, scale_ref = refs[2 * LINE : 2 * LINE + 3]
    inputs_hbm = refs[2 * LINE + 3 : 2 * LINE + 6]
    z_ref, inverse_ref, rows, total, inputs, sems = refs[2 * LINE + 6 :]
    step = pl.program_id(0)
    _, tiles, half, share = own[0].shape
    block = own_weight_ref.shape[1]
    copies = [
        pltpu.make_async_copy(source, inputs.at[i], sems.at[i]) for i, source in enumerate(inputs_hbm)
    ]

    @pl.when(step == 0)
    def _():
        for copy in copies:
            copy.start()
        for distance in range(LINE):
            start = pl.multiple_of(lax.rem(line_ref[0] + distance, LINE) * share, share)
            rows[0, :, pl.ds(start, share)] = own[distance][0].reshape(tiles * half, share)
            rows[1, :, pl.ds(start, share)] = other[distance][...].reshape(tiles * half, share)

    part = jnp.dot(rows[0], own_weight_ref[...], preferred_element_type=jnp.float32)
    part += jnp.dot(rows[1], other_weight_ref[...], preferred_element_type=jnp.float32)
    total[:, pl.ds(pl.multiple_of(step * block, block), block)] = part

    @pl.when(step == pl.num_programs(0) - 1)
    def _():
        for copy in copies:
            copy.wait()
        chunk = 64
        scale = mixing_ref[3] * scale_ref[...]
        for tile in range(tiles):
            for start in range(0, half, chunk):
                span = slice(start, start + chunk)
                joined = (
                    (mixing_ref[2] + mixing_ref[3]) * inputs[0, tile, span].astype(jnp.float32)
                    + mixing_ref[0] * inputs[1, tile, span].astype(jnp.float32)
                    + mixing_ref[1] * inputs[2, tile, span].astype(jnp.float32)
                    + scale * total[tile * half + start : tile * half + start + chunk]
                )
                centre = jnp.mean(joined, axis=-1, keepdims=True)
                shifted = joined - centre
                inverse = lax.rsqrt(jnp.mean(shifted * shifted, axis=-1, keepdims=True) + 1e-05)
                z_ref[tile, span] = (shifted * inverse).astype(jnp.bfloat16)
                inverse_ref[tile, span] = jnp.broadcast_to(inverse, (chunk, 128))


def join_rows(line_arg, mixing, attended, swapped, weights, scale, inputs):
    _, tiles, half, share = attended[0].shape
    depth = weights[0].shape[1]
    block = 640
    weight_spec = pl.BlockSpec((LINE * share, block), lambda n, line: (0, n))
    return pl.pallas_call(
        join_kernel,
        grid_spec=pltpu.PrefetchScalarGridSpec(
            num_scalar_prefetch=1,
            grid=(depth // block,),
            in_specs=[pl.BlockSpec(memory_space=pltpu.SMEM)]
            + [pl.BlockSpec((1, tiles, half, share), lambda n, line: (0, 0, 0, 0))] * LINE
            + [pl.BlockSpec((tiles, half, share), lambda n, line: (0, 0, 0))] * LINE
            + [weight_spec, weight_spec, pl.BlockSpec((1, depth), lambda n, line: (0, 0))]
            + [pl.BlockSpec(memory_space=pl.ANY)] * 3,
            out_specs=[
                pl.BlockSpec((tiles, half, depth), lambda n, line: (0, 0, 0)),
                pl.BlockSpec((tiles, half, 128), lambda n, line: (0, 0, 0)),
            ],
            scratch_shapes=[
                pltpu.VMEM((2, tiles * half, LINE * share), jnp.bfloat16),
                pltpu.VMEM((tiles * half, depth), jnp.float32),
                pltpu.VMEM((3, tiles, half, depth), jnp.bfloat16),
                pltpu.SemaphoreType.DMA((3,)),
            ],
        ),
        out_shape=[
            jax.ShapeDtypeStruct((tiles, half, depth), jnp.bfloat16),
            jax.ShapeDtypeStruct((tiles, half, 128), jnp.float32),
        ],
        compiler_params=pltpu.CompilerParams(vmem_limit_bytes=VMEM_BYTES),
        cost_estimate=SMALL_COST,
        name="join",
    )(line_arg, mixing, *attended, *swapped, *weights, scale, *inputs)


def final_kernel(own_ref, other_ref, z_ref, inverse_ref, out_ref):
    grad = own_ref[0].astype(jnp.float32) + other_ref[0].astype(jnp.float32)
    normal = z_ref[0].astype(jnp.float32)
    mean = jnp.mean(grad, axis=-1, keepdims=True)
    along = jnp.mean(grad * normal, axis=-1, keepdims=True)
    out_ref[0] = ((grad - mean - normal * along) * inverse_ref[0, :, :1]).astype(jnp.bfloat16)


def final_rows(own, other, z_rows, inverse):
    tiles, half, depth = own.shape
    block = 64
    spec = pl.BlockSpec((1, block, depth), lambda t, r: (t, r, 0))
    return pl.pallas_call(
        final_kernel,
        grid=(tiles, half // block),
        out_shape=jax.ShapeDtypeStruct(own.shape, jnp.bfloat16),
        in_specs=[spec, spec, spec, pl.BlockSpec((1, block, 128), lambda t, r: (t, r, 0))],
        out_specs=spec,
        compiler_params=pltpu.CompilerParams(vmem_limit_bytes=VMEM_BYTES),
        cost_estimate=SMALL_COST,
        name="final",
    )(own, other, z_rows, inverse)


def activate(preact):
    raised = jnp.exp(-0.5 * preact * preact)
    step = 1.0 / (1.0 + 0.3275911 * inv_root_two * jnp.abs(preact))
    series = 1.061405429 * step - 1.453152027
    series = series * step + 1.421413741
    series = series * step - 0.284496736
    series = series * step + 0.254829592
    tail = 0.5 * series * step * raised
    return jnp.where(preact >= 0.0, 1.0 - tail, tail), raised * inv_root_tau


def project_kernel(core_ref, own_ref, other_ref, weight_ref, bias_ref, projected_ref, slope_ref):
    core = core_ref[0]
    tiles, half, depth = own_ref.shape
    block = weight_ref.shape[1]
    rows = jnp.concatenate(
        [own_ref[...].reshape(tiles * half, depth), other_ref[...].reshape(tiles * half, depth)], axis=0
    )
    preact = jnp.dot(rows, weight_ref[...], preferred_element_type=jnp.float32) + bias_ref[...]
    cumulative, density = activate(preact)
    projected = (preact * cumulative).astype(jnp.bfloat16).reshape(2, tiles, 1, half, block)
    projected_ref[:, pl.ds(core, 1)] = projected[0]
    projected_ref[:, pl.ds(1 - core, 1)] = projected[1]
    slope_ref[...] = cumulative + preact * density


def home_project(core, own, other, weight, bias):
    tiles, half, depth = own.shape
    width = weight.shape[1]
    block = 512
    whole = pl.BlockSpec((tiles, half, depth), lambda n, c: (0, 0, 0))
    projected, slope = pl.pallas_call(
        project_kernel,
        grid_spec=pltpu.PrefetchScalarGridSpec(
            num_scalar_prefetch=1,
            grid=(width // block,),
            in_specs=[
                whole,
                whole,
                pl.BlockSpec((depth, block), lambda n, c: (0, n)),
                pl.BlockSpec((1, block), lambda n, c: (0, n)),
            ],
            out_specs=[
                pl.BlockSpec((tiles, 2, half, block), lambda n, c: (0, 0, 0, n)),
                pl.BlockSpec((2 * tiles * half, block), lambda n, c: (0, n)),
            ],
        ),
        out_shape=[
            jax.ShapeDtypeStruct((tiles, 2, half, width), jnp.bfloat16),
            jax.ShapeDtypeStruct((2 * tiles * half, width), jnp.float32),
        ],
        compiler_params=pltpu.CompilerParams(vmem_limit_bytes=VMEM_BYTES),
        cost_estimate=SMALL_COST,
        name="project",
    )(core, own, other, weight, bias)
    return projected.reshape(tiles, 2 * half, width), slope


def grad_kernel(core_ref, slope_ref, back_own_ref, back_other_ref, weight_ref, own_ref, other_ref, total):
    step = pl.program_id(0)
    tiles, half, depth = own_ref.shape
    rows, block = slope_ref.shape
    back = jnp.concatenate(
        [ref[...].reshape(tiles * half, block) for ref in (back_own_ref, back_other_ref)], axis=0
    )
    slope_rows = (back.astype(jnp.float32) * slope_ref[...]).astype(jnp.bfloat16)
    term = lax.dot_general(
        slope_rows, weight_ref[...], (((1,), (1,)), ((), ())), preferred_element_type=jnp.float32
    )

    @pl.when(step == 0)
    def _():
        total[...] = term

    @pl.when(step > 0)
    def _():
        total[...] += term

    @pl.when(step == pl.num_programs(0) - 1)
    def _():
        own_ref[...] = total[: tiles * half].astype(jnp.bfloat16).reshape(tiles, half, depth)
        other_ref[...] = total[tiles * half :].astype(jnp.bfloat16).reshape(tiles, half, depth)


def home_grad(core, slope, back, weight):
    tiles, full, width = back.shape
    half = full // 2
    depth = weight.shape[0]
    block = 512
    back = back.reshape(tiles, 2, half, width)
    whole = pl.BlockSpec((tiles, half, depth), lambda n, c: (0, 0, 0))
    shape = jax.ShapeDtypeStruct((tiles, half, depth), jnp.bfloat16)
    return pl.pallas_call(
        grad_kernel,
        grid_spec=pltpu.PrefetchScalarGridSpec(
            num_scalar_prefetch=1,
            grid=(width // block,),
            in_specs=[
                pl.BlockSpec((tiles * full, block), lambda n, c: (0, n)),
                pl.BlockSpec((tiles, 1, half, block), lambda n, c: (0, c[0], 0, n)),
                pl.BlockSpec((tiles, 1, half, block), lambda n, c: (0, 1 - c[0], 0, n)),
                pl.BlockSpec((depth, block), lambda n, c: (0, n)),
            ],
            out_specs=[whole, whole],
            scratch_shapes=[pltpu.VMEM((tiles * full, depth), jnp.float32)],
        ),
        out_shape=[shape, shape],
        compiler_params=pltpu.CompilerParams(vmem_limit_bytes=VMEM_BYTES),
        cost_estimate=SMALL_COST,
        name="grad",
    )(core, slope, back, back, weight)


def owner_kernel(core_ref, own_ref, other_ref, weight_ref, bias_ref, projected_ref):
    core = core_ref[0]
    tiles, half, depth = own_ref.shape
    block = weight_ref.shape[1]
    rows = jnp.concatenate(
        [own_ref[...].reshape(tiles * half, depth), other_ref[...].reshape(tiles * half, depth)], axis=0
    )
    preact = jnp.dot(rows, weight_ref[...], preferred_element_type=jnp.float32) + bias_ref[...]
    projected = (preact * activate(preact)[0]).astype(jnp.bfloat16).reshape(2, tiles, 1, half, block)
    projected_ref[:, pl.ds(core, 1)] = projected[0]
    projected_ref[:, pl.ds(1 - core, 1)] = projected[1]


def owner_project(core, own, other, weight, bias):
    tiles, half, depth = own.shape
    width = weight.shape[1]
    block = 512
    whole = pl.BlockSpec((tiles, half, depth), lambda n, c: (0, 0, 0))
    projected = pl.pallas_call(
        owner_kernel,
        grid_spec=pltpu.PrefetchScalarGridSpec(
            num_scalar_prefetch=1,
            grid=(width // block,),
            in_specs=[
                whole,
                whole,
                pl.BlockSpec((depth, block), lambda n, c: (0, n)),
                pl.BlockSpec((1, block), lambda n, c: (0, n)),
            ],
            out_specs=pl.BlockSpec((tiles, 2, half, block), lambda n, c: (0, 0, 0, n)),
        ),
        out_shape=jax.ShapeDtypeStruct((tiles, 2, half, width), jnp.bfloat16),
        compiler_params=pltpu.CompilerParams(vmem_limit_bytes=VMEM_BYTES),
        cost_estimate=SMALL_COST,
        name="owner",
    )(core, own, other, weight, bias)
    return projected.reshape(tiles, 2 * half, width)


def place_kernel(first_slot, split, slots_ref, *refs):
    low_ref, high_ref, out_ref = refs[0], refs[1], refs[-1]
    slot = pl.program_id(0) + first_slot
    index = slot + slots_ref[0]
    rows = jnp.where(index < split, low_ref[...], high_ref[...])
    out_ref[...] = jnp.where(slot < slots_ref[1], rows, jnp.zeros_like(rows))


def place_tiles(slots, low, high, own_tiles, held):
    tiles, full, width = low.shape
    count = own_tiles // 2
    first_slot = 0 if held is None else count
    split = tiles if held is None else 2 * tiles

    def spec(start):
        def at(k, s):
            return (jnp.clip(k + first_slot + s[0] - start, 0, tiles - 1), 0, 0)

        return pl.BlockSpec((1, full, width), at)

    in_specs = [spec(split - tiles), spec(split)]
    operands = [low, high]
    aliases = {}
    if held is not None:
        in_specs.append(pl.BlockSpec(memory_space=pl.ANY))
        operands.append(held)
        aliases = {3: 0}
    return pl.pallas_call(
        functools.partial(place_kernel, first_slot, split),
        grid_spec=pltpu.PrefetchScalarGridSpec(
            num_scalar_prefetch=1,
            grid=(count,),
            in_specs=in_specs,
            out_specs=pl.BlockSpec((1, full, width), lambda k, s: (k + first_slot, 0, 0)),
        ),
        out_shape=jax.ShapeDtypeStruct((own_tiles, full, width), jnp.bfloat16),
        input_output_aliases=aliases,
        compiler_params=pltpu.CompilerParams(vmem_limit_bytes=VMEM_BYTES),
        cost_estimate=SMALL_COST,
        name="place",
    )(slots, *operands)


def on_device(
    tokens, tap_early, tap_mid, tile_counts, qkv_weight, out_weight, layer_scale, layer_logits,
    proj_weight, proj_bias, grad_out,
):
    tile_group, token_share, depth = tokens.shape
    img_count = lax.axis_size(IMG)
    place = lax.axis_index(IMG)
    line_place = lax.axis_index("z")
    core = lax.axis_index("head")
    core_arg = core.astype(jnp.int32).reshape(1)
    tile_total = tile_group * img_count
    own_tiles = grad_out.shape[0]
    owner_of, first_tile = tile_owners(tile_counts, tile_total, tile_group)
    my_first = first_tile[place]

    depth_share, width = qkv_weight.shape
    share = width // LINE
    received = []
    for distance in range(LINE):
        target = (line_place + distance) % LINE
        columns = lax.dynamic_slice_in_dim(qkv_weight, target * share, share, axis=1)
        received.append(along_z(columns, distance) if distance else columns)
    normed = norm_rows(tokens)
    normed, received = lax.optimization_barrier((normed, received))
    ladder = jnp.stack([received[(LINE - 1 - j) % LINE] for j in range(2 * LINE - 1)], axis=0)
    sent = lax.dynamic_slice_in_dim(ladder, LINE - 1 - line_place, LINE, axis=0)
    weight = lax.all_gather(sent.reshape(LINE * depth_share, share), ("y", "x"), axis=0, tiled=True)

    def packet(distance, within, count, first):
        tile = (place + distance) * tile_group + within
        slot = jnp.clip(tile - first, 0, own_tiles - count)
        return lax.dynamic_slice_in_dim(grad_out, slot, count, axis=0)

    from_low = along_z(normed, 1)
    from_high = along_z(normed, -1)

    def packet(distance, within, count):
        tile = (place + distance) * tile_group + within
        slot = jnp.clip(tile - my_first, 0, own_tiles - count)
        return lax.dynamic_slice_in_dim(grad_out, slot, count, axis=0)

    packets = [packet(2, 0, tile_group), packet(1, 0, tile_group)]
    other_weight = swap(out_weight)
    from_low, from_high, packets, other_weight = lax.optimization_barrier(
        (from_low, from_high, packets, other_weight)
    )
    far_first = along_z(from_low[:1], 1)
    far_second = along_z(from_high[1:], -1)
    far_first, far_second, weight, packets = lax.optimization_barrier(
        (far_first, far_second, weight, packets)
    )
    far_back = along_img(packets[0], 2)
    near_back = along_img(packets[1], 1)

    far_others = [swap(far_first), swap(far_second)]
    att_far, att_low, att_high = attend(
        [([far_first, far_second], far_others)]
        + [([rows], [swap(rows)]) for rows in (from_low, from_high)],
        weight,
    )
    normed_other = swap(normed)
    normed, att_far = lax.optimization_barrier((normed, att_far))
    (att_own,) = attend([([normed], [normed_other])], weight)
    attended = [att_own, along_z(att_low, -1), along_z(att_far, 2), along_z(att_high, 1)]
    swapped = [swap(rows[1]) for rows in attended]
    swapped, far_back = lax.optimization_barrier((swapped, far_back))
    raised_logits = jnp.exp(layer_logits)
    mixing = raised_logits / jnp.sum(raised_logits)
    z_rows, inverse_std = join_rows(
        line_place.astype(jnp.int32).reshape(1),
        mixing,
        attended,
        swapped,
        [out_weight, other_weight],
        layer_scale.reshape(1, -1),
        [tokens, tap_early, tap_mid],
    )

    near = along_img(z_rows, -1)
    bias = proj_bias.reshape(1, -1)
    projected, slope = home_project(core_arg, z_rows, swap(z_rows), proj_weight, bias)
    near, z_later, slope = lax.optimization_barrier((near, z_rows, slope))
    far = along_img(z_later, -2)
    near_projected = owner_project(core_arg, near, swap(near), proj_weight, bias)
    offset = my_first - place * tile_group
    held = first_tile[place + 1] - my_first
    slots = jnp.stack([offset, held]).astype(jnp.int32)
    owner_rows = place_tiles(slots, projected, near_projected, own_tiles, None)
    slope, near_projected, near_back = lax.optimization_barrier((slope, near_projected, near_back))

    back = []
    for within in range(tile_group):
        tile = place * tile_group + within
        owner = owner_of[tile]
        slot = jnp.clip(tile - my_first, 0, own_tiles - 1)
        here = lax.dynamic_index_in_dim(grad_out, slot, axis=0, keepdims=False)
        other = jnp.where(owner == place - 1, near_back[within], far_back[within])
        back.append(jnp.where(owner == place, here, other))
    back_rows = jnp.stack(back, axis=0)
    grad_own, grad_other = home_grad(core_arg, slope, back_rows, proj_weight)

    grad_joined = final_rows(grad_own, swap(grad_other), z_rows, inverse_std)
    far, near_projected, grad_other = lax.optimization_barrier((far, near_projected, grad_other))
    far_other, grad_joined = lax.optimization_barrier((swap(far), grad_joined))
    far_projected = owner_project(core_arg, far, far_other, proj_weight, bias)
    owner_rows = place_tiles(slots, near_projected, far_projected, own_tiles, owner_rows)
    return (owner_rows, grad_joined)


def solution(mesh):
    cores = mesh.devices.shape[-1]
    inner = Mesh(mesh.devices.reshape(LINE, LINE, LINE, cores), IMG + ("head",))
    return jax.shard_map(
        on_device,
        mesh=inner,
        in_specs=(
            P(IMG, "head", None),
            P(IMG, "head", None),
            P(IMG, "head", None),
            P(),
            P(IMG, "head"),
            P("head", None),
            P(),
            P(),
            P(None, "head"),
            P("head"),
            P(IMG, None, "head"),
        ),
        out_specs=(P(IMG, None, "head"), P(IMG, "head", None)),
        check_vma=False,
    )
```

```python
import functools
import math

import jax
import jax.numpy as jnp
from jax import lax
from jax.experimental import pallas as pl
from jax.experimental.pallas import tpu as pltpu
from jax.sharding import Mesh, PartitionSpec as P

HEAD_DIM = 128
LINE = 4
IMG = ("z", "y", "x")
VMEM_BYTES = 56 * 1024 * 1024
SMALL_COST = pl.CostEstimate(flops=1, bytes_accessed=1, transcendentals=0)

inv_root_two = 0.7071067811865476
inv_root_tau = 0.3989422804014327


def swap(array):
    return lax.ppermute(array, "head", [(0, 1), (1, 0)])


def along_z(array, by):
    return lax.ppermute(array, "z", [(i, (i + by) % LINE) for i in range(LINE)])


def along_img(array, by):
    peers = lax.axis_size(IMG)
    pairs = [(i, i + by) for i in range(peers) if 0 <= i + by < peers]
    return lax.ppermute(array, IMG, pairs)


def tile_owners(tile_counts, tile_total, tile_group):
    starts = jnp.cumsum(tile_counts) - tile_counts
    tile_index = jnp.arange(tile_total, dtype=jnp.int32)
    start_of = jnp.max(
        jnp.where(starts[None, :] <= tile_index[:, None], starts[None, :], -1), axis=1
    )
    owner_of = start_of // tile_group
    owners_total = tile_total // tile_group
    edge_tiles = jnp.arange(owners_total + 1, dtype=jnp.int32) * tile_group
    first_tile = jnp.min(
        jnp.where(starts[None, :] >= edge_tiles[:, None], starts[None, :], tile_total), axis=1
    )
    return (owner_of, first_tile)


def norm_kernel(tokens_ref, out_ref, ordered):
    rows = tokens_ref[0].astype(jnp.float32)
    normed = rows * lax.rsqrt(jnp.mean(rows * rows, axis=-1, keepdims=True) + 1e-06)
    groups = LINE * LINE
    share = rows.shape[1] // (LINE * groups)
    for line in range(LINE):
        for group in range(groups):
            source = (line * groups + group) * share
            target = (group * LINE + line) * share
            ordered[:, target : target + share] = normed[:, source : source + share]
    out_ref[0] = ordered[...].astype(jnp.bfloat16)


def norm_rows(tokens):
    tiles, half, depth = tokens.shape
    block = 64
    spec = pl.BlockSpec((1, block, depth), lambda t, r: (t, r, 0))
    return pl.pallas_call(
        norm_kernel,
        grid=(tiles, half // block),
        out_shape=jax.ShapeDtypeStruct(tokens.shape, jnp.bfloat16),
        in_specs=[spec],
        out_specs=spec,
        scratch_shapes=[pltpu.VMEM((block, depth), jnp.float32)],
        compiler_params=pltpu.CompilerParams(vmem_limit_bytes=VMEM_BYTES),
        cost_estimate=SMALL_COST,
        name="norm",
    )(tokens)


def attend_kernel(layout, *refs):
    count = len(layout)
    pieces = sum(2 * len(tiles) for tiles in layout)
    sources, weight_hbm = list(refs[:pieces]), refs[pieces]
    outs = refs[pieces + 1 : pieces + 1 + count]
    rows, weight, qkv, row_sems, weight_sem = refs[pieces + 1 + count :]
    _, _, tiles, half, depth = rows.shape
    heads = weight.shape[1] // (3 * HEAD_DIM)

    def fetch(index):
        slot = index % 2
        copies = []
        for part in range(2):
            start = 0
            for place, length in enumerate(layout[index]):
                target = rows.at[slot, part, pl.ds(start, length)]
                copies.append(
                    pltpu.make_async_copy(sources.pop(0), target, row_sems.at[slot, part, place])
                )
                start += length
        return copies

    weight_copy = pltpu.make_async_copy(weight_hbm, weight, weight_sem)
    pending = fetch(0)
    for copy in pending:
        copy.start()
    weight_copy.start()
    for index in range(count):
        current = pending
        if index + 1 < count:
            pending = fetch(index + 1)
            for copy in pending:
                copy.start()
        for copy in current:
            copy.wait()
        if index == 0:
            weight_copy.wait()
        block = rows[index % 2].reshape(2 * tiles * half, depth)
        qkv[...] = jnp.dot(block, weight[...], preferred_element_type=jnp.float32).astype(jnp.bfloat16)
        for tile in range(tiles):
            for head in range(heads):

                def piece(kind):
                    start = (head * 3 + kind) * HEAD_DIM
                    columns = slice(start, start + HEAD_DIM)
                    low = qkv[tile * half : (tile + 1) * half, columns]
                    high = qkv[(tiles + tile) * half : (tiles + tile + 1) * half, columns]
                    return jnp.concatenate([low, high], axis=0)

                scores = lax.dot_general(
                    piece(0), piece(1), (((1,), (1,)), ((), ())), preferred_element_type=jnp.float32
                ) * (1.0 / math.sqrt(HEAD_DIM))
                scores = scores - jnp.max(scores, axis=-1, keepdims=True)
                raised = jnp.exp(scores)
                inverse = 1.0 / jnp.sum(raised, axis=-1, keepdims=True)
                soft = (raised * inverse).astype(jnp.bfloat16)
                mixed = jnp.dot(soft, piece(2), preferred_element_type=jnp.float32)
                columns = slice(head * HEAD_DIM, (head + 1) * HEAD_DIM)
                outs[index][:, tile, :, columns] = mixed.astype(jnp.bfloat16).reshape(2, half, HEAD_DIM)


def attend(sources, weight):
    layout = tuple(tuple(array.shape[0] for array in own) for own, _ in sources)
    tiles = sum(layout[0])
    _, half, depth = sources[0][0][0].shape
    width = weight.shape[1]
    shape = (2, tiles, half, width // 3)
    arrays = [array for own, other in sources for array in (*own, *other)]
    return pl.pallas_call(
        functools.partial(attend_kernel, layout),
        out_shape=[jax.ShapeDtypeStruct(shape, jnp.bfloat16)] * len(layout),
        in_specs=[pl.BlockSpec(memory_space=pl.ANY)] * (len(arrays) + 1),
        out_specs=[pl.BlockSpec(memory_space=pltpu.VMEM)] * len(layout),
        scratch_shapes=[
            pltpu.VMEM((2, 2, tiles, half, depth), jnp.bfloat16),
            pltpu.VMEM((depth, width), jnp.bfloat16),
            pltpu.VMEM((2 * tiles * half, width), jnp.bfloat16),
            pltpu.SemaphoreType.DMA((2, 2, tiles)),
            pltpu.SemaphoreType.DMA,
        ],
        compiler_params=pltpu.CompilerParams(vmem_limit_bytes=VMEM_BYTES),
        cost_estimate=SMALL_COST,
        name="attend",
    )(*arrays, weight)


def join_kernel(line_ref, mixing_ref, *refs):
    own, other = refs[:LINE], refs[LINE : 2 * LINE]
    own_weight_ref, other_weight_ref, scale_ref = refs[2 * LINE : 2 * LINE + 3]
    inputs_hbm = refs[2 * LINE + 3 : 2 * LINE + 6]
    z_ref, inverse_ref, rows, total, inputs, sems = refs[2 * LINE + 6 :]
    step = pl.program_id(0)
    _, tiles, half, share = own[0].shape
    block = own_weight_ref.shape[1]
    copies = [
        pltpu.make_async_copy(source, inputs.at[i], sems.at[i]) for i, source in enumerate(inputs_hbm)
    ]

    @pl.when(step == 0)
    def _():
        for copy in copies:
            copy.start()
        for distance in range(LINE):
            start = pl.multiple_of(lax.rem(line_ref[0] + distance, LINE) * share, share)
            rows[0, :, pl.ds(start, share)] = own[distance][0].reshape(tiles * half, share)
            rows[1, :, pl.ds(start, share)] = other[distance][...].reshape(tiles * half, share)

    part = jnp.dot(rows[0], own_weight_ref[...], preferred_element_type=jnp.float32)
    part += jnp.dot(rows[1], other_weight_ref[...], preferred_element_type=jnp.float32)
    total[:, pl.ds(pl.multiple_of(step * block, block), block)] = part

    @pl.when(step == pl.num_programs(0) - 1)
    def _():
        for copy in copies:
            copy.wait()
        chunk = 64
        scale = mixing_ref[3] * scale_ref[...]
        for tile in range(tiles):
            for start in range(0, half, chunk):
                span = slice(start, start + chunk)
                joined = (
                    (mixing_ref[2] + mixing_ref[3]) * inputs[0, tile, span].astype(jnp.float32)
                    + mixing_ref[0] * inputs[1, tile, span].astype(jnp.float32)
                    + mixing_ref[1] * inputs[2, tile, span].astype(jnp.float32)
                    + scale * total[tile * half + start : tile * half + start + chunk]
                )
                centre = jnp.mean(joined, axis=-1, keepdims=True)
                shifted = joined - centre
                inverse = lax.rsqrt(jnp.mean(shifted * shifted, axis=-1, keepdims=True) + 1e-05)
                z_ref[tile, span] = (shifted * inverse).astype(jnp.bfloat16)
                inverse_ref[tile, span] = jnp.broadcast_to(inverse, (chunk, 128))


def join_rows(line_arg, mixing, attended, swapped, weights, scale, inputs):
    _, tiles, half, share = attended[0].shape
    depth = weights[0].shape[1]
    block = 640
    weight_spec = pl.BlockSpec((LINE * share, block), lambda n, line: (0, n))
    return pl.pallas_call(
        join_kernel,
        grid_spec=pltpu.PrefetchScalarGridSpec(
            num_scalar_prefetch=1,
            grid=(depth // block,),
            in_specs=[pl.BlockSpec(memory_space=pltpu.SMEM)]
            + [pl.BlockSpec((1, tiles, half, share), lambda n, line: (0, 0, 0, 0))] * LINE
            + [pl.BlockSpec((tiles, half, share), lambda n, line: (0, 0, 0))] * LINE
            + [weight_spec, weight_spec, pl.BlockSpec((1, depth), lambda n, line: (0, 0))]
            + [pl.BlockSpec(memory_space=pl.ANY)] * 3,
            out_specs=[
                pl.BlockSpec((tiles, half, depth), lambda n, line: (0, 0, 0)),
                pl.BlockSpec((tiles, half, 128), lambda n, line: (0, 0, 0)),
            ],
            scratch_shapes=[
                pltpu.VMEM((2, tiles * half, LINE * share), jnp.bfloat16),
                pltpu.VMEM((tiles * half, depth), jnp.float32),
                pltpu.VMEM((3, tiles, half, depth), jnp.bfloat16),
                pltpu.SemaphoreType.DMA((3,)),
            ],
        ),
        out_shape=[
            jax.ShapeDtypeStruct((tiles, half, depth), jnp.bfloat16),
            jax.ShapeDtypeStruct((tiles, half, 128), jnp.float32),
        ],
        compiler_params=pltpu.CompilerParams(vmem_limit_bytes=VMEM_BYTES),
        cost_estimate=SMALL_COST,
        name="join",
    )(line_arg, mixing, *attended, *swapped, *weights, scale, *inputs)


def final_kernel(own_ref, other_ref, z_ref, inverse_ref, out_ref):
    grad = own_ref[0].astype(jnp.float32) + other_ref[0].astype(jnp.float32)
    normal = z_ref[0].astype(jnp.float32)
    mean = jnp.mean(grad, axis=-1, keepdims=True)
    along = jnp.mean(grad * normal, axis=-1, keepdims=True)
    out_ref[0] = ((grad - mean - normal * along) * inverse_ref[0, :, :1]).astype(jnp.bfloat16)


def final_rows(own, other, z_rows, inverse):
    tiles, half, depth = own.shape
    block = 64
    spec = pl.BlockSpec((1, block, depth), lambda t, r: (t, r, 0))
    return pl.pallas_call(
        final_kernel,
        grid=(tiles, half // block),
        out_shape=jax.ShapeDtypeStruct(own.shape, jnp.bfloat16),
        in_specs=[spec, spec, spec, pl.BlockSpec((1, block, 128), lambda t, r: (t, r, 0))],
        out_specs=spec,
        compiler_params=pltpu.CompilerParams(vmem_limit_bytes=VMEM_BYTES),
        cost_estimate=SMALL_COST,
        name="final",
    )(own, other, z_rows, inverse)


def activate(preact):
    raised = jnp.exp(-0.5 * preact * preact)
    step = 1.0 / (1.0 + 0.3275911 * inv_root_two * jnp.abs(preact))
    series = 1.061405429 * step - 1.453152027
    series = series * step + 1.421413741
    series = series * step - 0.284496736
    series = series * step + 0.254829592
    tail = 0.5 * series * step * raised
    return jnp.where(preact >= 0.0, 1.0 - tail, tail), raised * inv_root_tau


def project_kernel(core_ref, own_ref, other_ref, weight_ref, bias_ref, projected_ref, slope_ref):
    core = core_ref[0]
    tiles, half, depth = own_ref.shape
    block = weight_ref.shape[1]
    rows = jnp.concatenate(
        [own_ref[...].reshape(tiles * half, depth), other_ref[...].reshape(tiles * half, depth)], axis=0
    )
    preact = jnp.dot(rows, weight_ref[...], preferred_element_type=jnp.float32) + bias_ref[...]
    cumulative, density = activate(preact)
    projected = (preact * cumulative).astype(jnp.bfloat16).reshape(2, tiles, 1, half, block)
    projected_ref[:, pl.ds(core, 1)] = projected[0]
    projected_ref[:, pl.ds(1 - core, 1)] = projected[1]
    slope_ref[...] = cumulative + preact * density


def home_project(core, own, other, weight, bias):
    tiles, half, depth = own.shape
    width = weight.shape[1]
    block = 512
    whole = pl.BlockSpec((tiles, half, depth), lambda n, c: (0, 0, 0))
    projected, slope = pl.pallas_call(
        project_kernel,
        grid_spec=pltpu.PrefetchScalarGridSpec(
            num_scalar_prefetch=1,
            grid=(width // block,),
            in_specs=[
                whole,
                whole,
                pl.BlockSpec((depth, block), lambda n, c: (0, n)),
                pl.BlockSpec((1, block), lambda n, c: (0, n)),
            ],
            out_specs=[
                pl.BlockSpec((tiles, 2, half, block), lambda n, c: (0, 0, 0, n)),
                pl.BlockSpec((2 * tiles * half, block), lambda n, c: (0, n)),
            ],
        ),
        out_shape=[
            jax.ShapeDtypeStruct((tiles, 2, half, width), jnp.bfloat16),
            jax.ShapeDtypeStruct((2 * tiles * half, width), jnp.float32),
        ],
        compiler_params=pltpu.CompilerParams(vmem_limit_bytes=VMEM_BYTES),
        cost_estimate=SMALL_COST,
        name="project",
    )(core, own, other, weight, bias)
    return projected.reshape(tiles, 2 * half, width), slope


def grad_kernel(core_ref, slope_ref, back_own_ref, back_other_ref, weight_ref, own_ref, other_ref, total):
    step = pl.program_id(0)
    tiles, half, depth = own_ref.shape
    rows, block = slope_ref.shape
    back = jnp.concatenate(
        [ref[...].reshape(tiles * half, block) for ref in (back_own_ref, back_other_ref)], axis=0
    )
    slope_rows = (back.astype(jnp.float32) * slope_ref[...]).astype(jnp.bfloat16)
    term = lax.dot_general(
        slope_rows, weight_ref[...], (((1,), (1,)), ((), ())), preferred_element_type=jnp.float32
    )

    @pl.when(step == 0)
    def _():
        total[...] = term

    @pl.when(step > 0)
    def _():
        total[...] += term

    @pl.when(step == pl.num_programs(0) - 1)
    def _():
        own_ref[...] = total[: tiles * half].astype(jnp.bfloat16).reshape(tiles, half, depth)
        other_ref[...] = total[tiles * half :].astype(jnp.bfloat16).reshape(tiles, half, depth)


def home_grad(core, slope, back, weight):
    tiles, full, width = back.shape
    half = full // 2
    depth = weight.shape[0]
    block = 512
    back = back.reshape(tiles, 2, half, width)
    whole = pl.BlockSpec((tiles, half, depth), lambda n, c: (0, 0, 0))
    shape = jax.ShapeDtypeStruct((tiles, half, depth), jnp.bfloat16)
    return pl.pallas_call(
        grad_kernel,
        grid_spec=pltpu.PrefetchScalarGridSpec(
            num_scalar_prefetch=1,
            grid=(width // block,),
            in_specs=[
                pl.BlockSpec((tiles * full, block), lambda n, c: (0, n)),
                pl.BlockSpec((tiles, 1, half, block), lambda n, c: (0, c[0], 0, n)),
                pl.BlockSpec((tiles, 1, half, block), lambda n, c: (0, 1 - c[0], 0, n)),
                pl.BlockSpec((depth, block), lambda n, c: (0, n)),
            ],
            out_specs=[whole, whole],
            scratch_shapes=[pltpu.VMEM((tiles * full, depth), jnp.float32)],
        ),
        out_shape=[shape, shape],
        compiler_params=pltpu.CompilerParams(vmem_limit_bytes=VMEM_BYTES),
        cost_estimate=SMALL_COST,
        name="grad",
    )(core, slope, back, back, weight)


def owner_kernel(core_ref, own_ref, other_ref, weight_ref, bias_ref, projected_ref):
    core = core_ref[0]
    tiles, half, depth = own_ref.shape
    block = weight_ref.shape[1]
    rows = jnp.concatenate(
        [own_ref[...].reshape(tiles * half, depth), other_ref[...].reshape(tiles * half, depth)], axis=0
    )
    preact = jnp.dot(rows, weight_ref[...], preferred_element_type=jnp.float32) + bias_ref[...]
    projected = (preact * activate(preact)[0]).astype(jnp.bfloat16).reshape(2, tiles, 1, half, block)
    projected_ref[:, pl.ds(core, 1)] = projected[0]
    projected_ref[:, pl.ds(1 - core, 1)] = projected[1]


def owner_project(core, own, other, weight, bias):
    tiles, half, depth = own.shape
    width = weight.shape[1]
    block = 512
    whole = pl.BlockSpec((tiles, half, depth), lambda n, c: (0, 0, 0))
    projected = pl.pallas_call(
        owner_kernel,
        grid_spec=pltpu.PrefetchScalarGridSpec(
            num_scalar_prefetch=1,
            grid=(width // block,),
            in_specs=[
                whole,
                whole,
                pl.BlockSpec((depth, block), lambda n, c: (0, n)),
                pl.BlockSpec((1, block), lambda n, c: (0, n)),
            ],
            out_specs=pl.BlockSpec((tiles, 2, half, block), lambda n, c: (0, 0, 0, n)),
        ),
        out_shape=jax.ShapeDtypeStruct((tiles, 2, half, width), jnp.bfloat16),
        compiler_params=pltpu.CompilerParams(vmem_limit_bytes=VMEM_BYTES),
        cost_estimate=SMALL_COST,
        name="owner",
    )(core, own, other, weight, bias)
    return projected.reshape(tiles, 2 * half, width)


def place_kernel(first_slot, split, slots_ref, *refs):
    low_ref, high_ref, out_ref = refs[0], refs[1], refs[-1]
    slot = pl.program_id(0) + first_slot
    index = slot + slots_ref[0]
    rows = jnp.where(index < split, low_ref[...], high_ref[...])
    out_ref[...] = jnp.where(slot < slots_ref[1], rows, jnp.zeros_like(rows))


def place_tiles(slots, low, high, own_tiles, held):
    tiles, full, width = low.shape
    count = own_tiles // 2
    first_slot = 0 if held is None else count
    split = tiles if held is None else 2 * tiles

    def spec(start):
        def at(k, r, s):
            return (jnp.clip(k + first_slot + s[0] - start, 0, tiles - 1), r, 0)

        return pl.BlockSpec((1, full // 2, width), at)

    in_specs = [spec(split - tiles), spec(split)]
    operands = [low, high]
    aliases = {}
    if held is not None:
        in_specs.append(pl.BlockSpec(memory_space=pl.ANY))
        operands.append(held)
        aliases = {3: 0}
    return pl.pallas_call(
        functools.partial(place_kernel, first_slot, split),
        grid_spec=pltpu.PrefetchScalarGridSpec(
            num_scalar_prefetch=1,
            grid=(count, 2),
            in_specs=in_specs,
            out_specs=pl.BlockSpec((1, full // 2, width), lambda k, r, s: (k + first_slot, r, 0)),
        ),
        out_shape=jax.ShapeDtypeStruct((own_tiles, full, width), jnp.bfloat16),
        input_output_aliases=aliases,
        compiler_params=pltpu.CompilerParams(vmem_limit_bytes=VMEM_BYTES),
        cost_estimate=SMALL_COST,
        name="place",
    )(slots, *operands)


def on_device(
    tokens, tap_early, tap_mid, tile_counts, qkv_weight, out_weight, layer_scale, layer_logits,
    proj_weight, proj_bias, grad_out,
):
    tile_group, token_share, depth = tokens.shape
    img_count = lax.axis_size(IMG)
    place = lax.axis_index(IMG)
    line_place = lax.axis_index("z")
    core = lax.axis_index("head")
    core_arg = core.astype(jnp.int32).reshape(1)
    tile_total = tile_group * img_count
    own_tiles = grad_out.shape[0]
    owner_of, first_tile = tile_owners(tile_counts, tile_total, tile_group)
    my_first = first_tile[place]

    depth_share, width = qkv_weight.shape
    share = width // LINE
    received = []
    for distance in range(LINE):
        target = (line_place + distance) % LINE
        columns = lax.dynamic_slice_in_dim(qkv_weight, target * share, share, axis=1)
        received.append(along_z(columns, distance) if distance else columns)
    normed = norm_rows(tokens)
    normed, received = lax.optimization_barrier((normed, received))
    ladder = jnp.stack([received[(LINE - 1 - j) % LINE] for j in range(2 * LINE - 1)], axis=0)
    sent = lax.dynamic_slice_in_dim(ladder, LINE - 1 - line_place, LINE, axis=0)
    weight = lax.all_gather(sent.reshape(LINE * depth_share, share), ("y", "x"), axis=0, tiled=True)

    from_low = along_z(normed, 1)
    from_high = along_z(normed, -1)

    def packet(distance, within, count):
        tile = (place + distance) * tile_group + within
        slot = jnp.clip(tile - my_first, 0, own_tiles - count)
        return lax.dynamic_slice_in_dim(grad_out, slot, count, axis=0)

    packets = [packet(2, 0, tile_group), packet(1, 0, tile_group)]
    other_weight = swap(out_weight)
    from_low, from_high, packets, other_weight = lax.optimization_barrier(
        (from_low, from_high, packets, other_weight)
    )
    far_first = along_z(from_low[:1], 1)
    far_second = along_z(from_high[1:], -1)
    weight, packets = lax.optimization_barrier((weight, packets))
    far_back = along_img(packets[0], 2)

    far_others = [swap(far_first), swap(far_second)]
    att_far, att_low, att_high, att_own = attend(
        [([far_first, far_second], far_others)]
        + [([rows], [swap(rows)]) for rows in (from_low, from_high, normed)],
        weight,
    )
    attended = [att_own, along_z(att_low, -1), along_z(att_far, 2), along_z(att_high, 1)]
    attended[2], near_packet = lax.optimization_barrier((attended[2], packets[1]))
    near_back = along_img(near_packet, 1)
    swapped = [swap(rows[1]) for rows in attended]
    swapped, far_back = lax.optimization_barrier((swapped, far_back))
    raised_logits = jnp.exp(layer_logits)
    mixing = raised_logits / jnp.sum(raised_logits)
    z_rows, inverse_std = join_rows(
        line_place.astype(jnp.int32).reshape(1),
        mixing,
        attended,
        swapped,
        [out_weight, other_weight],
        layer_scale.reshape(1, -1),
        [tokens, tap_early, tap_mid],
    )

    near = along_img(z_rows, -1)
    bias = proj_bias.reshape(1, -1)
    projected, slope = home_project(core_arg, z_rows, swap(z_rows), proj_weight, bias)
    slope, near_back = lax.optimization_barrier((slope, near_back))

    back = []
    for within in range(tile_group):
        tile = place * tile_group + within
        owner = owner_of[tile]
        slot = jnp.clip(tile - my_first, 0, own_tiles - 1)
        here = lax.dynamic_index_in_dim(grad_out, slot, axis=0, keepdims=False)
        other = jnp.where(owner == place - 1, near_back[within], far_back[within])
        back.append(jnp.where(owner == place, here, other))
    back_rows = jnp.stack(back, axis=0)
    grad_own, grad_other = home_grad(core_arg, slope, back_rows, proj_weight)

    near, z_later, grad_other = lax.optimization_barrier((near, z_rows, grad_other))
    far = along_img(z_later, -2)
    near_projected = owner_project(core_arg, near, swap(near), proj_weight, bias)
    offset = my_first - place * tile_group
    held = first_tile[place + 1] - my_first
    slots = jnp.stack([offset, held]).astype(jnp.int32)
    owner_rows = place_tiles(slots, projected, near_projected, own_tiles, None)
    grad_joined = final_rows(grad_own, swap(grad_other), z_rows, inverse_std)
    far, grad_joined, owner_rows = lax.optimization_barrier((far, grad_joined, owner_rows))
    far_projected = owner_project(core_arg, far, swap(far), proj_weight, bias)
    owner_rows = place_tiles(slots, near_projected, far_projected, own_tiles, owner_rows)
    return (owner_rows, grad_joined)


def solution(mesh):
    cores = mesh.devices.shape[-1]
    inner = Mesh(mesh.devices.reshape(LINE, LINE, LINE, cores), IMG + ("head",))
    return jax.shard_map(
        on_device,
        mesh=inner,
        in_specs=(
            P(IMG, "head", None),
            P(IMG, "head", None),
            P(IMG, "head", None),
            P(),
            P(IMG, "head"),
            P("head", None),
            P(),
            P(),
            P(None, "head"),
            P("head"),
            P(IMG, None, "head"),
        ),
        out_specs=(P(IMG, None, "head"), P(IMG, "head", None)),
        check_vma=False,
    )
```

```python
import functools
import math

import jax
import jax.numpy as jnp
from jax import lax
from jax.experimental import pallas as pl
from jax.experimental.pallas import tpu as pltpu
from jax.sharding import Mesh, PartitionSpec as P

HEAD_DIM = 128
LINE = 4
IMG = ("z", "y", "x")
VMEM_BYTES = 56 * 1024 * 1024
SMALL_COST = pl.CostEstimate(flops=1, bytes_accessed=1, transcendentals=0)

inv_root_two = 0.7071067811865476
inv_root_tau = 0.3989422804014327


def swap(array):
    return lax.ppermute(array, "head", [(0, 1), (1, 0)])


def along_z(array, by):
    return lax.ppermute(array, "z", [(i, (i + by) % LINE) for i in range(LINE)])


def along_img(array, by):
    peers = lax.axis_size(IMG)
    pairs = [(i, i + by) for i in range(peers) if 0 <= i + by < peers]
    return lax.ppermute(array, IMG, pairs)


def tile_owners(tile_counts, tile_total, tile_group):
    starts = jnp.cumsum(tile_counts) - tile_counts
    tile_index = jnp.arange(tile_total, dtype=jnp.int32)
    start_of = jnp.max(
        jnp.where(starts[None, :] <= tile_index[:, None], starts[None, :], -1), axis=1
    )
    owner_of = start_of // tile_group
    owners_total = tile_total // tile_group
    edge_tiles = jnp.arange(owners_total + 1, dtype=jnp.int32) * tile_group
    first_tile = jnp.min(
        jnp.where(starts[None, :] >= edge_tiles[:, None], starts[None, :], tile_total), axis=1
    )
    return (owner_of, first_tile)


def norm_kernel(tokens_ref, out_ref, ordered):
    rows = tokens_ref[0].astype(jnp.float32)
    normed = rows * lax.rsqrt(jnp.mean(rows * rows, axis=-1, keepdims=True) + 1e-06)
    groups = LINE * LINE
    share = rows.shape[1] // (LINE * groups)
    for line in range(LINE):
        for group in range(groups):
            source = (line * groups + group) * share
            target = (group * LINE + line) * share
            ordered[:, target : target + share] = normed[:, source : source + share]
    out_ref[0] = ordered[...].astype(jnp.bfloat16)


def norm_rows(tokens):
    tiles, half, depth = tokens.shape
    block = 64
    spec = pl.BlockSpec((1, block, depth), lambda t, r: (t, r, 0))
    return pl.pallas_call(
        norm_kernel,
        grid=(tiles, half // block),
        out_shape=jax.ShapeDtypeStruct(tokens.shape, jnp.bfloat16),
        in_specs=[spec],
        out_specs=spec,
        scratch_shapes=[pltpu.VMEM((block, depth), jnp.float32)],
        compiler_params=pltpu.CompilerParams(vmem_limit_bytes=VMEM_BYTES),
        cost_estimate=SMALL_COST,
        name="norm",
    )(tokens)


def attend_kernel(layout, *refs):
    count = len(layout)
    pieces = sum(2 * len(tiles) for tiles in layout)
    sources, weight_hbm = list(refs[:pieces]), refs[pieces]
    outs = refs[pieces + 1 : pieces + 1 + count]
    rows, weight, qkv, row_sems, weight_sem = refs[pieces + 1 + count :]
    _, _, tiles, half, depth = rows.shape
    heads = weight.shape[1] // (3 * HEAD_DIM)

    def fetch(index):
        slot = index % 2
        copies = []
        for part in range(2):
            start = 0
            for place, length in enumerate(layout[index]):
                target = rows.at[slot, part, pl.ds(start, length)]
                copies.append(
                    pltpu.make_async_copy(sources.pop(0), target, row_sems.at[slot, part, place])
                )
                start += length
        return copies

    weight_copy = pltpu.make_async_copy(weight_hbm, weight, weight_sem)
    pending = fetch(0)
    for copy in pending:
        copy.start()
    weight_copy.start()
    for index in range(count):
        current = pending
        if index + 1 < count:
            pending = fetch(index + 1)
            for copy in pending:
                copy.start()
        for copy in current:
            copy.wait()
        if index == 0:
            weight_copy.wait()
        block = rows[index % 2].reshape(2 * tiles * half, depth)
        qkv[...] = jnp.dot(block, weight[...], preferred_element_type=jnp.float32).astype(jnp.bfloat16)
        for tile in range(tiles):
            for head in range(heads):

                def piece(kind):
                    start = (head * 3 + kind) * HEAD_DIM
                    columns = slice(start, start + HEAD_DIM)
                    low = qkv[tile * half : (tile + 1) * half, columns]
                    high = qkv[(tiles + tile) * half : (tiles + tile + 1) * half, columns]
                    return jnp.concatenate([low, high], axis=0)

                scores = lax.dot_general(
                    piece(0), piece(1), (((1,), (1,)), ((), ())), preferred_element_type=jnp.float32
                ) * (1.0 / math.sqrt(HEAD_DIM))
                scores = scores - jnp.max(scores, axis=-1, keepdims=True)
                raised = jnp.exp(scores)
                inverse = 1.0 / jnp.sum(raised, axis=-1, keepdims=True)
                soft = (raised * inverse).astype(jnp.bfloat16)
                mixed = jnp.dot(soft, piece(2), preferred_element_type=jnp.float32)
                columns = slice(head * HEAD_DIM, (head + 1) * HEAD_DIM)
                outs[index][:, tile, :, columns] = mixed.astype(jnp.bfloat16).reshape(2, half, HEAD_DIM)


def attend(sources, weight):
    layout = tuple(tuple(array.shape[0] for array in own) for own, _ in sources)
    tiles = sum(layout[0])
    _, half, depth = sources[0][0][0].shape
    width = weight.shape[1]
    shape = (2, tiles, half, width // 3)
    arrays = [array for own, other in sources for array in (*own, *other)]
    return pl.pallas_call(
        functools.partial(attend_kernel, layout),
        out_shape=[jax.ShapeDtypeStruct(shape, jnp.bfloat16)] * len(layout),
        in_specs=[pl.BlockSpec(memory_space=pl.ANY)] * (len(arrays) + 1),
        out_specs=[pl.BlockSpec(memory_space=pltpu.VMEM)] * len(layout),
        scratch_shapes=[
            pltpu.VMEM((2, 2, tiles, half, depth), jnp.bfloat16),
            pltpu.VMEM((depth, width), jnp.bfloat16),
            pltpu.VMEM((2 * tiles * half, width), jnp.bfloat16),
            pltpu.SemaphoreType.DMA((2, 2, tiles)),
            pltpu.SemaphoreType.DMA,
        ],
        compiler_params=pltpu.CompilerParams(vmem_limit_bytes=VMEM_BYTES),
        cost_estimate=SMALL_COST,
        name="attend",
    )(*arrays, weight)


def join_kernel(line_ref, mixing_ref, *refs):
    own, other = refs[:LINE], refs[LINE : 2 * LINE]
    own_weight_ref, other_weight_ref, scale_ref = refs[2 * LINE : 2 * LINE + 3]
    inputs_hbm = refs[2 * LINE + 3 : 2 * LINE + 6]
    z_ref, inverse_ref, rows, total, inputs, sems = refs[2 * LINE + 6 :]
    step = pl.program_id(0)
    _, tiles, half, share = own[0].shape
    block = own_weight_ref.shape[1]
    copies = [
        pltpu.make_async_copy(source, inputs.at[i], sems.at[i]) for i, source in enumerate(inputs_hbm)
    ]

    @pl.when(step == 0)
    def _():
        for copy in copies:
            copy.start()
        for distance in range(LINE):
            start = pl.multiple_of(lax.rem(line_ref[0] + distance, LINE) * share, share)
            rows[0, :, pl.ds(start, share)] = own[distance][0].reshape(tiles * half, share)
            rows[1, :, pl.ds(start, share)] = other[distance][...].reshape(tiles * half, share)

    part = jnp.dot(rows[0], own_weight_ref[...], preferred_element_type=jnp.float32)
    part += jnp.dot(rows[1], other_weight_ref[...], preferred_element_type=jnp.float32)
    total[:, pl.ds(pl.multiple_of(step * block, block), block)] = part

    @pl.when(step == pl.num_programs(0) - 1)
    def _():
        for copy in copies:
            copy.wait()
        chunk = 64
        scale = mixing_ref[3] * scale_ref[...]
        for tile in range(tiles):
            for start in range(0, half, chunk):
                span = slice(start, start + chunk)
                joined = (
                    (mixing_ref[2] + mixing_ref[3]) * inputs[0, tile, span].astype(jnp.float32)
                    + mixing_ref[0] * inputs[1, tile, span].astype(jnp.float32)
                    + mixing_ref[1] * inputs[2, tile, span].astype(jnp.float32)
                    + scale * total[tile * half + start : tile * half + start + chunk]
                )
                centre = jnp.mean(joined, axis=-1, keepdims=True)
                shifted = joined - centre
                inverse = lax.rsqrt(jnp.mean(shifted * shifted, axis=-1, keepdims=True) + 1e-05)
                z_ref[tile, span] = (shifted * inverse).astype(jnp.bfloat16)
                inverse_ref[tile, span] = jnp.broadcast_to(inverse, (chunk, 128))


def join_rows(line_arg, mixing, attended, swapped, weights, scale, inputs):
    _, tiles, half, share = attended[0].shape
    depth = weights[0].shape[1]
    block = 640
    weight_spec = pl.BlockSpec((LINE * share, block), lambda n, line: (0, n))
    return pl.pallas_call(
        join_kernel,
        grid_spec=pltpu.PrefetchScalarGridSpec(
            num_scalar_prefetch=1,
            grid=(depth // block,),
            in_specs=[pl.BlockSpec(memory_space=pltpu.SMEM)]
            + [pl.BlockSpec((1, tiles, half, share), lambda n, line: (0, 0, 0, 0))] * LINE
            + [pl.BlockSpec((tiles, half, share), lambda n, line: (0, 0, 0))] * LINE
            + [weight_spec, weight_spec, pl.BlockSpec((1, depth), lambda n, line: (0, 0))]
            + [pl.BlockSpec(memory_space=pl.ANY)] * 3,
            out_specs=[
                pl.BlockSpec((tiles, half, depth), lambda n, line: (0, 0, 0)),
                pl.BlockSpec((tiles, half, 128), lambda n, line: (0, 0, 0)),
            ],
            scratch_shapes=[
                pltpu.VMEM((2, tiles * half, LINE * share), jnp.bfloat16),
                pltpu.VMEM((tiles * half, depth), jnp.float32),
                pltpu.VMEM((3, tiles, half, depth), jnp.bfloat16),
                pltpu.SemaphoreType.DMA((3,)),
            ],
        ),
        out_shape=[
            jax.ShapeDtypeStruct((tiles, half, depth), jnp.bfloat16),
            jax.ShapeDtypeStruct((tiles, half, 128), jnp.float32),
        ],
        compiler_params=pltpu.CompilerParams(vmem_limit_bytes=VMEM_BYTES),
        cost_estimate=SMALL_COST,
        name="join",
    )(line_arg, mixing, *attended, *swapped, *weights, scale, *inputs)


def final_kernel(own_ref, other_ref, z_ref, inverse_ref, out_ref):
    grad = own_ref[0].astype(jnp.float32) + other_ref[0].astype(jnp.float32)
    normal = z_ref[0].astype(jnp.float32)
    mean = jnp.mean(grad, axis=-1, keepdims=True)
    along = jnp.mean(grad * normal, axis=-1, keepdims=True)
    out_ref[0] = ((grad - mean - normal * along) * inverse_ref[0, :, :1]).astype(jnp.bfloat16)


def final_rows(own, other, z_rows, inverse):
    tiles, half, depth = own.shape
    block = 64
    spec = pl.BlockSpec((1, block, depth), lambda t, r: (t, r, 0))
    return pl.pallas_call(
        final_kernel,
        grid=(tiles, half // block),
        out_shape=jax.ShapeDtypeStruct(own.shape, jnp.bfloat16),
        in_specs=[spec, spec, spec, pl.BlockSpec((1, block, 128), lambda t, r: (t, r, 0))],
        out_specs=spec,
        compiler_params=pltpu.CompilerParams(vmem_limit_bytes=VMEM_BYTES),
        cost_estimate=SMALL_COST,
        name="final",
    )(own, other, z_rows, inverse)


def activate(preact):
    raised = jnp.exp(-0.5 * preact * preact)
    step = 1.0 / (1.0 + 0.3275911 * inv_root_two * jnp.abs(preact))
    series = 1.061405429 * step - 1.453152027
    series = series * step + 1.421413741
    series = series * step - 0.284496736
    series = series * step + 0.254829592
    tail = 0.5 * series * step * raised
    return jnp.where(preact >= 0.0, 1.0 - tail, tail), raised * inv_root_tau


def project_kernel(core_ref, own_ref, other_ref, weight_ref, bias_ref, projected_ref, slope_ref):
    core = core_ref[0]
    tiles, half, depth = own_ref.shape
    block = weight_ref.shape[1]
    rows = jnp.concatenate(
        [own_ref[...].reshape(tiles * half, depth), other_ref[...].reshape(tiles * half, depth)], axis=0
    )
    preact = jnp.dot(rows, weight_ref[...], preferred_element_type=jnp.float32) + bias_ref[...]
    cumulative, density = activate(preact)
    projected = (preact * cumulative).astype(jnp.bfloat16).reshape(2, tiles, 1, half, block)
    projected_ref[:, pl.ds(core, 1)] = projected[0]
    projected_ref[:, pl.ds(1 - core, 1)] = projected[1]
    slope_ref[...] = cumulative + preact * density


def home_project(core, own, other, weight, bias):
    tiles, half, depth = own.shape
    width = weight.shape[1]
    block = 512
    whole = pl.BlockSpec((tiles, half, depth), lambda n, c: (0, 0, 0))
    projected, slope = pl.pallas_call(
        project_kernel,
        grid_spec=pltpu.PrefetchScalarGridSpec(
            num_scalar_prefetch=1,
            grid=(width // block,),
            in_specs=[
                whole,
                whole,
                pl.BlockSpec((depth, block), lambda n, c: (0, n)),
                pl.BlockSpec((1, block), lambda n, c: (0, n)),
            ],
            out_specs=[
                pl.BlockSpec((tiles, 2, half, block), lambda n, c: (0, 0, 0, n)),
                pl.BlockSpec((2 * tiles * half, block), lambda n, c: (0, n)),
            ],
        ),
        out_shape=[
            jax.ShapeDtypeStruct((tiles, 2, half, width), jnp.bfloat16),
            jax.ShapeDtypeStruct((2 * tiles * half, width), jnp.float32),
        ],
        compiler_params=pltpu.CompilerParams(vmem_limit_bytes=VMEM_BYTES),
        cost_estimate=SMALL_COST,
        name="project",
    )(core, own, other, weight, bias)
    return projected.reshape(tiles, 2 * half, width), slope


def grad_kernel(core_ref, slope_ref, back_own_ref, back_other_ref, weight_ref, own_ref, other_ref, total):
    step = pl.program_id(0)
    tiles, half, depth = own_ref.shape
    rows, block = slope_ref.shape
    back = jnp.concatenate(
        [ref[...].reshape(tiles * half, block) for ref in (back_own_ref, back_other_ref)], axis=0
    )
    slope_rows = (back.astype(jnp.float32) * slope_ref[...]).astype(jnp.bfloat16)
    term = lax.dot_general(
        slope_rows, weight_ref[...], (((1,), (1,)), ((), ())), preferred_element_type=jnp.float32
    )

    @pl.when(step == 0)
    def _():
        total[...] = term

    @pl.when(step > 0)
    def _():
        total[...] += term

    @pl.when(step == pl.num_programs(0) - 1)
    def _():
        own_ref[...] = total[: tiles * half].astype(jnp.bfloat16).reshape(tiles, half, depth)
        other_ref[...] = total[tiles * half :].astype(jnp.bfloat16).reshape(tiles, half, depth)


def home_grad(core, slope, back, weight):
    tiles, full, width = back.shape
    half = full // 2
    depth = weight.shape[0]
    block = 512
    back = back.reshape(tiles, 2, half, width)
    whole = pl.BlockSpec((tiles, half, depth), lambda n, c: (0, 0, 0))
    shape = jax.ShapeDtypeStruct((tiles, half, depth), jnp.bfloat16)
    return pl.pallas_call(
        grad_kernel,
        grid_spec=pltpu.PrefetchScalarGridSpec(
            num_scalar_prefetch=1,
            grid=(width // block,),
            in_specs=[
                pl.BlockSpec((tiles * full, block), lambda n, c: (0, n)),
                pl.BlockSpec((tiles, 1, half, block), lambda n, c: (0, c[0], 0, n)),
                pl.BlockSpec((tiles, 1, half, block), lambda n, c: (0, 1 - c[0], 0, n)),
                pl.BlockSpec((depth, block), lambda n, c: (0, n)),
            ],
            out_specs=[whole, whole],
            scratch_shapes=[pltpu.VMEM((tiles * full, depth), jnp.float32)],
        ),
        out_shape=[shape, shape],
        compiler_params=pltpu.CompilerParams(vmem_limit_bytes=VMEM_BYTES),
        cost_estimate=SMALL_COST,
        name="grad",
    )(core, slope, back, back, weight)


def owner_kernel(core_ref, own_ref, other_ref, weight_ref, bias_ref, projected_ref):
    core = core_ref[0]
    tiles, half, depth = own_ref.shape
    block = weight_ref.shape[1]
    rows = jnp.concatenate(
        [own_ref[...].reshape(tiles * half, depth), other_ref[...].reshape(tiles * half, depth)], axis=0
    )
    preact = jnp.dot(rows, weight_ref[...], preferred_element_type=jnp.float32) + bias_ref[...]
    projected = (preact * activate(preact)[0]).astype(jnp.bfloat16).reshape(2, tiles, 1, half, block)
    projected_ref[:, pl.ds(core, 1)] = projected[0]
    projected_ref[:, pl.ds(1 - core, 1)] = projected[1]


def owner_project(core, own, other, weight, bias):
    tiles, half, depth = own.shape
    width = weight.shape[1]
    block = 512
    whole = pl.BlockSpec((tiles, half, depth), lambda n, c: (0, 0, 0))
    projected = pl.pallas_call(
        owner_kernel,
        grid_spec=pltpu.PrefetchScalarGridSpec(
            num_scalar_prefetch=1,
            grid=(width // block,),
            in_specs=[
                whole,
                whole,
                pl.BlockSpec((depth, block), lambda n, c: (0, n)),
                pl.BlockSpec((1, block), lambda n, c: (0, n)),
            ],
            out_specs=pl.BlockSpec((tiles, 2, half, block), lambda n, c: (0, 0, 0, n)),
        ),
        out_shape=jax.ShapeDtypeStruct((tiles, 2, half, width), jnp.bfloat16),
        compiler_params=pltpu.CompilerParams(vmem_limit_bytes=VMEM_BYTES),
        cost_estimate=SMALL_COST,
        name="owner",
    )(core, own, other, weight, bias)
    return projected.reshape(tiles, 2 * half, width)


def place_kernel(slots_ref, home_ref, near_ref, out_ref):
    slot = pl.program_id(0)
    index = slot + slots_ref[0]
    tiles = 2
    live = jnp.logical_and(slot < slots_ref[1], index < 2 * tiles)

    @pl.when(jnp.logical_and(live, index < tiles))
    def _():
        out_ref[...] = home_ref[...]

    @pl.when(jnp.logical_and(live, index >= tiles))
    def _():
        out_ref[...] = near_ref[...]

    @pl.when(jnp.logical_not(live))
    def _():
        out_ref[...] = jnp.zeros_like(out_ref)


def place_tiles(slots, home, near, own_tiles):
    tiles, full, width = home.shape

    def spec(start):
        def at(k, s):
            return (jnp.clip(k + s[0] - start, 0, tiles - 1), 0, 0)

        return pl.BlockSpec((1, full, width), at)

    return pl.pallas_call(
        place_kernel,
        grid_spec=pltpu.PrefetchScalarGridSpec(
            num_scalar_prefetch=1,
            grid=(own_tiles,),
            in_specs=[spec(0), spec(tiles)],
            out_specs=pl.BlockSpec((1, full, width), lambda k, s: (k, 0, 0)),
        ),
        out_shape=jax.ShapeDtypeStruct((own_tiles, full, width), jnp.bfloat16),
        compiler_params=pltpu.CompilerParams(vmem_limit_bytes=VMEM_BYTES),
        cost_estimate=SMALL_COST,
        name="place",
    )(slots, home, near)


def owner_slots_kernel(slots_ref, own_ref, other_ref, weight_ref, bias_ref, held_ref, out_ref, projected):
    tile = pl.program_id(1)
    core = slots_ref[2]
    tiles, half, depth = own_ref.shape
    block = weight_ref.shape[1]

    @pl.when(tile == 0)
    def _():
        rows = jnp.concatenate(
            [own_ref[...].reshape(tiles * half, depth), other_ref[...].reshape(tiles * half, depth)],
            axis=0,
        )
        preact = jnp.dot(rows, weight_ref[...], preferred_element_type=jnp.float32) + bias_ref[...]
        values = (preact * activate(preact)[0]).astype(jnp.bfloat16).reshape(2, tiles, 1, half, block)
        projected[:, pl.ds(core, 1)] = values[0]
        projected[:, pl.ds(1 - core, 1)] = values[1]

    slot = 2 * tiles + tile - slots_ref[0]
    rows = projected[pl.ds(tile, 1)]
    out_ref[...] = jnp.where(slot < slots_ref[1], rows, jnp.zeros_like(rows))


def owner_slots(slots, own, other, weight, bias, held):
    tiles, half, depth = own.shape
    own_tiles, full, width = held.shape
    block = 512
    whole = pl.BlockSpec((tiles, half, depth), lambda n, t, s: (0, 0, 0))
    shape = (own_tiles, 2, half, width)
    out = pl.pallas_call(
        owner_slots_kernel,
        grid_spec=pltpu.PrefetchScalarGridSpec(
            num_scalar_prefetch=1,
            grid=(width // block, tiles),
            in_specs=[
                whole,
                whole,
                pl.BlockSpec((depth, block), lambda n, t, s: (0, n)),
                pl.BlockSpec((1, block), lambda n, t, s: (0, n)),
                pl.BlockSpec(memory_space=pl.ANY),
            ],
            out_specs=pl.BlockSpec(
                (1, 2, half, block), lambda n, t, s: (2 * tiles + t - s[0], 0, 0, n)
            ),
            scratch_shapes=[pltpu.VMEM((tiles, 2, half, block), jnp.bfloat16)],
        ),
        out_shape=jax.ShapeDtypeStruct(shape, jnp.bfloat16),
        input_output_aliases={5: 0},
        compiler_params=pltpu.CompilerParams(vmem_limit_bytes=VMEM_BYTES),
        cost_estimate=SMALL_COST,
        name="slots",
    )(slots, own, other, weight, bias, held.reshape(shape))
    return out.reshape(own_tiles, full, width)


def on_device(
    tokens, tap_early, tap_mid, tile_counts, qkv_weight, out_weight, layer_scale, layer_logits,
    proj_weight, proj_bias, grad_out,
):
    tile_group, token_share, depth = tokens.shape
    img_count = lax.axis_size(IMG)
    place = lax.axis_index(IMG)
    line_place = lax.axis_index("z")
    core = lax.axis_index("head")
    core_arg = core.astype(jnp.int32).reshape(1)
    tile_total = tile_group * img_count
    own_tiles = grad_out.shape[0]
    owner_of, first_tile = tile_owners(tile_counts, tile_total, tile_group)
    my_first = first_tile[place]

    depth_share, width = qkv_weight.shape
    share = width // LINE
    received = []
    for distance in range(LINE):
        target = (line_place + distance) % LINE
        columns = lax.dynamic_slice_in_dim(qkv_weight, target * share, share, axis=1)
        received.append(along_z(columns, distance) if distance else columns)
    normed = norm_rows(tokens)
    normed, received = lax.optimization_barrier((normed, received))
    ladder = jnp.stack([received[(LINE - 1 - j) % LINE] for j in range(2 * LINE - 1)], axis=0)
    sent = lax.dynamic_slice_in_dim(ladder, LINE - 1 - line_place, LINE, axis=0)
    weight = lax.all_gather(sent.reshape(LINE * depth_share, share), ("y", "x"), axis=0, tiled=True)

    from_low = along_z(normed, 1)
    from_high = along_z(normed, -1)

    def packet(distance, within, count):
        tile = (place + distance) * tile_group + within
        slot = jnp.clip(tile - my_first, 0, own_tiles - count)
        return lax.dynamic_slice_in_dim(grad_out, slot, count, axis=0)

    packets = [packet(2, 0, tile_group), packet(1, 0, tile_group)]
    other_weight = swap(out_weight)
    from_low, from_high, packets, other_weight = lax.optimization_barrier(
        (from_low, from_high, packets, other_weight)
    )
    far_first = along_z(from_low[:1], 1)
    far_second = along_z(from_high[1:], -1)
    weight, packets = lax.optimization_barrier((weight, packets))
    far_back = along_img(packets[0], 2)

    far_others = [swap(far_first), swap(far_second)]
    att_far, att_low, att_high, att_own = attend(
        [([far_first, far_second], far_others)]
        + [([rows], [swap(rows)]) for rows in (from_low, from_high, normed)],
        weight,
    )
    attended = [att_own, along_z(att_low, -1), along_z(att_far, 2), along_z(att_high, 1)]
    attended, near_packet = lax.optimization_barrier((attended, packets[1]))
    near_back = along_img(near_packet, 1)
    swapped = [swap(rows[1]) for rows in attended]
    swapped, far_back = lax.optimization_barrier((swapped, far_back))
    raised_logits = jnp.exp(layer_logits)
    mixing = raised_logits / jnp.sum(raised_logits)
    z_rows, inverse_std = join_rows(
        line_place.astype(jnp.int32).reshape(1),
        mixing,
        attended,
        swapped,
        [out_weight, other_weight],
        layer_scale.reshape(1, -1),
        [tokens, tap_early, tap_mid],
    )

    near = along_img(z_rows, -1)
    bias = proj_bias.reshape(1, -1)
    projected, slope = home_project(core_arg, z_rows, swap(z_rows), proj_weight, bias)
    slope, near_back = lax.optimization_barrier((slope, near_back))

    back = []
    for within in range(tile_group):
        tile = place * tile_group + within
        owner = owner_of[tile]
        slot = jnp.clip(tile - my_first, 0, own_tiles - 1)
        here = lax.dynamic_index_in_dim(grad_out, slot, axis=0, keepdims=False)
        other = jnp.where(owner == place - 1, near_back[within], far_back[within])
        back.append(jnp.where(owner == place, here, other))
    back_rows = jnp.stack(back, axis=0)
    grad_own, grad_other = home_grad(core_arg, slope, back_rows, proj_weight)

    near, z_later, grad_other = lax.optimization_barrier((near, z_rows, grad_other))
    far = along_img(z_later, -2)
    near_projected = owner_project(core_arg, near, swap(near), proj_weight, bias)
    offset = jnp.clip(my_first - place * tile_group, 0, 1)
    held = first_tile[place + 1] - my_first
    slots = jnp.stack([offset, held, core]).astype(jnp.int32)
    owner_rows = place_tiles(slots, projected, near_projected, own_tiles)
    grad_joined = final_rows(grad_own, swap(grad_other), z_rows, inverse_std)
    far, grad_joined, owner_rows = lax.optimization_barrier((far, grad_joined, owner_rows))
    owner_rows = owner_slots(slots, far, swap(far), proj_weight, bias, owner_rows)
    return (owner_rows, grad_joined)


def solution(mesh):
    cores = mesh.devices.shape[-1]
    inner = Mesh(mesh.devices.reshape(LINE, LINE, LINE, cores), IMG + ("head",))
    return jax.shard_map(
        on_device,
        mesh=inner,
        in_specs=(
            P(IMG, "head", None),
            P(IMG, "head", None),
            P(IMG, "head", None),
            P(),
            P(IMG, "head"),
            P("head", None),
            P(),
            P(),
            P(None, "head"),
            P("head"),
            P(IMG, None, "head"),
        ),
        out_specs=(P(IMG, None, "head"), P(IMG, "head", None)),
        check_vma=False,
    )
```

```python
import functools
import math

import jax
import jax.numpy as jnp
from jax import lax
from jax.experimental import pallas as pl
from jax.experimental.pallas import tpu as pltpu
from jax.sharding import Mesh, PartitionSpec as P

HEAD_DIM = 128
LINE = 4
IMG = ("z", "y", "x")
VMEM_BYTES = 56 * 1024 * 1024
SMALL_COST = pl.CostEstimate(flops=1, bytes_accessed=1, transcendentals=0)

inv_root_two = 0.7071067811865476
inv_root_tau = 0.3989422804014327


def swap(array):
    return lax.ppermute(array, "head", [(0, 1), (1, 0)])


def along_z(array, by):
    return lax.ppermute(array, "z", [(i, (i + by) % LINE) for i in range(LINE)])


def along_img(array, by):
    peers = lax.axis_size(IMG)
    pairs = [(i, i + by) for i in range(peers) if 0 <= i + by < peers]
    return lax.ppermute(array, IMG, pairs)


def around(place, side):
    return place - place % LINE + (place % LINE + side) % LINE


def two_on(array, by):
    peers = lax.axis_size(IMG)
    side = -by // 2
    turning = 2 if by > 0 else 1

    def middle(i):
        return i + side + LINE * (by // 2) if i % LINE == turning else around(i, side)

    ends = [(i, i + by) for i in range(peers) if 0 <= i + by < peers]
    halfway = lax.ppermute(array, IMG, [(i, middle(i)) for i, _ in ends])
    return halfway, lambda held: lax.ppermute(held, IMG, [(middle(i), j) for i, j in ends])


def tile_owners(tile_counts, tile_total, tile_group):
    starts = jnp.cumsum(tile_counts) - tile_counts
    tile_index = jnp.arange(tile_total, dtype=jnp.int32)
    start_of = jnp.max(
        jnp.where(starts[None, :] <= tile_index[:, None], starts[None, :], -1), axis=1
    )
    owner_of = start_of // tile_group
    owners_total = tile_total // tile_group
    edge_tiles = jnp.arange(owners_total + 1, dtype=jnp.int32) * tile_group
    first_tile = jnp.min(
        jnp.where(starts[None, :] >= edge_tiles[:, None], starts[None, :], tile_total), axis=1
    )
    return (owner_of, first_tile)


def norm_kernel(tokens_ref, out_ref, ordered):
    rows = tokens_ref[0].astype(jnp.float32)
    normed = rows * lax.rsqrt(jnp.mean(rows * rows, axis=-1, keepdims=True) + 1e-06)
    groups = LINE * LINE
    share = rows.shape[1] // (LINE * groups)
    for line in range(LINE):
        for group in range(groups):
            source = (line * groups + group) * share
            target = (group * LINE + line) * share
            ordered[:, target : target + share] = normed[:, source : source + share]
    out_ref[0] = ordered[...].astype(jnp.bfloat16)


def norm_rows(tokens):
    tiles, half, depth = tokens.shape
    block = 64
    spec = pl.BlockSpec((1, block, depth), lambda t, r: (t, r, 0))
    return pl.pallas_call(
        norm_kernel,
        grid=(tiles, half // block),
        out_shape=jax.ShapeDtypeStruct(tokens.shape, jnp.bfloat16),
        in_specs=[spec],
        out_specs=spec,
        scratch_shapes=[pltpu.VMEM((block, depth), jnp.float32)],
        compiler_params=pltpu.CompilerParams(vmem_limit_bytes=VMEM_BYTES),
        cost_estimate=SMALL_COST,
        name="norm",
    )(tokens)


def attend_kernel(layout, *refs):
    count = len(layout)
    pieces = sum(2 * len(tiles) for tiles in layout)
    sources, weight_hbm = list(refs[:pieces]), refs[pieces]
    outs = refs[pieces + 1 : pieces + 1 + count]
    rows, weight, qkv, row_sems, weight_sem = refs[pieces + 1 + count :]
    _, _, tiles, half, depth = rows.shape
    heads = weight.shape[1] // (3 * HEAD_DIM)

    def fetch(index):
        slot = index % 2
        copies = []
        for part in range(2):
            start = 0
            for place, length in enumerate(layout[index]):
                target = rows.at[slot, part, pl.ds(start, length)]
                copies.append(
                    pltpu.make_async_copy(sources.pop(0), target, row_sems.at[slot, part, place])
                )
                start += length
        return copies

    weight_copy = pltpu.make_async_copy(weight_hbm, weight, weight_sem)
    pending = fetch(0)
    for copy in pending:
        copy.start()
    weight_copy.start()
    for index in range(count):
        current = pending
        if index + 1 < count:
            pending = fetch(index + 1)
            for copy in pending:
                copy.start()
        for copy in current:
            copy.wait()
        if index == 0:
            weight_copy.wait()
        block = rows[index % 2].reshape(2 * tiles * half, depth)
        qkv[...] = jnp.dot(block, weight[...], preferred_element_type=jnp.float32).astype(jnp.bfloat16)
        for tile in range(tiles):
            for head in range(heads):

                def piece(kind):
                    start = (head * 3 + kind) * HEAD_DIM
                    columns = slice(start, start + HEAD_DIM)
                    low = qkv[tile * half : (tile + 1) * half, columns]
                    high = qkv[(tiles + tile) * half : (tiles + tile + 1) * half, columns]
                    return jnp.concatenate([low, high], axis=0)

                scores = lax.dot_general(
                    piece(0), piece(1), (((1,), (1,)), ((), ())), preferred_element_type=jnp.float32
                ) * (1.0 / math.sqrt(HEAD_DIM))
                scores = scores - jnp.max(scores, axis=-1, keepdims=True)
                raised = jnp.exp(scores)
                inverse = 1.0 / jnp.sum(raised, axis=-1, keepdims=True)
                soft = (raised * inverse).astype(jnp.bfloat16)
                mixed = jnp.dot(soft, piece(2), preferred_element_type=jnp.float32)
                outs[index][tile, :, head * HEAD_DIM : (head + 1) * HEAD_DIM] = mixed.astype(jnp.bfloat16)


def attend(sources, weight):
    layout = tuple(tuple(array.shape[0] for array in own) for own, _ in sources)
    tiles = sum(layout[0])
    _, half, depth = sources[0][0][0].shape
    width = weight.shape[1]
    shape = (tiles, 2 * half, width // 3)
    arrays = [array for own, other in sources for array in (*own, *other)]
    return pl.pallas_call(
        functools.partial(attend_kernel, layout),
        out_shape=[jax.ShapeDtypeStruct(shape, jnp.bfloat16)] * len(layout),
        in_specs=[pl.BlockSpec(memory_space=pl.ANY)] * (len(arrays) + 1),
        out_specs=[pl.BlockSpec(memory_space=pltpu.VMEM)] * len(layout),
        scratch_shapes=[
            pltpu.VMEM((2, 2, tiles, half, depth), jnp.bfloat16),
            pltpu.VMEM((depth, width), jnp.bfloat16),
            pltpu.VMEM((2 * tiles * half, width), jnp.bfloat16),
            pltpu.SemaphoreType.DMA((2, 2, tiles)),
            pltpu.SemaphoreType.DMA,
        ],
        compiler_params=pltpu.CompilerParams(vmem_limit_bytes=VMEM_BYTES),
        cost_estimate=SMALL_COST,
        name="attend",
    )(*arrays, weight)


def out_kernel(line_ref, *refs):
    attended, weight_ref, part_ref, rows = refs[:LINE], refs[LINE], refs[LINE + 1], refs[LINE + 2]
    tiles, half, block = part_ref.shape
    share = attended[0].shape[2]

    @pl.when(pl.program_id(0) == 0)
    def _():
        for distance, source in enumerate(attended):
            start = pl.multiple_of(lax.rem(line_ref[0] + distance, LINE) * share, share)
            rows[:, pl.ds(start, share)] = source[...].reshape(tiles * half, share)

    total = jnp.dot(rows[...], weight_ref[...], preferred_element_type=jnp.float32)
    part_ref[...] = total.astype(jnp.bfloat16).reshape(tiles, half, block)


def out_project(line_arg, attended, out_weight, part):
    tiles, full, share = attended[0].shape
    half = full // 2
    depth = out_weight.shape[1]
    block = 640
    return pl.pallas_call(
        out_kernel,
        grid_spec=pltpu.PrefetchScalarGridSpec(
            num_scalar_prefetch=1,
            grid=(depth // block,),
            in_specs=[pl.BlockSpec((tiles, half, share), lambda n, line: (0, part, 0))] * LINE
            + [pl.BlockSpec((LINE * share, block), lambda n, line: (0, n))],
            out_specs=pl.BlockSpec((tiles, half, block), lambda n, line: (0, 0, n)),
            scratch_shapes=[pltpu.VMEM((tiles * half, LINE * share), jnp.bfloat16)],
        ),
        out_shape=jax.ShapeDtypeStruct((tiles, half, depth), jnp.bfloat16),
        compiler_params=pltpu.CompilerParams(vmem_limit_bytes=VMEM_BYTES),
        cost_estimate=SMALL_COST,
        name="out",
    )(line_arg, *attended, out_weight)


def join_kernel(
    mixing_ref, tokens_ref, early_ref, mid_ref, own_ref, other_ref, scale_ref, z_ref, inverse_ref
):
    inputs = tokens_ref[0].astype(jnp.float32)
    attended_out = own_ref[0].astype(jnp.float32) + other_ref[0].astype(jnp.float32)
    joined = (
        mixing_ref[0] * early_ref[0].astype(jnp.float32)
        + mixing_ref[1] * mid_ref[0].astype(jnp.float32)
        + (mixing_ref[2] + mixing_ref[3]) * inputs
        + (mixing_ref[3] * scale_ref[...]) * attended_out
    )
    centre = jnp.mean(joined, axis=-1, keepdims=True)
    shifted = joined - centre
    inverse = lax.rsqrt(jnp.mean(shifted * shifted, axis=-1, keepdims=True) + 1e-05)
    z_ref[0] = (shifted * inverse).astype(jnp.bfloat16)
    inverse_ref[0] = jnp.broadcast_to(inverse, inverse_ref.shape[1:])


def join_rows(tile, mixing, tokens, early, mid, own, other, scale):
    _, half, depth = tokens.shape
    block = 64
    spec = pl.BlockSpec((1, block, depth), lambda r: (tile, r, 0))
    return pl.pallas_call(
        join_kernel,
        grid=(half // block,),
        out_shape=[
            jax.ShapeDtypeStruct((1, half, depth), jnp.bfloat16),
            jax.ShapeDtypeStruct((1, half, 128), jnp.float32),
        ],
        in_specs=[pl.BlockSpec(memory_space=pltpu.SMEM)]
        + [spec] * 5
        + [pl.BlockSpec((1, depth), lambda r: (0, 0))],
        out_specs=[
            pl.BlockSpec((1, block, depth), lambda r: (0, r, 0)),
            pl.BlockSpec((1, block, 128), lambda r: (0, r, 0)),
        ],
        compiler_params=pltpu.CompilerParams(vmem_limit_bytes=VMEM_BYTES),
        cost_estimate=SMALL_COST,
        name="join",
    )(mixing, tokens, early, mid, own, other, scale)


def final_kernel(own_ref, other_ref, z_ref, later_z_ref, inverse_ref, later_inverse_ref, out_ref):
    first = pl.program_id(0) == 0
    grad = own_ref[0].astype(jnp.float32) + other_ref[0].astype(jnp.float32)
    normal = jnp.where(first, z_ref[0], later_z_ref[0]).astype(jnp.float32)
    inverse = jnp.where(first, inverse_ref[0, :, :1], later_inverse_ref[0, :, :1])
    mean = jnp.mean(grad, axis=-1, keepdims=True)
    along = jnp.mean(grad * normal, axis=-1, keepdims=True)
    out_ref[0] = ((grad - mean - normal * along) * inverse).astype(jnp.bfloat16)


def final_rows(own, other, z_tiles, inverse_tiles):
    tiles, half, depth = own.shape
    block = 64
    spec = pl.BlockSpec((1, block, depth), lambda t, r: (t, r, 0))
    z_spec = pl.BlockSpec((1, block, depth), lambda t, r: (0, r, 0))
    inverse_spec = pl.BlockSpec((1, block, 128), lambda t, r: (0, r, 0))
    return pl.pallas_call(
        final_kernel,
        grid=(tiles, half // block),
        out_shape=jax.ShapeDtypeStruct(own.shape, jnp.bfloat16),
        in_specs=[spec, spec, z_spec, z_spec, inverse_spec, inverse_spec],
        out_specs=spec,
        compiler_params=pltpu.CompilerParams(vmem_limit_bytes=VMEM_BYTES),
        cost_estimate=SMALL_COST,
        name="final",
    )(own, other, *z_tiles, *inverse_tiles)


def activate(preact):
    raised = jnp.exp(-0.5 * preact * preact)
    step = 1.0 / (1.0 + 0.3275911 * inv_root_two * jnp.abs(preact))
    series = 1.061405429 * step - 1.453152027
    series = series * step + 1.421413741
    series = series * step - 0.284496736
    series = series * step + 0.254829592
    tail = 0.5 * series * step * raised
    return jnp.where(preact >= 0.0, 1.0 - tail, tail), raised * inv_root_tau


def project_kernel(core_ref, *refs):
    sources = refs[:-4]
    weight_ref, bias_ref, projected_ref, slope_ref = refs[-4:]
    core = core_ref[0]
    tiles, _, half, block = projected_ref.shape
    rows = jnp.concatenate([source[0] for source in sources], axis=0)
    preact = jnp.dot(rows, weight_ref[...], preferred_element_type=jnp.float32) + bias_ref[...]
    cumulative, density = activate(preact)
    projected = (preact * cumulative).astype(jnp.bfloat16).reshape(2, tiles, 1, half, block)
    projected_ref[:, pl.ds(core, 1)] = projected[0]
    projected_ref[:, pl.ds(1 - core, 1)] = projected[1]
    slope_ref[...] = cumulative + preact * density


def home_project(core, own, other, weight, bias):
    tiles = len(own)
    _, half, depth = own[0].shape
    width = weight.shape[1]
    block = 512
    projected, slope = pl.pallas_call(
        project_kernel,
        grid_spec=pltpu.PrefetchScalarGridSpec(
            num_scalar_prefetch=1,
            grid=(width // block,),
            in_specs=[pl.BlockSpec((1, half, depth), lambda n, c: (0, 0, 0))] * (2 * tiles)
            + [
                pl.BlockSpec((depth, block), lambda n, c: (0, n)),
                pl.BlockSpec((1, block), lambda n, c: (0, n)),
            ],
            out_specs=[
                pl.BlockSpec((tiles, 2, half, block), lambda n, c: (0, 0, 0, n)),
                pl.BlockSpec((2 * tiles * half, block), lambda n, c: (0, n)),
            ],
        ),
        out_shape=[
            jax.ShapeDtypeStruct((tiles, 2, half, width), jnp.bfloat16),
            jax.ShapeDtypeStruct((2 * tiles * half, width), jnp.float32),
        ],
        compiler_params=pltpu.CompilerParams(vmem_limit_bytes=VMEM_BYTES),
        cost_estimate=SMALL_COST,
        name="project",
    )(core, *own, *other, weight, bias)
    return projected.reshape(tiles, 2 * half, width), slope


def grad_kernel(core_ref, slope_ref, back_own_ref, back_other_ref, weight_ref, own_ref, other_ref, total):
    step = pl.program_id(0)
    tiles, half, depth = own_ref.shape
    rows, block = slope_ref.shape
    back = jnp.concatenate(
        [ref[...].reshape(tiles * half, block) for ref in (back_own_ref, back_other_ref)], axis=0
    )
    slope_rows = (back.astype(jnp.float32) * slope_ref[...]).astype(jnp.bfloat16)
    term = lax.dot_general(
        slope_rows, weight_ref[...], (((1,), (1,)), ((), ())), preferred_element_type=jnp.float32
    )

    @pl.when(step == 0)
    def _():
        total[...] = term

    @pl.when(step > 0)
    def _():
        total[...] += term

    @pl.when(step == pl.num_programs(0) - 1)
    def _():
        own_ref[...] = total[: tiles * half].astype(jnp.bfloat16).reshape(tiles, half, depth)
        other_ref[...] = total[tiles * half :].astype(jnp.bfloat16).reshape(tiles, half, depth)


def home_grad(core, slope, back, weight):
    tiles, full, width = back.shape
    half = full // 2
    depth = weight.shape[0]
    block = 512
    back = back.reshape(tiles, 2, half, width)
    whole = pl.BlockSpec((tiles, half, depth), lambda n, c: (0, 0, 0))
    shape = jax.ShapeDtypeStruct((tiles, half, depth), jnp.bfloat16)
    return pl.pallas_call(
        grad_kernel,
        grid_spec=pltpu.PrefetchScalarGridSpec(
            num_scalar_prefetch=1,
            grid=(width // block,),
            in_specs=[
                pl.BlockSpec((tiles * full, block), lambda n, c: (0, n)),
                pl.BlockSpec((tiles, 1, half, block), lambda n, c: (0, c[0], 0, n)),
                pl.BlockSpec((tiles, 1, half, block), lambda n, c: (0, 1 - c[0], 0, n)),
                pl.BlockSpec((depth, block), lambda n, c: (0, n)),
            ],
            out_specs=[whole, whole],
            scratch_shapes=[pltpu.VMEM((tiles * full, depth), jnp.float32)],
        ),
        out_shape=[shape, shape],
        compiler_params=pltpu.CompilerParams(vmem_limit_bytes=VMEM_BYTES),
        cost_estimate=SMALL_COST,
        name="grad",
    )(core, slope, back, back, weight)


def owner_kernel(count, core_ref, *refs):
    sources = refs[: 2 * count]
    weight_ref, bias_ref, projected_ref = refs[2 * count :]
    core = core_ref[0]
    _, half, depth = sources[0].shape
    block = weight_ref.shape[1]
    rows = jnp.concatenate([source[0] for source in sources], axis=0)
    preact = jnp.dot(rows, weight_ref[...], preferred_element_type=jnp.float32) + bias_ref[...]
    projected = (preact * activate(preact)[0]).astype(jnp.bfloat16)
    projected = projected.reshape(count, 2, half, block)
    for index in range(count):
        projected_ref[index, pl.ds(core, 1)] = projected[index, :1]
        projected_ref[index, pl.ds(1 - core, 1)] = projected[index, 1:]


def owner_project(core, pairs, weight, bias):
    count = len(pairs)
    _, half, depth = pairs[0][0].shape
    width = weight.shape[1]
    block = 512
    projected = pl.pallas_call(
        functools.partial(owner_kernel, count),
        grid_spec=pltpu.PrefetchScalarGridSpec(
            num_scalar_prefetch=1,
            grid=(width // block,),
            in_specs=[pl.BlockSpec((1, half, depth), lambda n, c: (0, 0, 0))] * (2 * count)
            + [
                pl.BlockSpec((depth, block), lambda n, c: (0, n)),
                pl.BlockSpec((1, block), lambda n, c: (0, n)),
            ],
            out_specs=pl.BlockSpec((count, 2, half, block), lambda n, c: (0, 0, 0, n)),
        ),
        out_shape=jax.ShapeDtypeStruct((count, 2, half, width), jnp.bfloat16),
        compiler_params=pltpu.CompilerParams(vmem_limit_bytes=VMEM_BYTES),
        cost_estimate=SMALL_COST,
        name="owner",
    )(core, *[rows for pair in pairs for rows in pair], weight, bias)
    return projected.reshape(count, 2 * half, width)


def on_device(
    tokens, tap_early, tap_mid, tile_counts, qkv_weight, out_weight, layer_scale, layer_logits,
    proj_weight, proj_bias, grad_out,
):
    tile_group, token_share, depth = tokens.shape
    img_count = lax.axis_size(IMG)
    place = lax.axis_index(IMG)
    line_place = lax.axis_index("z")
    core = lax.axis_index("head")
    core_arg = core.astype(jnp.int32).reshape(1)
    tile_total = tile_group * img_count
    own_tiles = grad_out.shape[0]
    owner_of, first_tile = tile_owners(tile_counts, tile_total, tile_group)
    my_first = first_tile[place]

    depth_share, width = qkv_weight.shape
    share = width // LINE
    received = []
    for distance in range(LINE):
        target = (line_place + distance) % LINE
        columns = lax.dynamic_slice_in_dim(qkv_weight, target * share, share, axis=1)
        received.append(along_z(columns, distance) if distance else columns)
    normed = norm_rows(tokens)
    normed, received = lax.optimization_barrier((normed, received))
    ladder = jnp.stack([received[(LINE - 1 - j) % LINE] for j in range(2 * LINE - 1)], axis=0)
    sent = lax.dynamic_slice_in_dim(ladder, LINE - 1 - line_place, LINE, axis=0)
    weight = lax.all_gather(sent.reshape(LINE * depth_share, share), ("y", "x"), axis=0, tiled=True)

    def packet(distance, within, count, first):
        tile = (place + distance) * tile_group + within
        slot = jnp.clip(tile - first, 0, own_tiles - count)
        return lax.dynamic_slice_in_dim(grad_out, slot, count, axis=0)

    from_low = along_z(normed, 1)
    from_high = along_z(normed, -1)

    def packet(distance, within, count):
        tile = (place + distance) * tile_group + within
        slot = jnp.clip(tile - my_first, 0, own_tiles - count)
        return lax.dynamic_slice_in_dim(grad_out, slot, count, axis=0)

    packets = [packet(distance, within, 1) for distance in (1, 2) for within in range(tile_group)]
    from_low, from_high, packets = lax.optimization_barrier((from_low, from_high, packets))
    far_first = along_z(from_low[:1], 1)
    far_second = along_z(from_high[1:], -1)
    weight, packets = lax.optimization_barrier((weight, packets))
    halfway, far_on = two_on(packets[3], 2)
    far_back = [along_img(packets[2], 2), None]
    near_back = [along_img(packets[0], 1), along_img(packets[1], 1)]

    far_others = [swap(far_first), swap(far_second)]
    att_far, att_low, att_high = attend(
        [([far_first, far_second], far_others)]
        + [([rows], [swap(rows)]) for rows in (from_low, from_high)],
        weight,
    )
    (att_own,) = attend([([normed], [swap(normed)])], weight)
    att_far, att_low, att_high = along_z(att_far, 2), along_z(att_low, -1), along_z(att_high, 1)
    att_own, halfway, near_back[0] = lax.optimization_barrier((att_own, halfway, near_back[0]))
    far_back[1] = far_on(halfway)
    attended = [att_own, att_low, att_far, att_high]
    line_arg = line_place.astype(jnp.int32).reshape(1)
    part_other = swap(out_project(line_arg, attended, out_weight, 1))
    part_own = out_project(line_arg, attended, out_weight, 0)
    raised_logits = jnp.exp(layer_logits)
    mixing = raised_logits / jnp.sum(raised_logits)
    scale = layer_scale.reshape(1, -1)
    joined = [
        join_rows(tile, mixing, tokens, tap_early, tap_mid, part_own, part_other, scale)
        for tile in range(tile_group)
    ]
    z_tiles = [z_rows for z_rows, _ in joined]
    inverse_tiles = [inverse for _, inverse in joined]

    near_first = along_img(z_tiles[0], -1)
    far_first = along_img(z_tiles[0], -2)
    halfway, far_on = two_on(z_tiles[1], -2)
    bias = proj_bias.reshape(1, -1)
    projected, slope = home_project(
        core_arg, z_tiles, [swap(z_rows) for z_rows in z_tiles], proj_weight, bias
    )
    slope, near_back[1], far_back[1] = lax.optimization_barrier((slope, near_back[1], far_back[1]))

    back = []
    for within in range(tile_group):
        tile = place * tile_group + within
        owner = owner_of[tile]
        slot = jnp.clip(tile - my_first, 0, own_tiles - 1)
        here = lax.dynamic_index_in_dim(grad_out, slot, axis=0, keepdims=False)
        near, far = near_back[within][0], far_back[within][0]
        back.append(jnp.where(owner == place, here, jnp.where(owner == place - 1, near, far)))
    back_rows = jnp.stack(back, axis=0)
    grad_own, grad_other = home_grad(core_arg, slope, back_rows, proj_weight)

    near_first, far_first, halfway, second, grad_other = lax.optimization_barrier(
        (near_first, far_first, halfway, z_tiles[1], grad_other)
    )
    near_second = along_img(second, -1)
    far_second = far_on(halfway)

    def guests(first, second):
        return owner_project(
            core_arg, [(first, swap(first)), (second, swap(second))], proj_weight, bias
        )

    early = guests(near_first, far_first)
    grad_joined = final_rows(grad_own, swap(grad_other), z_tiles, inverse_tiles)
    near_second, far_second, early, grad_joined = lax.optimization_barrier(
        (near_second, far_second, early, grad_joined)
    )
    late = guests(near_second, far_second)

    offset = my_first - place * tile_group
    held = first_tile[place + 1] - my_first
    at_hand = [projected[0], projected[1], early[0], late[0], early[1], late[1]]
    slots = []
    for slot in range(own_tiles):
        later = at_hand[min(slot + 1, len(at_hand) - 1)]
        picked = jnp.where(offset == 0, at_hand[slot], later)
        slots.append(jnp.where(slot < held, picked, jnp.zeros((), jnp.bfloat16)))
    owner_rows = jnp.stack(slots, axis=0)
    return (owner_rows, grad_joined)


def solution(mesh):
    cores = mesh.devices.shape[-1]
    inner = Mesh(mesh.devices.reshape(LINE, LINE, LINE, cores), IMG + ("head",))
    return jax.shard_map(
        on_device,
        mesh=inner,
        in_specs=(
            P(IMG, "head", None),
            P(IMG, "head", None),
            P(IMG, "head", None),
            P(),
            P(IMG, "head"),
            P("head", None),
            P(),
            P(),
            P(None, "head"),
            P("head"),
            P(IMG, None, "head"),
        ),
        out_specs=(P(IMG, None, "head"), P(IMG, "head", None)),
        check_vma=False,
    )
```

```python
import functools
import math

import jax
import jax.numpy as jnp
from jax import lax
from jax.experimental import pallas as pl
from jax.experimental.pallas import tpu as pltpu
from jax.sharding import Mesh, PartitionSpec as P

HEAD_DIM = 128
LINE = 4
IMG = ("z", "y", "x")
VMEM_BYTES = 56 * 1024 * 1024
SMALL_COST = pl.CostEstimate(flops=1, bytes_accessed=1, transcendentals=0)

inv_root_two = 0.7071067811865476
inv_root_tau = 0.3989422804014327


def swap(array):
    return lax.ppermute(array, "head", [(0, 1), (1, 0)])


def along_z(array, by):
    return lax.ppermute(array, "z", [(i, (i + by) % LINE) for i in range(LINE)])


def along_img(array, by):
    peers = lax.axis_size(IMG)
    pairs = [(i, i + by) for i in range(peers) if 0 <= i + by < peers]
    return lax.ppermute(array, IMG, pairs)


def around(place, side):
    return place - place % LINE + (place % LINE + side) % LINE


def two_on(array, by):
    peers = lax.axis_size(IMG)
    side = -by // 2
    turning = 2 if by > 0 else 1

    def middle(i):
        return i + side + LINE * (by // 2) if i % LINE == turning else around(i, side)

    ends = [(i, i + by) for i in range(peers) if 0 <= i + by < peers]
    halfway = lax.ppermute(array, IMG, [(i, middle(i)) for i, _ in ends])
    return halfway, lambda held: lax.ppermute(held, IMG, [(middle(i), j) for i, j in ends])


def tile_owners(tile_counts, tile_total, tile_group):
    starts = jnp.cumsum(tile_counts) - tile_counts
    tile_index = jnp.arange(tile_total, dtype=jnp.int32)
    start_of = jnp.max(
        jnp.where(starts[None, :] <= tile_index[:, None], starts[None, :], -1), axis=1
    )
    owner_of = start_of // tile_group
    owners_total = tile_total // tile_group
    edge_tiles = jnp.arange(owners_total + 1, dtype=jnp.int32) * tile_group
    first_tile = jnp.min(
        jnp.where(starts[None, :] >= edge_tiles[:, None], starts[None, :], tile_total), axis=1
    )
    return (owner_of, first_tile)


def norm_kernel(tokens_ref, out_ref, ordered):
    rows = tokens_ref[0].astype(jnp.float32)
    normed = rows * lax.rsqrt(jnp.mean(rows * rows, axis=-1, keepdims=True) + 1e-06)
    groups = LINE * LINE
    share = rows.shape[1] // (LINE * groups)
    for line in range(LINE):
        for group in range(groups):
            source = (line * groups + group) * share
            target = (group * LINE + line) * share
            ordered[:, target : target + share] = normed[:, source : source + share]
    out_ref[0] = ordered[...].astype(jnp.bfloat16)


def norm_rows(tokens):
    tiles, half, depth = tokens.shape
    block = 64
    spec = pl.BlockSpec((1, block, depth), lambda t, r: (t, r, 0))
    return pl.pallas_call(
        norm_kernel,
        grid=(tiles, half // block),
        out_shape=jax.ShapeDtypeStruct(tokens.shape, jnp.bfloat16),
        in_specs=[spec],
        out_specs=spec,
        scratch_shapes=[pltpu.VMEM((block, depth), jnp.float32)],
        compiler_params=pltpu.CompilerParams(vmem_limit_bytes=VMEM_BYTES),
        cost_estimate=SMALL_COST,
        name="norm",
    )(tokens)


def attend_kernel(layout, *refs):
    count = len(layout)
    pieces = sum(2 * len(tiles) for tiles in layout)
    sources, weight_hbm = list(refs[:pieces]), refs[pieces]
    outs = refs[pieces + 1 : pieces + 1 + count]
    rows, weight, qkv, row_sems, weight_sem = refs[pieces + 1 + count :]
    _, _, tiles, half, depth = rows.shape
    heads = weight.shape[1] // (3 * HEAD_DIM)

    def fetch(index):
        slot = index % 2
        copies = []
        for part in range(2):
            start = 0
            for place, length in enumerate(layout[index]):
                target = rows.at[slot, part, pl.ds(start, length)]
                copies.append(
                    pltpu.make_async_copy(sources.pop(0), target, row_sems.at[slot, part, place])
                )
                start += length
        return copies

    weight_copy = pltpu.make_async_copy(weight_hbm, weight, weight_sem)
    pending = fetch(0)
    for copy in pending:
        copy.start()
    weight_copy.start()
    for index in range(count):
        current = pending
        if index + 1 < count:
            pending = fetch(index + 1)
            for copy in pending:
                copy.start()
        for copy in current:
            copy.wait()
        if index == 0:
            weight_copy.wait()
        block = rows[index % 2].reshape(2 * tiles * half, depth)
        qkv[...] = jnp.dot(block, weight[...], preferred_element_type=jnp.float32).astype(jnp.bfloat16)
        for tile in range(tiles):
            for head in range(heads):

                def piece(kind):
                    start = (head * 3 + kind) * HEAD_DIM
                    columns = slice(start, start + HEAD_DIM)
                    low = qkv[tile * half : (tile + 1) * half, columns]
                    high = qkv[(tiles + tile) * half : (tiles + tile + 1) * half, columns]
                    return jnp.concatenate([low, high], axis=0)

                scores = lax.dot_general(
                    piece(0), piece(1), (((1,), (1,)), ((), ())), preferred_element_type=jnp.float32
                ) * (1.0 / math.sqrt(HEAD_DIM))
                scores = scores - jnp.max(scores, axis=-1, keepdims=True)
                raised = jnp.exp(scores)
                inverse = 1.0 / jnp.sum(raised, axis=-1, keepdims=True)
                soft = (raised * inverse).astype(jnp.bfloat16)
                mixed = jnp.dot(soft, piece(2), preferred_element_type=jnp.float32)
                outs[index][tile, :, head * HEAD_DIM : (head + 1) * HEAD_DIM] = mixed.astype(jnp.bfloat16)


def attend(sources, weight):
    layout = tuple(tuple(array.shape[0] for array in own) for own, _ in sources)
    tiles = sum(layout[0])
    _, half, depth = sources[0][0][0].shape
    width = weight.shape[1]
    shape = (tiles, 2 * half, width // 3)
    arrays = [array for own, other in sources for array in (*own, *other)]
    return pl.pallas_call(
        functools.partial(attend_kernel, layout),
        out_shape=[jax.ShapeDtypeStruct(shape, jnp.bfloat16)] * len(layout),
        in_specs=[pl.BlockSpec(memory_space=pl.ANY)] * (len(arrays) + 1),
        out_specs=[pl.BlockSpec(memory_space=pltpu.VMEM)] * len(layout),
        scratch_shapes=[
            pltpu.VMEM((2, 2, tiles, half, depth), jnp.bfloat16),
            pltpu.VMEM((depth, width), jnp.bfloat16),
            pltpu.VMEM((2 * tiles * half, width), jnp.bfloat16),
            pltpu.SemaphoreType.DMA((2, 2, tiles)),
            pltpu.SemaphoreType.DMA,
        ],
        compiler_params=pltpu.CompilerParams(vmem_limit_bytes=VMEM_BYTES),
        cost_estimate=SMALL_COST,
        name="attend",
    )(*arrays, weight)


def out_kernel(line_ref, *refs):
    attended, weight_ref, own_ref, other_ref, rows = refs[:LINE], *refs[LINE:]
    tiles, half, block = own_ref.shape
    share = attended[0].shape[2]
    count = tiles * half

    @pl.when(pl.program_id(0) == 0)
    def _():
        for distance, source in enumerate(attended):
            start = pl.multiple_of(lax.rem(line_ref[0] + distance, LINE) * share, share)
            for part in range(2):
                piece = source[:, part * half : (part + 1) * half].reshape(count, share)
                rows[part * count : (part + 1) * count, pl.ds(start, share)] = piece

    total = jnp.dot(rows[...], weight_ref[...], preferred_element_type=jnp.float32)
    total = total.astype(jnp.bfloat16)
    own_ref[...] = total[:count].reshape(tiles, half, block)
    other_ref[...] = total[count:].reshape(tiles, half, block)


def out_project(line_arg, attended, out_weight):
    tiles, full, share = attended[0].shape
    half = full // 2
    depth = out_weight.shape[1]
    block = 640
    part = pl.BlockSpec((tiles, half, block), lambda n, line: (0, 0, n))
    shape = jax.ShapeDtypeStruct((tiles, half, depth), jnp.bfloat16)
    return pl.pallas_call(
        out_kernel,
        grid_spec=pltpu.PrefetchScalarGridSpec(
            num_scalar_prefetch=1,
            grid=(depth // block,),
            in_specs=[pl.BlockSpec((tiles, full, share), lambda n, line: (0, 0, 0))] * LINE
            + [pl.BlockSpec((LINE * share, block), lambda n, line: (0, n))],
            out_specs=[part, part],
            scratch_shapes=[pltpu.VMEM((tiles * full, LINE * share), jnp.bfloat16)],
        ),
        out_shape=[shape, shape],
        compiler_params=pltpu.CompilerParams(vmem_limit_bytes=VMEM_BYTES),
        cost_estimate=SMALL_COST,
        name="out",
    )(line_arg, *attended, out_weight)


def join_kernel(
    mixing_ref, tokens_ref, early_ref, mid_ref, own_ref, other_ref, scale_ref, z_ref, inverse_ref
):
    inputs = tokens_ref[0].astype(jnp.float32)
    attended_out = own_ref[0].astype(jnp.float32) + other_ref[0].astype(jnp.float32)
    joined = (
        mixing_ref[0] * early_ref[0].astype(jnp.float32)
        + mixing_ref[1] * mid_ref[0].astype(jnp.float32)
        + (mixing_ref[2] + mixing_ref[3]) * inputs
        + (mixing_ref[3] * scale_ref[...]) * attended_out
    )
    centre = jnp.mean(joined, axis=-1, keepdims=True)
    shifted = joined - centre
    inverse = lax.rsqrt(jnp.mean(shifted * shifted, axis=-1, keepdims=True) + 1e-05)
    z_ref[0] = (shifted * inverse).astype(jnp.bfloat16)
    inverse_ref[0] = jnp.broadcast_to(inverse, inverse_ref.shape[1:])


def join_rows(tile, mixing, tokens, early, mid, own, other, scale):
    _, half, depth = tokens.shape
    block = 64
    spec = pl.BlockSpec((1, block, depth), lambda r: (tile, r, 0))
    return pl.pallas_call(
        join_kernel,
        grid=(half // block,),
        out_shape=[
            jax.ShapeDtypeStruct((1, half, depth), jnp.bfloat16),
            jax.ShapeDtypeStruct((1, half, 128), jnp.float32),
        ],
        in_specs=[pl.BlockSpec(memory_space=pltpu.SMEM)]
        + [spec] * 5
        + [pl.BlockSpec((1, depth), lambda r: (0, 0))],
        out_specs=[
            pl.BlockSpec((1, block, depth), lambda r: (0, r, 0)),
            pl.BlockSpec((1, block, 128), lambda r: (0, r, 0)),
        ],
        compiler_params=pltpu.CompilerParams(vmem_limit_bytes=VMEM_BYTES),
        cost_estimate=SMALL_COST,
        name="join",
    )(mixing, tokens, early, mid, own, other, scale)


def final_kernel(own_ref, other_ref, z_ref, later_z_ref, inverse_ref, later_inverse_ref, out_ref):
    first = pl.program_id(0) == 0
    grad = own_ref[0].astype(jnp.float32) + other_ref[0].astype(jnp.float32)
    normal = jnp.where(first, z_ref[0], later_z_ref[0]).astype(jnp.float32)
    inverse = jnp.where(first, inverse_ref[0, :, :1], later_inverse_ref[0, :, :1])
    mean = jnp.mean(grad, axis=-1, keepdims=True)
    along = jnp.mean(grad * normal, axis=-1, keepdims=True)
    out_ref[0] = ((grad - mean - normal * along) * inverse).astype(jnp.bfloat16)


def final_rows(own, other, z_tiles, inverse_tiles):
    tiles, half, depth = own.shape
    block = 64
    spec = pl.BlockSpec((1, block, depth), lambda t, r: (t, r, 0))
    z_spec = pl.BlockSpec((1, block, depth), lambda t, r: (0, r, 0))
    inverse_spec = pl.BlockSpec((1, block, 128), lambda t, r: (0, r, 0))
    return pl.pallas_call(
        final_kernel,
        grid=(tiles, half // block),
        out_shape=jax.ShapeDtypeStruct(own.shape, jnp.bfloat16),
        in_specs=[spec, spec, z_spec, z_spec, inverse_spec, inverse_spec],
        out_specs=spec,
        compiler_params=pltpu.CompilerParams(vmem_limit_bytes=VMEM_BYTES),
        cost_estimate=SMALL_COST,
        name="final",
    )(own, other, *z_tiles, *inverse_tiles)


def activate(preact):
    raised = jnp.exp(-0.5 * preact * preact)
    step = 1.0 / (1.0 + 0.3275911 * inv_root_two * jnp.abs(preact))
    series = 1.061405429 * step - 1.453152027
    series = series * step + 1.421413741
    series = series * step - 0.284496736
    series = series * step + 0.254829592
    tail = 0.5 * series * step * raised
    return jnp.where(preact >= 0.0, 1.0 - tail, tail), raised * inv_root_tau


def project_kernel(core_ref, *refs):
    sources = refs[:-4]
    weight_ref, bias_ref, projected_ref, slope_ref = refs[-4:]
    core = core_ref[0]
    tiles, _, half, block = projected_ref.shape
    rows = jnp.concatenate([source[0] for source in sources], axis=0)
    preact = jnp.dot(rows, weight_ref[...], preferred_element_type=jnp.float32) + bias_ref[...]
    cumulative, density = activate(preact)
    projected = (preact * cumulative).astype(jnp.bfloat16).reshape(2, tiles, 1, half, block)
    projected_ref[:, pl.ds(core, 1)] = projected[0]
    projected_ref[:, pl.ds(1 - core, 1)] = projected[1]
    slope_ref[...] = cumulative + preact * density


def home_project(core, own, other, weight, bias):
    tiles = len(own)
    _, half, depth = own[0].shape
    width = weight.shape[1]
    block = 512
    projected, slope = pl.pallas_call(
        project_kernel,
        grid_spec=pltpu.PrefetchScalarGridSpec(
            num_scalar_prefetch=1,
            grid=(width // block,),
            in_specs=[pl.BlockSpec((1, half, depth), lambda n, c: (0, 0, 0))] * (2 * tiles)
            + [
                pl.BlockSpec((depth, block), lambda n, c: (0, n)),
                pl.BlockSpec((1, block), lambda n, c: (0, n)),
            ],
            out_specs=[
                pl.BlockSpec((tiles, 2, half, block), lambda n, c: (0, 0, 0, n)),
                pl.BlockSpec((2 * tiles * half, block), lambda n, c: (0, n)),
            ],
        ),
        out_shape=[
            jax.ShapeDtypeStruct((tiles, 2, half, width), jnp.bfloat16),
            jax.ShapeDtypeStruct((2 * tiles * half, width), jnp.float32),
        ],
        compiler_params=pltpu.CompilerParams(vmem_limit_bytes=VMEM_BYTES),
        cost_estimate=SMALL_COST,
        name="project",
    )(core, *own, *other, weight, bias)
    return projected.reshape(tiles, 2 * half, width), slope


def grad_kernel(core_ref, slope_ref, back_own_ref, back_other_ref, weight_ref, own_ref, other_ref, total):
    step = pl.program_id(0)
    tiles, half, depth = own_ref.shape
    rows, block = slope_ref.shape
    back = jnp.concatenate(
        [ref[...].reshape(tiles * half, block) for ref in (back_own_ref, back_other_ref)], axis=0
    )
    slope_rows = (back.astype(jnp.float32) * slope_ref[...]).astype(jnp.bfloat16)
    term = lax.dot_general(
        slope_rows, weight_ref[...], (((1,), (1,)), ((), ())), preferred_element_type=jnp.float32
    )

    @pl.when(step == 0)
    def _():
        total[...] = term

    @pl.when(step > 0)
    def _():
        total[...] += term

    @pl.when(step == pl.num_programs(0) - 1)
    def _():
        own_ref[...] = total[: tiles * half].astype(jnp.bfloat16).reshape(tiles, half, depth)
        other_ref[...] = total[tiles * half :].astype(jnp.bfloat16).reshape(tiles, half, depth)


def home_grad(core, slope, back, weight):
    tiles, full, width = back.shape
    half = full // 2
    depth = weight.shape[0]
    block = 512
    back = back.reshape(tiles, 2, half, width)
    whole = pl.BlockSpec((tiles, half, depth), lambda n, c: (0, 0, 0))
    shape = jax.ShapeDtypeStruct((tiles, half, depth), jnp.bfloat16)
    return pl.pallas_call(
        grad_kernel,
        grid_spec=pltpu.PrefetchScalarGridSpec(
            num_scalar_prefetch=1,
            grid=(width // block,),
            in_specs=[
                pl.BlockSpec((tiles * full, block), lambda n, c: (0, n)),
                pl.BlockSpec((tiles, 1, half, block), lambda n, c: (0, c[0], 0, n)),
                pl.BlockSpec((tiles, 1, half, block), lambda n, c: (0, 1 - c[0], 0, n)),
                pl.BlockSpec((depth, block), lambda n, c: (0, n)),
            ],
            out_specs=[whole, whole],
            scratch_shapes=[pltpu.VMEM((tiles * full, depth), jnp.float32)],
        ),
        out_shape=[shape, shape],
        compiler_params=pltpu.CompilerParams(vmem_limit_bytes=VMEM_BYTES),
        cost_estimate=SMALL_COST,
        name="grad",
    )(core, slope, back, back, weight)


def owner_kernel(count, core_ref, *refs):
    sources = refs[: 2 * count]
    weight_ref, bias_ref, projected_ref = refs[2 * count :]
    core = core_ref[0]
    _, half, depth = sources[0].shape
    block = weight_ref.shape[1]
    rows = jnp.concatenate([source[0] for source in sources], axis=0)
    preact = jnp.dot(rows, weight_ref[...], preferred_element_type=jnp.float32) + bias_ref[...]
    projected = (preact * activate(preact)[0]).astype(jnp.bfloat16)
    projected = projected.reshape(count, 2, half, block)
    for index in range(count):
        projected_ref[index, pl.ds(core, 1)] = projected[index, :1]
        projected_ref[index, pl.ds(1 - core, 1)] = projected[index, 1:]


def owner_project(core, pairs, weight, bias):
    count = len(pairs)
    _, half, depth = pairs[0][0].shape
    width = weight.shape[1]
    block = 512
    projected = pl.pallas_call(
        functools.partial(owner_kernel, count),
        grid_spec=pltpu.PrefetchScalarGridSpec(
            num_scalar_prefetch=1,
            grid=(width // block,),
            in_specs=[pl.BlockSpec((1, half, depth), lambda n, c: (0, 0, 0))] * (2 * count)
            + [
                pl.BlockSpec((depth, block), lambda n, c: (0, n)),
                pl.BlockSpec((1, block), lambda n, c: (0, n)),
            ],
            out_specs=pl.BlockSpec((count, 2, half, block), lambda n, c: (0, 0, 0, n)),
        ),
        out_shape=jax.ShapeDtypeStruct((count, 2, half, width), jnp.bfloat16),
        compiler_params=pltpu.CompilerParams(vmem_limit_bytes=VMEM_BYTES),
        cost_estimate=SMALL_COST,
        name="owner",
    )(core, *[rows for pair in pairs for rows in pair], weight, bias)
    return projected.reshape(count, 2 * half, width)


def on_device(
    tokens, tap_early, tap_mid, tile_counts, qkv_weight, out_weight, layer_scale, layer_logits,
    proj_weight, proj_bias, grad_out,
):
    tile_group, token_share, depth = tokens.shape
    img_count = lax.axis_size(IMG)
    place = lax.axis_index(IMG)
    line_place = lax.axis_index("z")
    core = lax.axis_index("head")
    core_arg = core.astype(jnp.int32).reshape(1)
    tile_total = tile_group * img_count
    own_tiles = grad_out.shape[0]
    owner_of, first_tile = tile_owners(tile_counts, tile_total, tile_group)
    my_first = first_tile[place]

    depth_share, width = qkv_weight.shape
    share = width // LINE
    received = []
    for distance in range(LINE):
        target = (line_place + distance) % LINE
        columns = lax.dynamic_slice_in_dim(qkv_weight, target * share, share, axis=1)
        received.append(along_z(columns, distance) if distance else columns)
    normed = norm_rows(tokens)
    normed, received = lax.optimization_barrier((normed, received))
    ladder = jnp.stack([received[(LINE - 1 - j) % LINE] for j in range(2 * LINE - 1)], axis=0)
    sent = lax.dynamic_slice_in_dim(ladder, LINE - 1 - line_place, LINE, axis=0)
    weight = lax.all_gather(sent.reshape(LINE * depth_share, share), ("y", "x"), axis=0, tiled=True)

    def packet(distance, within, count, first):
        tile = (place + distance) * tile_group + within
        slot = jnp.clip(tile - first, 0, own_tiles - count)
        return lax.dynamic_slice_in_dim(grad_out, slot, count, axis=0)

    from_low = along_z(normed, 1)
    from_high = along_z(normed, -1)

    def packet(distance, within, count):
        tile = (place + distance) * tile_group + within
        slot = jnp.clip(tile - my_first, 0, own_tiles - count)
        return lax.dynamic_slice_in_dim(grad_out, slot, count, axis=0)

    packets = [packet(distance, within, 1) for distance in (1, 2) for within in range(tile_group)]
    from_low, from_high, packets = lax.optimization_barrier((from_low, from_high, packets))
    far_first = along_z(from_low[:1], 1)
    far_second = along_z(from_high[1:], -1)
    weight, packets = lax.optimization_barrier((weight, packets))
    halfway, far_on = two_on(packets[3], 2)
    far_back = [along_img(packets[2], 2), None]
    near_back = [along_img(packets[0], 1), along_img(packets[1], 1)]

    far_others = [swap(far_first), swap(far_second)]
    att_far, att_low, att_high = attend(
        [([far_first, far_second], far_others)]
        + [([rows], [swap(rows)]) for rows in (from_low, from_high)],
        weight,
    )
    (att_own,) = attend([([normed], [swap(normed)])], weight)
    att_far, att_low, att_high = along_z(att_far, 2), along_z(att_low, -1), along_z(att_high, 1)
    att_own, halfway, near_back[0] = lax.optimization_barrier((att_own, halfway, near_back[0]))
    far_back[1] = far_on(halfway)
    attended = [att_own, att_low, att_far, att_high]
    line_arg = line_place.astype(jnp.int32).reshape(1)
    part_own, part_other = out_project(line_arg, attended, out_weight)
    part_other = swap(part_other)
    raised_logits = jnp.exp(layer_logits)
    mixing = raised_logits / jnp.sum(raised_logits)
    scale = layer_scale.reshape(1, -1)
    joined = [
        join_rows(tile, mixing, tokens, tap_early, tap_mid, part_own, part_other, scale)
        for tile in range(tile_group)
    ]
    z_tiles = [z_rows for z_rows, _ in joined]
    inverse_tiles = [inverse for _, inverse in joined]

    near_first = along_img(z_tiles[0], -1)
    far_first = along_img(z_tiles[0], -2)
    halfway, far_on = two_on(z_tiles[1], -2)
    bias = proj_bias.reshape(1, -1)
    projected, slope = home_project(
        core_arg, z_tiles, [swap(z_rows) for z_rows in z_tiles], proj_weight, bias
    )
    slope, near_back[1], far_back[1] = lax.optimization_barrier((slope, near_back[1], far_back[1]))

    back = []
    for within in range(tile_group):
        tile = place * tile_group + within
        owner = owner_of[tile]
        slot = jnp.clip(tile - my_first, 0, own_tiles - 1)
        here = lax.dynamic_index_in_dim(grad_out, slot, axis=0, keepdims=False)
        near, far = near_back[within][0], far_back[within][0]
        back.append(jnp.where(owner == place, here, jnp.where(owner == place - 1, near, far)))
    back_rows = jnp.stack(back, axis=0)
    grad_own, grad_other = home_grad(core_arg, slope, back_rows, proj_weight)

    near_first, far_first, halfway, second, grad_other = lax.optimization_barrier(
        (near_first, far_first, halfway, z_tiles[1], grad_other)
    )
    near_second = along_img(second, -1)
    far_second = far_on(halfway)

    def guests(first, second):
        return owner_project(
            core_arg, [(first, swap(first)), (second, swap(second))], proj_weight, bias
        )

    early = guests(near_first, far_first)
    grad_joined = final_rows(grad_own, swap(grad_other), z_tiles, inverse_tiles)
    near_second, far_second, early, grad_joined = lax.optimization_barrier(
        (near_second, far_second, early, grad_joined)
    )
    late = guests(near_second, far_second)

    offset = my_first - place * tile_group
    held = first_tile[place + 1] - my_first
    at_hand = [projected[0], projected[1], early[0], late[0], early[1], late[1]]
    slots = []
    for slot in range(own_tiles):
        later = at_hand[min(slot + 1, len(at_hand) - 1)]
        picked = jnp.where(offset == 0, at_hand[slot], later)
        slots.append(jnp.where(slot < held, picked, jnp.zeros((), jnp.bfloat16)))
    owner_rows = jnp.stack(slots, axis=0)
    return (owner_rows, grad_joined)


def solution(mesh):
    cores = mesh.devices.shape[-1]
    inner = Mesh(mesh.devices.reshape(LINE, LINE, LINE, cores), IMG + ("head",))
    return jax.shard_map(
        on_device,
        mesh=inner,
        in_specs=(
            P(IMG, "head", None),
            P(IMG, "head", None),
            P(IMG, "head", None),
            P(),
            P(IMG, "head"),
            P("head", None),
            P(),
            P(),
            P(None, "head"),
            P("head"),
            P(IMG, None, "head"),
        ),
        out_specs=(P(IMG, None, "head"), P(IMG, "head", None)),
        check_vma=False,
    )
```
